32 devices in a mesh: dp: 8 (over y, x, core), tensor: 4 (over z).
Axes of the slice: x: 2, y: 2, z: 4, core: 2. Of those that a mesh axis runs over, the one named last changes fastest.
Arguments:
- inputs: bfloat16 [2, 8, 256, 2048], P(None, 'dp'), may hold values from -6 to 6
- lengths: int32 [2, 8], P(None, 'dp'), may hold values from 64 to 256, as said below
- prompt_mask: int32 [2, 8, 256], P(None, 'dp'), may hold values from 0 to 1, as said below
- partner: int32 [2, 8], P(None, 'dp'), may hold values from 0 to 7, as said below
- positions: int32 [2, 8, 256], P(None, 'dp'), may hold values from 0 to 383, as said below
- attn_gain: bfloat16 [2048], replicated, may hold values from 0.099609375 to 1.8984375
- mlp_gain: bfloat16 [2048], replicated, may hold values from 0.099609375 to 1.8984375
- attention_input_frozen: bfloat16 [2048, 3, 2048], P(None, None, 'tensor'), may hold values from -0.125 to 0.125
- attention_input_first: float32 [3, 2048, 16], replicated, may hold values from -0.125 to 0.125
- attention_input_second: float32 [3, 16, 2048], P(None, None, 'tensor'), may hold values from -0.6 to 0.6
- attention_input_magnitude: float32 [3, 2048], P(None, 'tensor'), may hold values from 0.7 to 1.5
- attention_output_frozen: bfloat16 [2048, 2048], P('tensor'), may hold values from -0.125 to 0.125
- attention_output_first: float32 [2048, 16], P('tensor'), may hold values from -0.125 to 0.125
- attention_output_second: float32 [16, 2048], replicated, may hold values from -0.6 to 0.6
- attention_output_magnitude: float32 [2048], replicated, may hold values from 4 to 16
- feedforward_input_frozen: bfloat16 [2048, 2, 5632], P(None, None, 'tensor'), may hold values from -0.125 to 0.125
- feedforward_input_first: float32 [2, 2048, 16], replicated, may hold values from -0.125 to 0.125
- feedforward_input_second: float32 [2, 16, 5632], P(None, None, 'tensor'), may hold values from -0.6 to 0.6
- feedforward_input_magnitude: float32 [2, 5632], P(None, 'tensor'), may hold values from 0.7 to 1.5
- feedforward_output_frozen: bfloat16 [5632, 2048], P('tensor'), may hold values from -0.078125 to 0.078125
- feedforward_output_first: float32 [5632, 16], P('tensor'), may hold values from -0.078125 to 0.078125
- feedforward_output_second: float32 [16, 2048], replicated, may hold values from -0.6 to 0.6
- feedforward_output_magnitude: float32 [2048], replicated, may hold values from 1 to 2.5
- grad_out: bfloat16 [2, 8, 256, 2048], P(None, 'dp'), may hold values from -6 to 6
Outputs:
- output: bfloat16 [2, 8, 256, 2048], P(None, 'dp')
- grad_in: bfloat16 [2, 8, 256, 2048], P(None, 'dp')
- attn_in_a_grad: float32 [3, 2048, 16], replicated
- attn_in_b_grad: float32 [3, 16, 2048], P(None, None, 'tensor')
- attn_in_mag_grad: float32 [3, 2048], P(None, 'tensor')
- attn_out_a_grad: float32 [2048, 16], P('tensor')
- attn_out_b_grad: float32 [16, 2048], replicated
- attn_out_mag_grad: float32 [2048], replicated
- mlp_in_a_grad: float32 [2, 2048, 16], replicated
- mlp_in_b_grad: float32 [2, 16, 5632], P(None, None, 'tensor')
- mlp_in_mag_grad: float32 [2, 5632], P(None, 'tensor')
- mlp_out_a_grad: float32 [5632, 16], P('tensor')
- mlp_out_b_grad: float32 [16, 2048], replicated
- mlp_out_mag_grad: float32 [2048], replicated
The draws below stay inside these ranges and needn't reach their ends.
Inputs may be any that keep to these rules, and one draw needn't show every extreme that they name: `lengths`: in every micro-batch the rows form pairs (partner of partner is the row itself): a prompt row holds the pair's prompt and then the chosen response, its partner, a response row, holds the rejected response alone. Valid tokens fill a row's first slots. `prompt_mask`: 1 exactly on the first slots of a prompt row that hold its prompt, at most 128 of them; 0 everywhere in a response row. `partner`: the other row of the row's pair, in the same micro-batch. `positions`: in a prompt row the slot's index; in a response row the slot's index plus the prompt length of its partner.
All inputs are finite; a program needn't handle non-finite values.
Results may differ from the reference program's by a relative error of at most 0.028.
Values may be sent and summed in bfloat16 or wider, within the bound.
No kernel may reach another device: no remote copies, remote signals or barrier semaphores. Data moves between devices by JAX's collectives and lax.ppermute only.
A program may use at most 384 MiB of HBM per device.

```python
import math
from functools import partial
import jax
import jax.numpy as jnp
from jax import lax

D = 2048
HEADS = 16
HEAD_DIM = 128
FF = 5632
ADAPTER_RANK = 16
ADAPTER_NUMER = 32
SLOTS = 256
MICRO = 2
ROWS = 8


def layout(key):
    rows_at = jnp.arange(ROWS, dtype=jnp.int32)
    slots_at = jnp.arange(SLOTS, dtype=jnp.int32)
    start_key, order_key, role_key, prompt_key, chosen_key, rejected_key = jax.random.split(key, 6)
    lengths_all = []
    masks_all = []
    partners_all = []
    positions_all = []
    for micro_at in range(MICRO):
        if micro_at % 2 == 0:
            first = jax.random.randint(jax.random.fold_in(start_key, micro_at), (), 0, ROWS, dtype=jnp.int32)
        else:
            first = jnp.int32(ROWS - 1)
        second = (first + 1) % ROWS
        order = jax.random.permutation(jax.random.fold_in(order_key, micro_at), ROWS - 2).astype(jnp.int32)
        others = (first + 2 + order) % ROWS
        left_rows = others[0::2]
        right_rows = others[1::2]
        partner_now = jnp.zeros((ROWS,), jnp.int32)
        partner_now = partner_now.at[left_rows].set(right_rows).at[right_rows].set(left_rows)
        partner_now = partner_now.at[first].set(second).at[second].set(first)
        lower = jnp.minimum(rows_at, partner_now)
        roles = jax.random.randint(jax.random.fold_in(role_key, micro_at), (ROWS,), 0, 2, dtype=jnp.int32)
        prompt_len = jax.random.randint(jax.random.fold_in(prompt_key, micro_at), (ROWS,), SLOTS // 4, SLOTS // 2 + 1, dtype=jnp.int32)
        chosen_len = jax.random.randint(jax.random.fold_in(chosen_key, micro_at), (ROWS,), SLOTS // 4, SLOTS // 2 + 1, dtype=jnp.int32)
        rejected_len = jax.random.randint(jax.random.fold_in(rejected_key, micro_at), (ROWS,), SLOTS // 4, SLOTS // 2 + 1, dtype=jnp.int32)
        forced_low = jnp.minimum(first, second)
        prompt_len = prompt_len.at[forced_low].set(SLOTS // 2)
        chosen_len = chosen_len.at[forced_low].set(SLOTS // 2)
        other_low = jnp.minimum(left_rows[0], right_rows[0])
        rejected_len = rejected_len.at[other_low].set(SLOTS // 4)
        picked_role = roles[lower]
        rejected = jnp.where(rows_at == lower, picked_role, 1 - picked_role)
        rejected = rejected.at[first].set(0).at[second].set(1)
        prompt_row = prompt_len[lower]
        length_row = jnp.where(rejected == 1, rejected_len[lower], prompt_row + chosen_len[lower])
        mask_row = jnp.where((rejected[:, None] == 0) & (slots_at[None, :] < prompt_row[:, None]), 1, 0)
        position_row = slots_at[None, :] + jnp.where(rejected == 1, prompt_row, 0)[:, None]
        lengths_all.append(length_row)
        masks_all.append(mask_row)
        partners_all.append(partner_now)
        positions_all.append(position_row)
    return (jnp.stack(lengths_all).astype(jnp.int32), jnp.stack(masks_all).astype(jnp.int32), jnp.stack(partners_all).astype(jnp.int32), jnp.stack(positions_all).astype(jnp.int32))


def draw_lengths(key, part):
    return layout(key)[0]


def draw_prompt_mask(key, part):
    return layout(key)[1]


def draw_partner(key, part):
    return layout(key)[2]


def draw_positions(key, part):
    return layout(key)[3]


def steps_of(rng, dims, shards, smallest, largest):
    factor_of, own = 1.0, jax.random.fold_in(rng, 6)
    for axis_at, shards_of in shards:
        heights = jnp.exp(jax.random.uniform(jax.random.fold_in(own, axis_at), (shards_of,), jnp.float32, smallest / len(shards), largest / len(shards)))
        factor_of = factor_of * jnp.repeat(heights, dims[axis_at] // shards_of).reshape([-1 if axis == axis_at else 1 for axis in range(len(dims))])
    return factor_of


def noise(rng, extent, deviation, reach, shards=(), held_as=jnp.bfloat16):
    drawn = deviation * jax.random.normal(rng, extent, jnp.float32)
    if shards:
        drawn = drawn * steps_of(rng, extent, shards, -0.22, 0.18)
    return jnp.clip(drawn, -reach, reach).astype(held_as)


def setup_inputs(seed: int = 0) -> dict:
    splits = jax.random.split(jax.random.key(seed), 25)
    return {
        "inputs": noise(splits[0], (MICRO, ROWS, SLOTS, D), 1.0, 6.0, ((1, 8),)),
        "lengths": draw_lengths(jax.random.fold_in(splits[24], 71), 0),
        "prompt_mask": draw_prompt_mask(jax.random.fold_in(splits[24], 71), 0),
        "partner": draw_partner(jax.random.fold_in(splits[24], 71), 0),
        "positions": draw_positions(jax.random.fold_in(splits[24], 71), 0),
        "attn_gain": jnp.clip(1.0 + 0.18 * jax.random.normal(splits[5], (D,), jnp.float32), 0.099609375, 1.8984375).astype(jnp.bfloat16),
        "mlp_gain": jnp.clip(1.0 + 0.18 * jax.random.normal(splits[6], (D,), jnp.float32), 0.099609375, 1.8984375).astype(jnp.bfloat16),
        "attention_input_frozen": noise(splits[7], (D, 3, D), D ** -0.5, 0.125, ((2, 4),)),
        "attention_input_first": noise(splits[8], (3, D, ADAPTER_RANK), D ** -0.5, 0.125, (), jnp.float32),
        "attention_input_second": noise(splits[9], (3, ADAPTER_RANK, D), 0.1, 0.6, ((2, 4),), jnp.float32),
        "attention_input_magnitude": jnp.clip(0.7 + 0.8 * jax.random.uniform(splits[10], (3, D), jnp.float32) ** steps_of(splits[10], (3, D), ((1, 4),), -0.2, 0.2), 0.7, 1.5),
        "attention_output_frozen": noise(splits[11], (D, D), D ** -0.5, 0.125, ((0, 4),)),
        "attention_output_first": noise(splits[12], (D, ADAPTER_RANK), D ** -0.5, 0.125, ((0, 4),), jnp.float32),
        "attention_output_second": noise(splits[13], (ADAPTER_RANK, D), 0.1, 0.6, (), jnp.float32),
        "attention_output_magnitude": jnp.clip(jnp.exp(jax.random.uniform(splits[14], (D,), jnp.float32, math.log(4.0), math.log(16.0))), 4.0, 16.0),
        "feedforward_input_frozen": noise(splits[15], (D, 2, FF), D ** -0.5, 0.125, ((2, 4),)),
        "feedforward_input_first": noise(splits[16], (2, D, ADAPTER_RANK), D ** -0.5, 0.125, (), jnp.float32),
        "feedforward_input_second": noise(splits[17], (2, ADAPTER_RANK, FF), 0.1, 0.6, ((2, 4),), jnp.float32),
        "feedforward_input_magnitude": jnp.clip(0.7 + 0.8 * jax.random.uniform(splits[18], (2, FF), jnp.float32) ** steps_of(splits[18], (2, FF), ((1, 4),), -0.2, 0.2), 0.7, 1.5),
        "feedforward_output_frozen": noise(splits[19], (FF, D), FF ** -0.5, 0.078125, ((0, 4),)),
        "feedforward_output_first": noise(splits[20], (FF, ADAPTER_RANK), FF ** -0.5, 0.078125, ((0, 4),), jnp.float32),
        "feedforward_output_second": noise(splits[21], (ADAPTER_RANK, D), 0.1, 0.6, (), jnp.float32),
        "feedforward_output_magnitude": jnp.clip(jax.random.uniform(splits[22], (D,), jnp.float32, 1.0, 2.5), 1.0, 2.5),
        "grad_out": noise(splits[23], (MICRO, ROWS, SLOTS, D), 1.0, 6.0, ((1, 8),)),
    }


epsilon = 1e-05
rope_base = 10000.0
highest_precision = lax.Precision.HIGHEST
masked_score = -1e+30

@jax.custom_vjp
def low(v):
    return lax.optimization_barrier(v.astype(jnp.bfloat16)).astype(jnp.float32)

@jax.custom_vjp
def low_back(v):
    return v

def low_keep(v):
    return (low(v), None)

def low_pass(kept, grad):
    return (grad,)

def back_keep(v):
    return (v, None)

def back_low(kept, grad):
    return (low(grad),)
low.defvjp(low_keep, low_pass)
low_back.defvjp(back_keep, back_low)

def rms_scale(values):
    return lax.rsqrt(lax.optimization_barrier(jnp.mean(values * values, axis=-1, keepdims=True)) + epsilon)

def turn_half(values):
    middle = values.shape[-1] // 2
    return jnp.concatenate([-values[..., middle:], values[..., :middle]], axis=-1)

def rope_tables(positions):
    indices = jnp.arange(HEAD_DIM // 2, dtype=jnp.float32)
    inverse = rope_base ** (-2.0 * indices / HEAD_DIM)
    angles = positions.astype(jnp.float32)[..., None] * inverse
    angles = jnp.concatenate([angles, angles], axis=-1)
    return (jnp.cos(angles), jnp.sin(angles))

def merged(base, left_factor, right_factor, column_magnitude):
    merged_matrix = base + ADAPTER_NUMER / ADAPTER_RANK * jnp.dot(left_factor, right_factor, precision=highest_precision)
    column_norm_value = jnp.sqrt(lax.optimization_barrier(jnp.sum(merged_matrix * merged_matrix, axis=0)))
    return low(merged_matrix * (column_magnitude / column_norm_value))

def attend_row(pieces):
    queries, keys_own, values_own, keys_far, values_far, far_mask = pieces
    slot_count = queries.shape[0]
    all_keys = jnp.concatenate([keys_own, keys_far], axis=0)
    all_values = jnp.concatenate([values_own, values_far], axis=0)
    scores = low_back(jnp.einsum('ihd,jhd->hij', queries, all_keys, precision=highest_precision) * (1.0 / math.sqrt(HEAD_DIM)))
    rows_at = jnp.arange(slot_count)[:, None]
    own_ok = jnp.arange(slot_count)[None, :] <= rows_at
    far_ok = jnp.broadcast_to(far_mask[None, :] > 0, (slot_count, slot_count))
    allowed = jnp.concatenate([own_ok, far_ok], axis=1)
    scores = jnp.where(allowed[None], scores, masked_score)
    row_top = lax.optimization_barrier(jnp.max(scores, axis=-1, keepdims=True))
    exponent = jnp.exp(scores - row_top)
    shares = low(exponent / lax.optimization_barrier(jnp.sum(exponent, axis=-1, keepdims=True)))
    attended = jnp.einsum('hij,jhd->ihd', shares, all_values, precision=highest_precision)
    return low(low_back(attended.reshape(slot_count, -1)))

def one_batch(weights, pieces):
    qkv_weight, out_weight, gate_up_weight, down_weight, attn_scale, mlp_scale = weights
    tokens, lengths_now, mask_now, partner_now, positions_now = pieces
    normed = low(tokens * rms_scale(tokens) * attn_scale)
    projected = jnp.dot(normed.reshape(-1, D), qkv_weight.reshape(D, 3 * D), precision=highest_precision)
    projected = projected.reshape(ROWS, SLOTS, 3, HEADS, HEAD_DIM)
    cosine, sine_tab = rope_tables(positions_now)
    cosine = cosine[:, :, None, :]
    sine_tab = sine_tab[:, :, None, :]
    queries = low_back(projected[:, :, 0])
    keys_rot = low_back(projected[:, :, 1])
    values_in = low_back(projected[:, :, 2])
    queries = low(queries * cosine + turn_half(queries) * sine_tab)
    keys_rot = low(keys_rot * cosine + turn_half(keys_rot) * sine_tab)
    values_in = low(values_in)
    keys_far = low_back(jnp.take(keys_rot, partner_now, axis=0))
    values_far = low_back(jnp.take(values_in, partner_now, axis=0))
    mask_far = jnp.take(mask_now, partner_now, axis=0)
    attended = lax.map(jax.checkpoint(attend_row), (queries, keys_rot, values_in, keys_far, values_far, mask_far))
    live_mask = (jnp.arange(SLOTS)[None, :] < lengths_now[:, None]).astype(tokens.dtype)[..., None]
    branch = low_back(jnp.dot(attended.reshape(-1, D), out_weight, precision=highest_precision)).reshape(tokens.shape)
    middle = tokens + live_mask * branch
    normed_mlp = low(middle * rms_scale(middle) * mlp_scale)
    gate_up = jnp.dot(normed_mlp.reshape(-1, D), gate_up_weight.reshape(D, 2 * FF), precision=highest_precision)
    gate_up = gate_up.reshape(ROWS, SLOTS, 2, FF)
    gate_pre = low_back(gate_up[:, :, 0])
    up_pre = low_back(gate_up[:, :, 1])
    hidden = low(jax.nn.silu(gate_pre) * up_pre)
    branch_mlp = low_back(jnp.dot(hidden.reshape(-1, FF), down_weight, precision=highest_precision)).reshape(tokens.shape)
    return middle + live_mask * branch_mlp

def reference(inputs, lengths, prompt_mask, partner, positions, attn_gain, mlp_gain, attention_input_frozen, attention_input_first, attention_input_second, attention_input_magnitude, attention_output_frozen, attention_output_first, attention_output_second, attention_output_magnitude, feedforward_input_frozen, feedforward_input_first, feedforward_input_second, feedforward_input_magnitude, feedforward_output_frozen, feedforward_output_first, feedforward_output_second, feedforward_output_magnitude, grad_out):
    qkv_base = attention_input_frozen.astype(jnp.float32)
    out_base = attention_output_frozen.astype(jnp.float32)
    gate_up_base = feedforward_input_frozen.astype(jnp.float32)
    down_base = feedforward_output_frozen.astype(jnp.float32)
    attn_scale = attn_gain.astype(jnp.float32)
    mlp_scale = mlp_gain.astype(jnp.float32)

    def forward(tokens, adapters):
        qa, qb, qm, oa, ob, om, ga, gb, gm, da, db, dm = adapters
        qkv_weight = jnp.stack([merged(qkv_base[:, i, :], qa[i], qb[i], qm[i]) for i in range(3)], axis=1)
        out_weight = merged(out_base, oa, ob, om)
        gate_up_weight = jnp.stack([merged(gate_up_base[:, i, :], ga[i], gb[i], gm[i]) for i in range(2)], axis=1)
        down_weight = merged(down_base, da, db, dm)
        weights = (qkv_weight, out_weight, gate_up_weight, down_weight, attn_scale, mlp_scale)
        return lax.map(jax.checkpoint(partial(one_batch, weights)), (tokens, lengths, prompt_mask, partner, positions))
    adapters = (attention_input_first, attention_input_second, attention_input_magnitude, attention_output_first, attention_output_second, attention_output_magnitude, feedforward_input_first, feedforward_input_second, feedforward_input_magnitude, feedforward_output_first, feedforward_output_second, feedforward_output_magnitude)
    result, pull = jax.vjp(forward, inputs.astype(jnp.float32), adapters)
    input_grad, grads = pull(grad_out.astype(jnp.float32))
    return (result.astype(jnp.bfloat16), input_grad.astype(jnp.bfloat16), grads[0], grads[1], grads[2], grads[3], grads[4], grads[5], grads[6], grads[7], grads[8], grads[9], grads[10], grads[11])
```

```python
import math

import jax
import jax.numpy as jnp
from jax import lax
from jax.experimental import pallas as pl
from jax.experimental.pallas import tpu as pltpu
from jax.sharding import PartitionSpec as P

HEAD_DIM = 128
ADAPTER_RANK = 16
ADAPTER_NUMER = 32


epsilon = 1e-05
rope_base = 10000.0
highest_precision = lax.Precision.HIGHEST
masked_score = -1e30


def rms_scale(values):
    return lax.rsqrt(jnp.mean(values * values, axis=-1, keepdims=True) + epsilon)


def rms_back(values, scale_rows, gain_row, gradient):
    scaled_update = gradient * gain_row
    normal = values * scale_rows
    return scale_rows * (
        scaled_update - normal * jnp.mean(scaled_update * normal, axis=-1, keepdims=True)
    )


def turn_half(values):
    middle = values.shape[-1] // 2
    return jnp.concatenate([-values[..., middle:], values[..., :middle]], axis=-1)


def rope_tables(positions, head_size):
    indices = jnp.arange(head_size // 2, dtype=jnp.float32)
    inverse = rope_base ** (-2.0 * indices / head_size)
    angles = positions.astype(jnp.float32)[:, None] * inverse[None, :]
    angles = jnp.concatenate([angles, angles], axis=-1)
    return (jnp.cos(angles)[:, None, :], jnp.sin(angles)[:, None, :])


def contract_rows(left_factor, right_factor):
    return lax.dot_general(
        left_factor, right_factor, (((0,), (0,)), ((), ())), preferred_element_type=jnp.float32
    )


def contract_cols(left_factor, right_factor):
    return lax.dot_general(
        left_factor, right_factor, (((1,), (1,)), ((), ())), preferred_element_type=jnp.float32
    )


def pick_partner(partner_row, far_slots, current, pieces):
    piece_rows = pieces[0].shape[0]
    wanted = partner_row * far_slots + jnp.arange(far_slots, dtype=jnp.int32)
    inside = (wanted >= 0) & (wanted < piece_rows)
    clipped = jnp.clip(wanted, 0, piece_rows - 1)
    packed = jnp.where(inside[:, None], jnp.take(pieces[0], clipped, axis=0), current[0])
    flags = jnp.where(inside, jnp.take(pieces[1], clipped, axis=0), current[1])
    return (packed, flags)


def place_far(partner_row, far_grad, row_count):
    far_slots = far_grad.shape[0]
    owners = jnp.arange(row_count // far_slots, dtype=jnp.int32)
    term = jnp.where((owners == partner_row)[:, None, None], far_grad[None], 0.0)
    return term.reshape(row_count, far_grad.shape[1])


def column_gradient_list(
    weight_total,
    merged_matrix,
    column_norm_value,
    column_magnitude,
    left_factor,
    right_factor,
    adapter_scale,
):
    inner = jnp.sum(weight_total * merged_matrix, axis=0)
    merged_matrix_gradient = (
        column_magnitude
        / column_norm_value
        * (weight_total - inner / (column_norm_value * column_norm_value) * merged_matrix)
    )
    left_factor_gradient = adapter_scale * jnp.einsum(
        "ypz,pvz->pyv", merged_matrix_gradient, right_factor, precision=highest_precision
    )
    right_factor_gradient = adapter_scale * jnp.einsum(
        "emn,mez->enz", left_factor, merged_matrix_gradient, precision=highest_precision
    )
    return (left_factor_gradient, right_factor_gradient, inner / column_norm_value)


def row_pieces_list(
    weight_total,
    merged_matrix,
    column_norm_value,
    column_magnitude,
    left_factor,
    right_factor,
    adapter_scale,
):
    scaled_update = weight_total * (column_magnitude / column_norm_value)
    inner = jnp.sum(weight_total * merged_matrix, axis=0)
    left_factor_part = adapter_scale * jnp.dot(
        scaled_update, right_factor.T, precision=highest_precision
    )
    right_factor_part = adapter_scale * jnp.dot(
        left_factor.T, scaled_update, precision=highest_precision
    )
    return (inner, left_factor_part, right_factor_part)


def general_device(
    inputs,
    lengths,
    prompt_mask,
    partner,
    positions,
    attn_gain,
    mlp_gain,
    attention_input_frozen,
    attention_input_first,
    attention_input_second,
    attention_input_magnitude,
    attention_output_frozen,
    attention_output_first,
    attention_output_second,
    attention_output_magnitude,
    feedforward_input_frozen,
    feedforward_input_first,
    feedforward_input_second,
    feedforward_input_magnitude,
    feedforward_output_frozen,
    feedforward_output_first,
    feedforward_output_second,
    feedforward_output_magnitude,
    grad_out,
):
    micro_count = inputs.shape[0]
    slot_count = inputs.shape[2]
    model_width = inputs.shape[3]
    head_cols = attention_input_frozen.shape[2]
    head_count = head_cols // HEAD_DIM
    unit_count = feedforward_input_frozen.shape[2]
    adapter_scale = ADAPTER_NUMER / ADAPTER_RANK
    score_scale = 1.0 / math.sqrt(HEAD_DIM)
    block_rows = min(512, slot_count)
    block_count = slot_count // block_rows
    attn_scale = attn_gain.astype(jnp.float32)
    mlp_scale = mlp_gain.astype(jnp.float32)
    query_key_value_merged = attention_input_frozen.astype(
        jnp.float32
    ) + adapter_scale * jnp.einsum(
        "kdr,kro->dko", attention_input_first, attention_input_second, precision=highest_precision
    )
    query_key_value_norm = jnp.sqrt(
        jnp.sum(query_key_value_merged * query_key_value_merged, axis=0)
    )
    qkv_weight = (
        (query_key_value_merged * (attention_input_magnitude / query_key_value_norm))
        .astype(jnp.bfloat16)
        .reshape(model_width, 3 * head_cols)
    )
    gate_merged_weight = feedforward_input_frozen.astype(jnp.float32) + adapter_scale * jnp.einsum(
        "kdr,kro->dko",
        feedforward_input_first,
        feedforward_input_second,
        precision=highest_precision,
    )
    gate_column_norm = jnp.sqrt(jnp.sum(gate_merged_weight * gate_merged_weight, axis=0))
    gate_up_weight = (
        (gate_merged_weight * (feedforward_input_magnitude / gate_column_norm))
        .astype(jnp.bfloat16)
        .reshape(model_width, 2 * unit_count)
    )
    output_merged_weight = attention_output_frozen.astype(jnp.float32) + adapter_scale * jnp.dot(
        attention_output_first, attention_output_second, precision=highest_precision
    )
    down_merged_weight = feedforward_output_frozen.astype(jnp.float32) + adapter_scale * jnp.dot(
        feedforward_output_first, feedforward_output_second, precision=highest_precision
    )
    out_square = jnp.sum(output_merged_weight * output_merged_weight, axis=0)
    down_square = jnp.sum(down_merged_weight * down_merged_weight, axis=0)
    output_cross_term = jnp.dot(
        attention_output_first.T, output_merged_weight, precision=highest_precision
    )
    down_cross_term = jnp.dot(
        feedforward_output_first.T, down_merged_weight, precision=highest_precision
    )
    out_square, down_square, output_cross_term, down_cross_term = (
        lax.psum(out_square.astype(jnp.bfloat16), "tensor").astype(jnp.float32),
        lax.psum(down_square.astype(jnp.bfloat16), "tensor").astype(jnp.float32),
        lax.psum(output_cross_term.astype(jnp.bfloat16), "tensor").astype(jnp.float32),
        lax.psum(down_cross_term.astype(jnp.bfloat16), "tensor").astype(jnp.float32),
    )
    output_column_norm = jnp.sqrt(out_square)
    down_column_norm = jnp.sqrt(down_square)
    out_weight = (output_merged_weight * (attention_output_magnitude / output_column_norm)).astype(
        jnp.bfloat16
    )
    down_weight = (down_merged_weight * (feedforward_output_magnitude / down_column_norm)).astype(
        jnp.bfloat16
    )
    grad_qkv = jnp.zeros((model_width, 3 * head_cols), jnp.float32)
    output_projection_gradient = jnp.zeros((head_cols, model_width), jnp.float32)
    grad_gate_up = jnp.zeros((model_width, 2 * unit_count), jnp.float32)
    down_projection_gradient = jnp.zeros((unit_count, model_width), jnp.float32)
    results = []
    input_grads = []
    for micro_at in range(micro_count):
        tokens = inputs[micro_at, 0].astype(jnp.float32)
        length_now = lengths[micro_at, 0]
        partner_row = partner[micro_at, 0]
        cosine, sine_tab = rope_tables(positions[micro_at, 0], HEAD_DIM)
        live_mask = (jnp.arange(slot_count) < length_now).astype(jnp.float32)[:, None]
        attn_rows = rms_scale(tokens)
        normed = (tokens * attn_rows * attn_scale).astype(jnp.bfloat16)
        projected = jnp.dot(normed, qkv_weight, preferred_element_type=jnp.float32).reshape(
            slot_count, 3, head_count, HEAD_DIM
        )
        queries = (projected[:, 0] * cosine + turn_half(projected[:, 0]) * sine_tab).astype(
            jnp.bfloat16
        )
        keys_rot = (projected[:, 1] * cosine + turn_half(projected[:, 1]) * sine_tab).astype(
            jnp.bfloat16
        )
        values_in = projected[:, 2].astype(jnp.bfloat16)
        own_pack = jnp.concatenate(
            [keys_rot.reshape(slot_count, head_cols), values_in.reshape(slot_count, head_cols)],
            axis=1,
        )
        own_flags = prompt_mask[micro_at, 0].astype(jnp.bfloat16)
        empty_pack = (
            jnp.zeros((slot_count, 2 * head_cols), jnp.bfloat16),
            jnp.zeros((slot_count,), jnp.bfloat16),
        )
        far_pack, far_flags = pick_partner(
            partner_row,
            slot_count,
            empty_pack,
            (
                lax.all_gather(own_pack, "dp", axis=0, tiled=True),
                lax.all_gather(own_flags, "dp", axis=0, tiled=True),
            ),
        )
        all_keys = jnp.concatenate(
            [keys_rot, far_pack[:, :head_cols].reshape(slot_count, head_count, HEAD_DIM)], axis=0
        )
        all_values = jnp.concatenate(
            [values_in, far_pack[:, head_cols:].reshape(slot_count, head_count, HEAD_DIM)], axis=0
        )
        far_ok = far_flags > 0

        def block_scores(queries_blk, first_row):
            raw = (
                jnp.einsum(
                    "ihd,jhd->hij", queries_blk, all_keys, preferred_element_type=jnp.float32
                )
                * score_scale
            )
            rows_at = first_row + jnp.arange(block_rows)[:, None]
            own_ok = jnp.arange(slot_count)[None, :] <= rows_at
            allowed = jnp.concatenate(
                [own_ok, jnp.broadcast_to(far_ok[None, :], (block_rows, slot_count))], axis=1
            )
            return jnp.where(allowed[None], raw, masked_score)

        def forward_block(block_at):
            first_row = block_at * block_rows
            scores = block_scores(queries, first_row)
            row_top = jnp.max(scores, axis=-1, keepdims=True)
            exponent = jnp.exp(scores - row_top)
            row_total = jnp.sum(exponent, axis=-1, keepdims=True)
            shares = (exponent / row_total).astype(jnp.bfloat16)
            attended_blk = jnp.einsum(
                "hij,jhd->ihd", shares, all_values, preferred_element_type=jnp.float32
            )
            return (
                attended_blk.reshape(block_rows, head_cols).astype(jnp.bfloat16),
                row_top,
                row_total,
            )

        attended, row_tops, row_totals = lax.map(
            forward_block, jnp.arange(block_count, dtype=jnp.int32)
        )
        attended = attended.reshape(slot_count, head_cols)
        branch = lax.psum(
            jnp.dot(attended, out_weight, preferred_element_type=jnp.float32).astype(jnp.bfloat16),
            "tensor",
        ).astype(jnp.float32)
        middle = tokens + live_mask * branch
        mlp_rows = rms_scale(middle)
        normed_mlp = (middle * mlp_rows * mlp_scale).astype(jnp.bfloat16)
        gate_up = jnp.dot(normed_mlp, gate_up_weight, preferred_element_type=jnp.float32)
        gate_pre = gate_up[:, :unit_count]
        up_pre = gate_up[:, unit_count:]
        gate_sigmoid = jax.nn.sigmoid(gate_pre)
        activated = gate_pre * gate_sigmoid
        hidden = (activated * up_pre).astype(jnp.bfloat16)
        branch_mlp = lax.psum(
            jnp.dot(hidden, down_weight, preferred_element_type=jnp.float32).astype(jnp.bfloat16),
            "tensor",
        ).astype(jnp.float32)
        results.append((middle + live_mask * branch_mlp).astype(jnp.bfloat16))
        upstream = grad_out[micro_at, 0].astype(jnp.float32)
        down_grad = (live_mask * upstream).astype(jnp.bfloat16)
        hidden_grad = contract_cols(down_grad, down_weight)
        down_projection_gradient = down_projection_gradient + contract_rows(hidden, down_grad)
        gate_grad = (
            hidden_grad * up_pre * gate_sigmoid * (1.0 + gate_pre * (1.0 - gate_sigmoid))
        ).astype(jnp.bfloat16)
        up_grad = (hidden_grad * activated).astype(jnp.bfloat16)
        gate_up_grad = jnp.concatenate([gate_grad, up_grad], axis=1)
        grad_gate_up = grad_gate_up + contract_rows(normed_mlp, gate_up_grad)
        mlp_in_grad = lax.psum(
            contract_cols(gate_up_grad, gate_up_weight).astype(jnp.bfloat16), "tensor"
        ).astype(jnp.float32)
        middle_grad = upstream + rms_back(middle, mlp_rows, mlp_scale, mlp_in_grad)
        attn_grad = (live_mask * middle_grad).astype(jnp.bfloat16)
        output_projection_gradient = output_projection_gradient + contract_rows(attended, attn_grad)
        attended_grad = (
            contract_cols(attn_grad, out_weight)
            .astype(jnp.bfloat16)
            .reshape(slot_count, head_count, HEAD_DIM)
        )

        def backward_block(carried, block_at):
            first_row = block_at * block_rows
            row_top = row_tops[block_at]
            row_total = row_totals[block_at]
            scores = block_scores(queries, first_row)
            shares = jnp.exp(scores - row_top) / row_total
            shares_low = shares.astype(jnp.bfloat16)
            share_grad = jnp.einsum(
                "ihd,jhd->hij", attended_grad, all_values, preferred_element_type=jnp.float32
            )
            inner = jnp.sum(shares * share_grad, axis=-1, keepdims=True)
            score_grad = (shares * (share_grad - inner)).astype(jnp.bfloat16)
            query_grad = (
                jnp.einsum("hij,jhd->ihd", score_grad, all_keys, preferred_element_type=jnp.float32)
                * score_scale
            )
            key_part = (
                jnp.einsum("hij,ihd->jhd", score_grad, queries, preferred_element_type=jnp.float32)
                * score_scale
            )
            value_part = jnp.einsum(
                "hij,ihd->jhd", shares_low, attended_grad, preferred_element_type=jnp.float32
            )
            query_grad, key_part, value_part = (query_grad, key_part, value_part)
            return ((carried[0] + key_part, carried[1] + value_part), query_grad)

        key_zero = jnp.zeros((slot_count + slot_count, head_count, HEAD_DIM), jnp.float32)
        (key_grad, value_grad), query_grads = lax.scan(
            backward_block, (key_zero, key_zero), jnp.arange(block_count, dtype=jnp.int32)
        )
        far_grad = jnp.concatenate(
            [
                key_grad[slot_count:].reshape(slot_count, head_cols),
                value_grad[slot_count:].reshape(slot_count, head_cols),
            ],
            axis=1,
        )
        far_low = far_grad.astype(jnp.bfloat16)
        returned = lax.psum_scatter(
            place_far(
                partner_row, far_low.astype(jnp.float32), slot_count * lax.axis_size("dp")
            ).astype(jnp.bfloat16),
            "dp",
            scatter_dimension=0,
            tiled=True,
        ).astype(jnp.float32)
        key_total = key_grad[:slot_count] + returned[:, :head_cols].reshape(
            slot_count, head_count, HEAD_DIM
        )
        value_total = value_grad[:slot_count] + returned[:, head_cols:].reshape(
            slot_count, head_count, HEAD_DIM
        )
        query_total = query_grads.reshape(slot_count, head_count, HEAD_DIM)
        query_back = (query_total * cosine - turn_half(query_total * sine_tab)).astype(jnp.bfloat16)
        key_back = (key_total * cosine - turn_half(key_total * sine_tab)).astype(jnp.bfloat16)
        value_back = value_total.astype(jnp.bfloat16)
        qkv_grad = jnp.concatenate(
            [
                query_back.reshape(slot_count, head_cols),
                key_back.reshape(slot_count, head_cols),
                value_back.reshape(slot_count, head_cols),
            ],
            axis=1,
        )
        grad_qkv = grad_qkv + contract_rows(normed, qkv_grad)
        attn_in_grad = lax.psum(
            contract_cols(qkv_grad, qkv_weight).astype(jnp.bfloat16), "tensor"
        ).astype(jnp.float32)
        input_grads.append(
            (middle_grad + rms_back(tokens, attn_rows, attn_scale, attn_in_grad)).astype(
                jnp.bfloat16
            )
        )
    query_key_value_total = grad_qkv.reshape(model_width, 3, head_cols)
    gate_weight_total = grad_gate_up.reshape(model_width, 2, unit_count)
    qkv_left, qkv_right, qkv_mag = column_gradient_list(
        query_key_value_total,
        query_key_value_merged,
        query_key_value_norm,
        attention_input_magnitude,
        attention_input_first,
        attention_input_second,
        adapter_scale,
    )
    gate_left, gate_right, gate_mag = column_gradient_list(
        gate_weight_total,
        gate_merged_weight,
        gate_column_norm,
        feedforward_input_magnitude,
        feedforward_input_first,
        feedforward_input_second,
        adapter_scale,
    )
    out_inner, output_left_factor, output_right_factor = row_pieces_list(
        output_projection_gradient,
        output_merged_weight,
        output_column_norm,
        attention_output_magnitude,
        attention_output_first,
        attention_output_second,
        adapter_scale,
    )
    down_inner, down_left_factor, down_right_factor = row_pieces_list(
        down_projection_gradient,
        down_merged_weight,
        down_column_norm,
        feedforward_output_magnitude,
        feedforward_output_first,
        feedforward_output_second,
        adapter_scale,
    )
    qkv_left, gate_left, output_right_factor, down_right_factor, out_inner, down_inner = lax.psum(
        (qkv_left, gate_left, output_right_factor, down_right_factor, out_inner, down_inner),
        ("dp", "tensor"),
    )
    qkv_right, qkv_mag, gate_right, gate_mag, output_left_factor, down_left_factor = (
        lax.psum(qkv_right.astype(jnp.bfloat16), "dp").astype(jnp.float32),
        lax.psum(qkv_mag.astype(jnp.bfloat16), "dp").astype(jnp.float32),
        lax.psum(gate_right.astype(jnp.bfloat16), "dp").astype(jnp.float32),
        lax.psum(gate_mag.astype(jnp.bfloat16), "dp").astype(jnp.float32),
        lax.psum(output_left_factor.astype(jnp.bfloat16), "dp").astype(jnp.float32),
        lax.psum(down_left_factor.astype(jnp.bfloat16), "dp").astype(jnp.float32),
    )
    output_norm_factor = (
        attention_output_magnitude
        * out_inner
        / (output_column_norm * output_column_norm * output_column_norm)
    )
    down_norm_factor = (
        feedforward_output_magnitude
        * down_inner
        / (down_column_norm * down_column_norm * down_column_norm)
    )
    output_left_factor = output_left_factor - adapter_scale * jnp.dot(
        output_merged_weight * output_norm_factor,
        attention_output_second.T,
        precision=highest_precision,
    )
    down_left_factor = down_left_factor - adapter_scale * jnp.dot(
        down_merged_weight * down_norm_factor,
        feedforward_output_second.T,
        precision=highest_precision,
    )
    output_right_factor = (
        output_right_factor - adapter_scale * output_cross_term * output_norm_factor
    )
    down_right_factor = down_right_factor - adapter_scale * down_cross_term * down_norm_factor
    out_mag = out_inner / output_column_norm
    down_mag = down_inner / down_column_norm
    layer_out = jnp.stack(results)[:, None]
    layer_grad = jnp.stack(input_grads)[:, None]
    return (
        layer_out,
        layer_grad,
        qkv_left,
        qkv_right,
        qkv_mag,
        output_left_factor,
        output_right_factor,
        out_mag,
        gate_left,
        gate_right,
        gate_mag,
        down_left_factor,
        down_right_factor,
        down_mag,
    )


FAR_SLOTS = 128
LANES = 128
VMEM_LIMIT = 56 * 1024 * 1024
f32 = jnp.float32
bf16 = jnp.bfloat16


def fits_fast(mesh):
    return mesh.shape["dp"] == 8 and mesh.shape["tensor"] == 4


def split_high_low(value):
    high = value.astype(bf16)
    return high, (value - high.astype(f32)).astype(bf16)


def adapter_product(first_t, second):
    a_high, a_low = split_high_low(first_t)
    b_high, b_low = split_high_low(second)
    left = jnp.concatenate([a_high, a_low, a_high], axis=0)
    right = jnp.concatenate([b_high, b_high, b_low], axis=0)
    return contract_rows(left, right)


def params(limit=VMEM_LIMIT):
    return pltpu.CompilerParams(vmem_limit_bytes=limit)


def whole_block(shape):
    zeros = (0,) * len(shape)
    return pl.BlockSpec(shape, lambda *_: zeros)


def merge_in(frozen, first_t, second, row_block):
    depth, groups, cols = frozen.shape
    rank = second.shape[1]
    scale = ADAPTER_NUMER / ADAPTER_RANK

    def kernel(w_ref, a_ref, b_ref, v_ref, sq_ref):
        @pl.when(pl.program_id(0) == 0)
        def _():
            sq_ref[...] = jnp.zeros_like(sq_ref)

        for g in range(groups):
            v = w_ref[:, g, :].astype(f32) + scale * adapter_product(a_ref[g], b_ref[g])
            v_ref[:, g * cols : (g + 1) * cols] = v.astype(bf16)
            sq_ref[:, g * cols : (g + 1) * cols] += jnp.sum(v * v, axis=0, keepdims=True)

    return pl.pallas_call(
        kernel,
        grid=(depth // row_block,),
        in_specs=[
            pl.BlockSpec((row_block, groups, cols), lambda i: (i, 0, 0)),
            pl.BlockSpec((groups, rank, row_block), lambda i: (0, 0, i)),
            whole_block((groups, rank, cols)),
        ],
        out_specs=[
            pl.BlockSpec((row_block, groups * cols), lambda i: (i, 0)),
            whole_block((1, groups * cols)),
        ],
        out_shape=[
            jax.ShapeDtypeStruct((depth, groups * cols), bf16),
            jax.ShapeDtypeStruct((1, groups * cols), f32),
        ],
        compiler_params=params(),
        cost_estimate=pl.CostEstimate(
            flops=2 * depth * groups * cols * 48,
            bytes_accessed=4 * depth * groups * cols,
            transcendentals=0,
        ),
        name="merge_in",
    )(frozen, first_t, second)


def merge_out(frozen, first_t, second, row_block):
    depth, cols = frozen.shape
    rank = second.shape[0]
    scale = ADAPTER_NUMER / ADAPTER_RANK

    def kernel(w_ref, a_ref, b_ref, v_ref, sq_ref):
        @pl.when(pl.program_id(0) == 0)
        def _():
            sq_ref[...] = jnp.zeros_like(sq_ref)

        v = w_ref[...].astype(f32) + scale * adapter_product(a_ref[...], b_ref[...])
        v_ref[...] = v.astype(bf16)
        sq_ref[...] += jnp.sum(v * v, axis=0, keepdims=True)

    return pl.pallas_call(
        kernel,
        grid=(depth // row_block,),
        in_specs=[
            pl.BlockSpec((row_block, cols), lambda i: (i, 0)),
            pl.BlockSpec((rank, row_block), lambda i: (0, i)),
            whole_block((rank, cols)),
        ],
        out_specs=[pl.BlockSpec((row_block, cols), lambda i: (i, 0)), whole_block((1, cols))],
        out_shape=[
            jax.ShapeDtypeStruct((depth, cols), bf16),
            jax.ShapeDtypeStruct((1, cols), f32),
        ],
        compiler_params=params(),
        cost_estimate=pl.CostEstimate(
            flops=2 * depth * cols * 48, bytes_accessed=4 * depth * cols, transcendentals=0
        ),
        name="merge_out",
    )(frozen, first_t, second)


def rotate(values, cosine, sine_signed):
    return values * cosine + pltpu.roll(values, HEAD_DIM // 2, 1) * sine_signed


def rotate_back(values, cosine, sine_signed):
    return values * cosine - pltpu.roll(values, HEAD_DIM // 2, 1) * sine_signed


def project_in(tokens, gain, merged, ratio, cosine, sine_signed):
    count, width = tokens.shape
    cols = merged.shape[1] // 3
    heads = cols // HEAD_DIM

    def kernel(x_ref, g_ref, w_ref, s_ref, c_ref, n_ref, a_ref, y_ref):
        part = pl.program_id(0)

        @pl.when(part == 0)
        def _():
            x = x_ref[...].astype(f32)
            a_ref[...] = (x * rms_scale(x) * g_ref[...]).astype(bf16)

        y = jnp.dot(a_ref[...], w_ref[...], preferred_element_type=f32) * s_ref[...]

        @pl.when(part < 2)
        def _():
            for h in range(heads):
                at = slice(h * HEAD_DIM, (h + 1) * HEAD_DIM)
                y_ref[:, at] = rotate(y[:, at], c_ref[...], n_ref[...]).astype(bf16)

        @pl.when(part == 2)
        def _():
            y_ref[...] = y.astype(bf16)

    return pl.pallas_call(
        kernel,
        grid=(3,),
        in_specs=[
            whole_block((count, width)),
            whole_block((1, width)),
            pl.BlockSpec((width, cols), lambda i: (0, i)),
            pl.BlockSpec((1, cols), lambda i: (0, i)),
            whole_block((count, HEAD_DIM)),
            whole_block((count, HEAD_DIM)),
        ],
        out_specs=[whole_block((count, width)), pl.BlockSpec((count, cols), lambda i: (0, i))],
        out_shape=[
            jax.ShapeDtypeStruct((count, width), bf16),
            jax.ShapeDtypeStruct((count, 3 * cols), bf16),
        ],
        compiler_params=params(),
        cost_estimate=pl.CostEstimate(
            flops=2 * count * width * 3 * cols,
            bytes_accessed=2 * (2 * count * width + 3 * cols * (width + count)),
            transcendentals=0,
        ),
        name="project_in",
    )(tokens, gain, merged, ratio, cosine, sine_signed)


def head_shares(q, k, far_k, far_ok):
    scale = 1.0 / math.sqrt(HEAD_DIM)
    own = contract_cols(q, k) * scale
    far = contract_cols(q, far_k) * scale
    rows_at = lax.broadcasted_iota(jnp.int32, own.shape, 0)
    slots_at = lax.broadcasted_iota(jnp.int32, own.shape, 1)
    own = jnp.where(slots_at <= rows_at, own, masked_score)
    far = jnp.where(far_ok > 0, far, masked_score)
    scores = jnp.concatenate([own, far], axis=1)
    top = jnp.max(scores, axis=-1, keepdims=True)
    exponent = jnp.exp(scores - top)
    return exponent / jnp.sum(exponent, axis=-1, keepdims=True)


def store_part(value, refs, inner):
    if len(refs) == 1:
        refs[0][...] = value
        return
    half = value.shape[0] // 2

    @pl.when(inner == 1)
    def _():
        refs[0][...] = value[half:]
        refs[1][...] = value[:half]

    @pl.when(inner != 1)
    def _():
        refs[0][...] = value[:half]
        refs[1][...] = value[half:]


def load_total(refs, inner):
    if len(refs) == 1:
        return refs[0][...].astype(f32)
    mine, other = refs[0][...], refs[1][...]
    flip = inner == 1
    first = jnp.where(flip, other, mine)
    last = jnp.where(flip, mine, other)
    return jnp.concatenate([first, last], axis=0).astype(f32)


def part_shapes(slots, width, pieces):
    return [jax.ShapeDtypeStruct((slots // pieces, width), bf16)] * pieces


def attend(inner, projected, far_pack, out_merged, pieces):
    slots = projected.shape[0]
    cols = projected.shape[1] // 3
    heads = cols // HEAD_DIM
    width = out_merged.shape[1]

    def kernel(i_ref, y_ref, f_ref, w_ref, o_ref, *z_refs):
        far_ok = f_ref[FAR_SLOTS : FAR_SLOTS + 1, :FAR_SLOTS].astype(f32)
        for h in range(heads):
            at = slice(h * HEAD_DIM, (h + 1) * HEAD_DIM)
            far_k = f_ref[:FAR_SLOTS, h * HEAD_DIM : (h + 1) * HEAD_DIM]
            far_v = f_ref[:FAR_SLOTS, cols + h * HEAD_DIM : cols + (h + 1) * HEAD_DIM]
            k = y_ref[:, cols + h * HEAD_DIM : cols + (h + 1) * HEAD_DIM]
            v = y_ref[:, 2 * cols + h * HEAD_DIM : 2 * cols + (h + 1) * HEAD_DIM]
            shares = head_shares(y_ref[:, at], k, far_k, far_ok).astype(bf16)
            values = jnp.concatenate([v, far_v], axis=0)
            o_ref[:, at] = jnp.dot(shares, values, preferred_element_type=f32).astype(bf16)
        part = jnp.dot(o_ref[...], w_ref[...], preferred_element_type=f32).astype(bf16)
        store_part(part, z_refs, i_ref[0])

    return pl.pallas_call(
        kernel,
        in_specs=[pl.BlockSpec(memory_space=pltpu.SMEM)]
        + [pl.BlockSpec(memory_space=pltpu.VMEM)] * 3,
        out_shape=[jax.ShapeDtypeStruct((slots, cols), bf16)]
        + part_shapes(slots, width, pieces),
        compiler_params=params(),
        cost_estimate=pl.CostEstimate(
            flops=2 * slots * cols * (width + 2 * (slots + FAR_SLOTS)),
            bytes_accessed=2 * (cols * width + slots * (4 * cols + width)),
            transcendentals=heads * slots * (slots + FAR_SLOTS),
        ),
        name="attend",
    )(inner, projected, far_pack, out_merged)


def feed_forward(
    scalars, branch_sum, tokens, upstream, out_ratio, down_ratio, gain, merged, ratio, down_merged
):
    slots, width = tokens.shape
    units = down_merged.shape[0]
    blocks = units // LANES
    pieces = len(branch_sum)

    def kernel(*refs):
        n_ref, *refs = refs
        s_refs, refs = refs[:pieces], refs[pieces:]
        x_ref, u_ref, or_ref, dr_ref, g_ref, wg_ref, wu_ref, rg_ref, ru_ref, wd_ref = refs[:10]
        h_ref, b_ref, d2_ref, hid_ref, dg_ref, du_ref, cg_ref, cu_ref, cd_ref, y_ref = refs[10:20]
        db_refs, (dba_ref, ya_ref) = refs[20:-2], refs[-2:]
        at = pl.program_id(0)

        def live_rows():
            return lax.broadcasted_iota(jnp.int32, (slots, 1), 0) < n_ref[0]

        @pl.when(at == 0)
        def _():
            live = live_rows()
            branch = load_total(s_refs, n_ref[1]) * or_ref[...]
            h = x_ref[...].astype(f32) + jnp.where(live, branch, 0.0)
            h_ref[...] = h
            b_ref[...] = (h * rms_scale(h) * g_ref[...]).astype(bf16)
            d2_ref[...] = jnp.where(live, u_ref[...].astype(f32) * dr_ref[...], 0.0).astype(bf16)
            dba_ref[...] = jnp.zeros_like(dba_ref)
            ya_ref[...] = jnp.zeros_like(ya_ref)

        weight = jnp.concatenate([wg_ref[...], wu_ref[...]], axis=1)
        raw = jnp.dot(b_ref[...], weight, preferred_element_type=f32)
        gate = raw[:, :LANES] * rg_ref[...]
        up = raw[:, LANES:] * ru_ref[...]
        sigmoid = jax.nn.sigmoid(gate)
        activated = gate * sigmoid
        hidden = (activated * up).astype(bf16)
        hid_ref[...] = hidden
        dhidden = contract_cols(d2_ref[...], wd_ref[...])
        dgate = dhidden * up * sigmoid * (1.0 + gate * (1.0 - sigmoid))
        dup = dhidden * activated
        cg_ref[...] = jnp.sum(dgate * raw[:, :LANES], axis=0, keepdims=True)
        cu_ref[...] = jnp.sum(dup * raw[:, LANES:], axis=0, keepdims=True)
        dgate = (dgate * rg_ref[...]).astype(bf16)
        dup = (dup * ru_ref[...]).astype(bf16)
        dg_ref[...] = dgate
        du_ref[...] = dup
        dba_ref[...] += contract_cols(jnp.concatenate([dgate, dup], axis=1), weight)
        ya_ref[...] += jnp.dot(hidden, wd_ref[...], preferred_element_type=f32)

        @pl.when(at == blocks - 1)
        def _():
            store_part(dba_ref[...].astype(bf16), db_refs, n_ref[1])
            y_ref[...] = ya_ref[...].astype(bf16)
            d2 = jnp.where(live_rows(), u_ref[...].astype(f32), 0.0)
            cd_ref[...] = jnp.sum(d2 * ya_ref[...], axis=0, keepdims=True)

    row = whole_block((1, width))
    full = whole_block((slots, width))
    part = whole_block((slots // pieces, width))
    unit_cols = pl.BlockSpec((slots, LANES), lambda i: (0, i))
    unit_row = pl.BlockSpec((1, LANES), lambda i: (0, i))
    return pl.pallas_call(
        kernel,
        grid=(blocks,),
        in_specs=[pl.BlockSpec(memory_space=pltpu.SMEM)]
        + [part] * pieces
        + [
            full,
            full,
            row,
            row,
            row,
            pl.BlockSpec((width, LANES), lambda i: (0, i)),
            pl.BlockSpec((width, LANES), lambda i: (0, blocks + i)),
            unit_row,
            pl.BlockSpec((1, LANES), lambda i: (0, blocks + i)),
            pl.BlockSpec((LANES, width), lambda i: (i, 0)),
        ],
        out_specs=[full] * 3 + [unit_cols] * 3 + [unit_row] * 2 + [row, full] + [part] * pieces,
        out_shape=[
            jax.ShapeDtypeStruct((slots, width), f32),
            jax.ShapeDtypeStruct((slots, width), bf16),
            jax.ShapeDtypeStruct((slots, width), bf16),
            jax.ShapeDtypeStruct((slots, units), bf16),
            jax.ShapeDtypeStruct((slots, units), bf16),
            jax.ShapeDtypeStruct((slots, units), bf16),
            jax.ShapeDtypeStruct((1, units), f32),
            jax.ShapeDtypeStruct((1, units), f32),
            jax.ShapeDtypeStruct((1, width), f32),
            jax.ShapeDtypeStruct((slots, width), bf16),
        ]
        + part_shapes(slots, width, pieces),
        scratch_shapes=[
            pltpu.VMEM((slots, width), f32),
            pltpu.VMEM((slots, width), f32),
        ],
        compiler_params=params(),
        cost_estimate=pl.CostEstimate(
            flops=2 * slots * width * units * 6,
            bytes_accessed=2 * 3 * width * units + 16 * slots * width,
            transcendentals=slots * units,
        ),
        name="feed_forward",
    )(
        scalars,
        *branch_sum,
        tokens,
        upstream,
        out_ratio,
        down_ratio,
        gain,
        merged,
        merged,
        ratio,
        ratio,
        down_merged,
    )


def attend_back(
    scalars,
    db_sum,
    middle,
    upstream,
    branch_sum,
    gain,
    out_ratio,
    out_merged,
    projected,
    far_pack,
    cosine,
    sine_signed,
):
    slots, width = middle.shape
    cols = projected.shape[1] // 3
    heads = cols // HEAD_DIM
    scale = 1.0 / math.sqrt(HEAD_DIM)
    pieces = len(db_sum)

    def kernel(*refs):
        n_ref, *refs = refs
        e_refs, s_refs, refs = refs[:pieces], refs[pieces : 2 * pieces], refs[2 * pieces :]
        h_ref, u_ref, g_ref, or_ref, w_ref, y_ref, f_ref, c_ref, sn_ref = refs[:9]
        dh_ref, d1_ref, co_ref, dy_ref, far_ref, do_ref = refs[9:]
        live = lax.broadcasted_iota(jnp.int32, (slots, 1), 0) < n_ref[0]
        h = h_ref[...]
        back = rms_back(h, rms_scale(h), g_ref[...], load_total(e_refs, n_ref[1]))
        dh = u_ref[...].astype(f32) + back
        dh_ref[...] = dh
        d1 = jnp.where(live, dh, 0.0)
        co_ref[...] = jnp.sum(d1 * load_total(s_refs, n_ref[1]), axis=0, keepdims=True)
        d1_ref[...] = (d1 * or_ref[...]).astype(bf16)
        do_ref[...] = contract_cols(d1_ref[...], w_ref[...]).astype(bf16)
        far_ok = f_ref[FAR_SLOTS : FAR_SLOTS + 1, :FAR_SLOTS].astype(f32)
        for i in range(heads):
            at = slice(i * HEAD_DIM, (i + 1) * HEAD_DIM)
            k_at = slice(cols + i * HEAD_DIM, cols + (i + 1) * HEAD_DIM)
            v_at = slice(2 * cols + i * HEAD_DIM, 2 * cols + (i + 1) * HEAD_DIM)
            q = y_ref[:, at]
            far_k = f_ref[:FAR_SLOTS, at]
            shares = head_shares(q, y_ref[:, k_at], far_k, far_ok)
            keys = jnp.concatenate([y_ref[:, k_at], far_k], axis=0)
            values = jnp.concatenate([y_ref[:, v_at], f_ref[:FAR_SLOTS, k_at]], axis=0)
            do = do_ref[:, at]
            share_grad = contract_cols(do, values)
            inner = jnp.sum(shares * share_grad, axis=-1, keepdims=True)
            score_grad = (shares * (share_grad - inner)).astype(bf16)
            dq = jnp.dot(score_grad, keys, preferred_element_type=f32) * scale
            dk = contract_rows(score_grad, q) * scale
            dv = contract_rows(shares.astype(bf16), do)
            dy_ref[:, at] = rotate_back(dq, c_ref[...], sn_ref[...])
            dy_ref[:, k_at] = dk[:slots]
            dy_ref[:, v_at] = dv[:slots]
            far_ref[:, at] = dk[slots:].astype(bf16)
            far_ref[:, k_at] = dv[slots:].astype(bf16)

    operands = (
        scalars,
        *db_sum,
        *branch_sum,
        middle,
        upstream,
        gain,
        out_ratio,
        out_merged,
        projected,
        far_pack,
        cosine,
        sine_signed,
    )
    return pl.pallas_call(
        kernel,
        in_specs=[pl.BlockSpec(memory_space=pltpu.SMEM)]
        + [pl.BlockSpec(memory_space=pltpu.VMEM)] * (len(operands) - 1),
        out_shape=[
            jax.ShapeDtypeStruct((slots, width), f32),
            jax.ShapeDtypeStruct((slots, width), bf16),
            jax.ShapeDtypeStruct((1, width), f32),
            jax.ShapeDtypeStruct((slots, 3 * cols), f32),
            jax.ShapeDtypeStruct((FAR_SLOTS, 2 * cols), bf16),
        ],
        scratch_shapes=[pltpu.VMEM((slots, cols), bf16)],
        compiler_params=params(),
        cost_estimate=pl.CostEstimate(
            flops=2 * slots * cols * (width + 5 * (slots + FAR_SLOTS)),
            bytes_accessed=2 * (cols * width + slots * (8 * width + 9 * cols)),
            transcendentals=heads * slots * (slots + FAR_SLOTS),
        ),
        name="attend_back",
    )(*operands)


def project_back(inner, dy, returned, projected, cosine, sine_signed, ratio, merged, pieces):
    slots, total = dy.shape
    cols = total // 3
    heads = cols // HEAD_DIM
    width = merged.shape[0]
    blocks = 4
    step = width // blocks

    def kernel(i_ref, d_ref, r_ref, y_ref, c_ref, sn_ref, s_ref, w_ref, o_ref, cs_ref, *da_refs):
        @pl.when(pl.program_id(0) == 0)
        def _():
            for i in range(3 * heads):
                at = slice(i * HEAD_DIM, (i + 1) * HEAD_DIM)
                d = d_ref[:, at]
                raw = y_ref[:, at].astype(f32)
                if i >= heads:
                    back = slice((i - heads) * HEAD_DIM, (i - heads + 1) * HEAD_DIM)
                    low = d[:FAR_SLOTS] + r_ref[:FAR_SLOTS, back].astype(f32)
                    d = jnp.concatenate([low, d[FAR_SLOTS:]], axis=0)
                if heads <= i < 2 * heads:
                    d = rotate_back(d, c_ref[...], sn_ref[...])
                if i < 2 * heads:
                    raw = rotate_back(raw, c_ref[...], sn_ref[...])
                cs_ref[:, at] = jnp.sum(d * raw, axis=0, keepdims=True)
                o_ref[:, at] = (d * s_ref[:, at]).astype(bf16)

        store_part(contract_cols(o_ref[...], w_ref[...]).astype(bf16), da_refs, i_ref[0])

    return pl.pallas_call(
        kernel,
        grid=(blocks,),
        in_specs=[
            pl.BlockSpec(memory_space=pltpu.SMEM),
            whole_block((slots, total)),
            whole_block(returned.shape),
            whole_block((slots, total)),
            whole_block((slots, HEAD_DIM)),
            whole_block((slots, HEAD_DIM)),
            whole_block((1, total)),
            pl.BlockSpec((step, total), lambda i: (i, 0)),
        ],
        out_specs=[
            whole_block((slots, total)),
            whole_block((1, total)),
        ]
        + [pl.BlockSpec((slots // pieces, step), lambda i: (0, i))] * pieces,
        out_shape=[
            jax.ShapeDtypeStruct((slots, total), bf16),
            jax.ShapeDtypeStruct((1, total), f32),
        ]
        + part_shapes(slots, width, pieces),
        compiler_params=params(),
        cost_estimate=pl.CostEstimate(
            flops=2 * slots * total * width,
            bytes_accessed=2 * (total * width + slots * (width + 5 * total)),
            transcendentals=0,
        ),
        name="project_back",
    )(inner, dy, returned, projected, cosine, sine_signed, ratio, merged)


LINE_PAIRS = [(0, 1), (1, 0), (2, 3), (3, 2)]
LINE_ACROSS = [(0, 3), (3, 0), (1, 2), (2, 1)]


def tensor_sum(parts):
    if len(parts) == 1:
        return [lax.psum(parts[0], "tensor")]
    keep, send = parts
    pair = keep + lax.ppermute(send, "tensor", LINE_PAIRS)
    total = pair + lax.ppermute(pair, "tensor", LINE_ACROSS)
    return [total, lax.ppermute(total, "tensor", LINE_PAIRS)]


def line_total(value):
    value = value + lax.ppermute(value, "tensor", LINE_PAIRS)
    return value + lax.ppermute(value, "tensor", LINE_ACROSS)


def dp_total(value, line_rows):
    me = lax.axis_index("dp")
    hops = (1, 2, 4)
    for hop in hops:
        half = value.shape[1] // 2
        low, high = value[:, :half], value[:, half:]
        upper = (me & hop) != 0
        keep = jnp.where(upper, high, low)
        send = jnp.where(upper, low, high)
        value = keep + lax.ppermute(send, "dp", [(i, i ^ hop) for i in range(8)])
    value = jnp.concatenate([line_total(value[:line_rows]), value[line_rows:]], axis=0)
    for hop in reversed(hops):
        upper = (me & hop) != 0
        other = lax.ppermute(value, "dp", [(i, i ^ hop) for i in range(8)])
        value = jnp.concatenate(
            [jnp.where(upper, other, value), jnp.where(upper, value, other)], axis=1
        )
    return value.astype(f32)


def pair_exchange(pack, distance, sibling_distance):
    held = [pack] + [
        lax.ppermute(pack, "dp", [(i, i ^ hop) for i in range(8)]) for hop in (2, 4, 6)
    ]

    def pick(index):
        return lax.select_n(index // 2, *held)

    asked = pick(sibling_distance & 6)
    across = lax.ppermute(asked, "dp", [(i, i ^ 1) for i in range(8)])
    return jnp.where(distance % 2 == 1, across, pick(distance & 6))


def block_rows_of(second, groups):
    rank, cols = second.shape[1:]
    parts = []
    for g in range(groups):
        parts.append(jnp.pad(second[g], ((g * rank, (groups - 1 - g) * rank), (0, 0))))
    return jnp.concatenate(parts, axis=1)


def low_dot(left, right, dims):
    return lax.dot_general(
        left.astype(bf16), right.astype(bf16), (dims, ((), ())), preferred_element_type=f32
    )


def adapter_in(inputs_seen, grads_scaled, inner, square, magnitude, merged, first_t, second):
    groups, rank, cols = second.shape
    scale = ADAPTER_NUMER / ADAPTER_RANK
    norm = jnp.sqrt(square)
    share = inner * magnitude / (square * norm)
    wide = block_rows_of(second, groups)
    tall = first_t.reshape(groups * rank, -1)
    seen = low_dot(inputs_seen, tall, ((1,), (1,)))
    sent = low_dot(grads_scaled, wide, ((1,), (1,)))
    left = low_dot(sent, inputs_seen, ((0,), (0,))) - low_dot(wide * share, merged, ((1,), (1,)))
    right = low_dot(seen, grads_scaled, ((0,), (0,))) - low_dot(tall, merged, ((1,), (0,))) * share
    right = jnp.stack(
        [right[g * rank : (g + 1) * rank, g * cols : (g + 1) * cols] for g in range(groups)]
    )
    return (
        scale * left.reshape(groups, rank, -1),
        scale * right,
        (inner / norm).reshape(groups, cols),
    )


def adapter_out(inputs_seen, grads_scaled, inner, square, magnitude, merged, first_t, second):
    scale = ADAPTER_NUMER / ADAPTER_RANK
    norm = jnp.sqrt(square)
    share = inner * magnitude / (square * norm)
    seen = low_dot(inputs_seen, first_t, ((1,), (1,)))
    sent = low_dot(grads_scaled, second, ((1,), (1,)))
    left = low_dot(sent, inputs_seen, ((0,), (0,))) - low_dot(second * share, merged, ((1,), (1,)))
    right = (
        low_dot(seen, grads_scaled, ((0,), (0,))) - low_dot(first_t, merged, ((1,), (0,))) * share
    )
    return scale * left, scale * right, inner / norm


def fast_device(
    inputs,
    lengths,
    prompt_mask,
    partner,
    positions,
    attn_gain,
    mlp_gain,
    attention_input_frozen,
    attention_input_first,
    attention_input_second,
    attention_input_magnitude,
    attention_output_frozen,
    attention_output_first,
    attention_output_second,
    attention_output_magnitude,
    feedforward_input_frozen,
    feedforward_input_first,
    feedforward_input_second,
    feedforward_input_magnitude,
    feedforward_output_frozen,
    feedforward_output_first,
    feedforward_output_second,
    feedforward_output_magnitude,
    grad_out,
):
    micros, _, slots, width = inputs.shape
    cols = attention_input_frozen.shape[2]
    attn_row = attn_gain.astype(f32)[None]
    mlp_row = mlp_gain.astype(f32)[None]
    qkv_first_t = jnp.swapaxes(attention_input_first, 1, 2)
    gate_first_t = jnp.swapaxes(feedforward_input_first, 1, 2)
    out_first_t = attention_output_first.T
    down_first_t = feedforward_output_first.T
    qkv_magnitude = attention_input_magnitude.reshape(1, -1)
    gate_magnitude = feedforward_input_magnitude.reshape(1, -1)
    out_magnitude = attention_output_magnitude[None]
    down_magnitude = feedforward_output_magnitude[None]

    me = lax.axis_index("dp")
    distance = partner[:, 0] ^ me
    sibling_distance = lax.ppermute(distance, "dp", [(i, i ^ 1) for i in range(8)])

    qkv_merged, qkv_square = merge_in(
        attention_input_frozen, qkv_first_t, attention_input_second, 256
    )
    qkv_ratio = qkv_magnitude * lax.rsqrt(qkv_square)
    indices = jnp.arange(HEAD_DIM // 2, dtype=f32)
    inverse = rope_base ** (-2.0 * indices / HEAD_DIM)
    angles = positions.reshape(micros * slots).astype(f32)[:, None] * inverse[None, :]
    cosine, sine = jnp.cos(angles), jnp.sin(angles)
    cosine = jnp.concatenate([cosine, cosine], axis=1)
    sine_signed = jnp.concatenate([-sine, sine], axis=1)
    tokens = inputs.reshape(micros * slots, width)
    upstream = grad_out.reshape(micros * slots, width)
    normed, projected = project_in(
        tokens, attn_row, qkv_merged, qkv_ratio, cosine, sine_signed
    )

    def rows(array, micro_at):
        return array[micro_at * slots : (micro_at + 1) * slots]

    far_packs = []
    for m in range(micros):
        flags = prompt_mask[m, :, :FAR_SLOTS].astype(bf16)
        flags = jnp.pad(flags, ((0, 15), (0, 2 * cols - FAR_SLOTS)))
        pack = jnp.concatenate([rows(projected, m)[:FAR_SLOTS, cols:], flags], axis=0)
        far_packs.append(pair_exchange(pack, distance[m], sibling_distance[m]))

    out_merged, out_square = merge_out(
        attention_output_frozen, out_first_t, attention_output_second, 256
    )
    down_merged, down_square = merge_out(
        feedforward_output_frozen, down_first_t, feedforward_output_second, 128
    )
    pieces = (2, 1)
    line_at = lax.axis_index("tensor")
    inner = ((line_at == 1) | (line_at == 2)).astype(jnp.int32)[None]
    scalars = [jnp.concatenate([lengths[m], inner]) for m in range(micros)]
    squares = line_total(jnp.concatenate([out_square, down_square], axis=0))
    out_square, down_square = squares[:1], squares[1:]
    out_ratio = out_magnitude * lax.rsqrt(out_square)
    down_ratio = down_magnitude * lax.rsqrt(down_square)

    attended, branch_sums = [], []
    for m in range(micros):
        seen, *part = attend(inner, rows(projected, m), far_packs[m], out_merged, pieces[m])
        attended.append(seen)
        branch_sums.append(tensor_sum(part))
    gate_second, _ = lax.optimization_barrier((feedforward_input_second, attended[0]))
    gate_merged, gate_square = merge_in(feedforward_input_frozen, gate_first_t, gate_second, 128)
    gate_ratio = gate_magnitude * lax.rsqrt(gate_square)

    middles, normed_mlp, hiddens, gate_grads, gate_inner = [], [], [], [], 0.0
    db_sums, down_parts, down_grads, down_inner = [], [], [], 0.0
    for m in range(micros):
        middle, b, d2, hidden, dgate, dup, c_gate, c_up, c_down, y, *db = feed_forward(
            scalars[m],
            branch_sums[m],
            rows(tokens, m),
            rows(upstream, m),
            out_ratio,
            down_ratio,
            mlp_row,
            gate_merged,
            gate_ratio,
            down_merged,
        )
        middles.append(middle)
        normed_mlp.append(b)
        hiddens.append(hidden)
        gate_grads.append(jnp.concatenate([dgate, dup], axis=1))
        gate_inner = gate_inner + jnp.concatenate([c_gate, c_up], axis=1)
        down_inner = down_inner + c_down
        down_grads.append(d2)
        db_sums.append(tensor_sum(db))
        down_parts.append(y)
    down_inner = line_total(down_inner)

    middle_grads, out_grads, out_inner, qkv_grads, qkv_inner, da_sums = [], [], 0.0, [], 0.0, []
    for m in range(micros):
        dh, d1, c_out, dy, far_grad = attend_back(
            scalars[m],
            db_sums[m],
            middles[m],
            rows(upstream, m),
            branch_sums[m],
            mlp_row,
            out_ratio,
            out_merged,
            rows(projected, m),
            far_packs[m],
            rows(cosine, m),
            rows(sine_signed, m),
        )
        middle_grads.append(dh)
        out_grads.append(d1)
        out_inner = out_inner + c_out
        returned = pair_exchange(far_grad, distance[m], sibling_distance[m])
        dqkv, c_qkv, *da = project_back(
            inner,
            dy,
            returned,
            rows(projected, m),
            rows(cosine, m),
            rows(sine_signed, m),
            qkv_ratio,
            qkv_merged,
            2,
        )
        qkv_grads.append(dqkv)
        qkv_inner = qkv_inner + c_qkv
        da_sums.append(tensor_sum(da))
    down_sums = [tensor_sum([y])[0] for y in down_parts]

    def assemble(total):
        if len(total) == 1:
            return total[0].astype(f32)
        first = jnp.where(inner[0] == 1, total[1], total[0])
        last = jnp.where(inner[0] == 1, total[0], total[1])
        return jnp.concatenate([first, last], axis=0).astype(f32)

    results, input_grads = [], []
    for m in range(micros):
        live = (jnp.arange(slots) < lengths[m, 0])[:, None]
        branch = down_sums[m].astype(f32) * down_ratio
        results.append((middles[m] + jnp.where(live, branch, 0.0)).astype(bf16))
        x = rows(tokens, m).astype(f32)
        back = rms_back(x, rms_scale(x), attn_row, assemble(da_sums[m]))
        input_grads.append((middle_grads[m] + back).astype(bf16))

    units = feedforward_input_frozen.shape[2]
    gate_left, gate_right, gate_mag = adapter_in(
        jnp.concatenate(normed_mlp, axis=0),
        jnp.concatenate(gate_grads, axis=0),
        gate_inner,
        gate_square,
        gate_magnitude,
        gate_merged,
        gate_first_t,
        feedforward_input_second,
    )
    down_left, down_right, down_mag = adapter_out(
        jnp.concatenate(hiddens, axis=0),
        jnp.concatenate(down_grads, axis=0),
        down_inner,
        down_square,
        down_magnitude,
        down_merged,
        down_first_t,
        feedforward_output_second,
    )
    rank = down_left.shape[0]

    def stack_rows(pieces, height):
        wide = [jnp.pad(p.astype(bf16), ((0, 0), (0, width - p.shape[1]))) for p in pieces]
        total = jnp.concatenate(wide, axis=0)
        return jnp.pad(total, ((0, height - total.shape[0]), (0, 0)))

    early = stack_rows(
        [
            gate_left.reshape(2 * rank, width),
            down_right,
            gate_right.reshape(2 * rank, units),
            down_left,
            gate_mag,
            down_mag,
        ],
        7 * rank,
    )
    early = dp_total(early, 3 * rank)
    gate_left = early[: 2 * rank].reshape(2, rank, width)
    down_right = early[2 * rank : 3 * rank]
    gate_right = early[3 * rank : 5 * rank, :units].reshape(2, rank, units)
    down_left = early[5 * rank : 6 * rank, :units]
    gate_mag = early[6 * rank : 6 * rank + 2, :units]
    down_mag = early[6 * rank + 2]

    out_left, out_right, out_mag = adapter_out(
        jnp.concatenate(attended, axis=0),
        jnp.concatenate(out_grads, axis=0),
        out_inner,
        out_square,
        out_magnitude,
        out_merged,
        out_first_t,
        attention_output_second,
    )
    qkv_left, qkv_right, qkv_mag = adapter_in(
        normed,
        jnp.concatenate(qkv_grads, axis=0),
        qkv_inner / qkv_ratio,
        qkv_square,
        qkv_magnitude,
        qkv_merged,
        qkv_first_t,
        attention_input_second,
    )
    late = stack_rows(
        [
            qkv_left.reshape(3 * rank, width),
            out_right,
            jnp.concatenate([qkv_right[0], qkv_right[1], qkv_right[2], out_left], axis=1),
            qkv_mag.reshape(1, 3 * cols),
            out_mag,
        ],
        6 * rank,
    )
    late = dp_total(late, 4 * rank)
    qkv_left = late[: 3 * rank].reshape(3, rank, width)
    out_right = late[3 * rank : 4 * rank]
    rights = late[4 * rank : 5 * rank]
    qkv_right = jnp.stack([rights[:, g * cols : (g + 1) * cols] for g in range(3)])
    out_left = rights[:, 3 * cols :]
    qkv_mag = late[5 * rank, : 3 * cols].reshape(3, cols)
    out_mag = late[5 * rank + 1]

    return (
        jnp.stack(results)[:, None],
        jnp.stack(input_grads)[:, None],
        jnp.swapaxes(qkv_left, 1, 2),
        qkv_right,
        qkv_mag,
        out_left.T,
        out_right,
        out_mag,
        jnp.swapaxes(gate_left, 1, 2),
        gate_right,
        gate_mag,
        down_left.T,
        down_right,
        down_mag,
    )


def solution(mesh):
    in_specs = (
        P(None, "dp", None, None),
        P(None, "dp"),
        P(None, "dp", None),
        P(None, "dp"),
        P(None, "dp", None),
        P(),
        P(),
        P(None, None, "tensor"),
        P(),
        P(None, None, "tensor"),
        P(None, "tensor"),
        P("tensor", None),
        P("tensor", None),
        P(),
        P(),
        P(None, None, "tensor"),
        P(),
        P(None, None, "tensor"),
        P(None, "tensor"),
        P("tensor", None),
        P("tensor", None),
        P(),
        P(),
        P(None, "dp", None, None),
    )
    out_specs = (
        P(None, "dp", None, None),
        P(None, "dp", None, None),
        P(),
        P(None, None, "tensor"),
        P(None, "tensor"),
        P("tensor", None),
        P(),
        P(),
        P(),
        P(None, None, "tensor"),
        P(None, "tensor"),
        P("tensor", None),
        P(),
        P(),
    )
    device_step = fast_device if fits_fast(mesh) else general_device
    return jax.shard_map(
        device_step, mesh=mesh, in_specs=in_specs, out_specs=out_specs, check_vma=False
    )
```

```python
import math

import jax
import jax.numpy as jnp
from jax import lax
from jax.experimental import pallas as pl
from jax.experimental.pallas import tpu as pltpu
from jax.sharding import PartitionSpec as P

HEAD_DIM = 128
ADAPTER_RANK = 16
ADAPTER_NUMER = 32


epsilon = 1e-05
rope_base = 10000.0
highest_precision = lax.Precision.HIGHEST
masked_score = -1e30


def rms_scale(values):
    return lax.rsqrt(jnp.mean(values * values, axis=-1, keepdims=True) + epsilon)


def rms_back(values, scale_rows, gain_row, gradient):
    scaled_update = gradient * gain_row
    normal = values * scale_rows
    return scale_rows * (
        scaled_update - normal * jnp.mean(scaled_update * normal, axis=-1, keepdims=True)
    )


def turn_half(values):
    middle = values.shape[-1] // 2
    return jnp.concatenate([-values[..., middle:], values[..., :middle]], axis=-1)


def rope_tables(positions, head_size):
    indices = jnp.arange(head_size // 2, dtype=jnp.float32)
    inverse = rope_base ** (-2.0 * indices / head_size)
    angles = positions.astype(jnp.float32)[:, None] * inverse[None, :]
    angles = jnp.concatenate([angles, angles], axis=-1)
    return (jnp.cos(angles)[:, None, :], jnp.sin(angles)[:, None, :])


def contract_rows(left_factor, right_factor):
    return lax.dot_general(
        left_factor, right_factor, (((0,), (0,)), ((), ())), preferred_element_type=jnp.float32
    )


def contract_cols(left_factor, right_factor):
    return lax.dot_general(
        left_factor, right_factor, (((1,), (1,)), ((), ())), preferred_element_type=jnp.float32
    )


def pick_partner(partner_row, far_slots, current, pieces):
    piece_rows = pieces[0].shape[0]
    wanted = partner_row * far_slots + jnp.arange(far_slots, dtype=jnp.int32)
    inside = (wanted >= 0) & (wanted < piece_rows)
    clipped = jnp.clip(wanted, 0, piece_rows - 1)
    packed = jnp.where(inside[:, None], jnp.take(pieces[0], clipped, axis=0), current[0])
    flags = jnp.where(inside, jnp.take(pieces[1], clipped, axis=0), current[1])
    return (packed, flags)


def place_far(partner_row, far_grad, row_count):
    far_slots = far_grad.shape[0]
    owners = jnp.arange(row_count // far_slots, dtype=jnp.int32)
    term = jnp.where((owners == partner_row)[:, None, None], far_grad[None], 0.0)
    return term.reshape(row_count, far_grad.shape[1])


def column_gradient_list(
    weight_total,
    merged_matrix,
    column_norm_value,
    column_magnitude,
    left_factor,
    right_factor,
    adapter_scale,
):
    inner = jnp.sum(weight_total * merged_matrix, axis=0)
    merged_matrix_gradient = (
        column_magnitude
        / column_norm_value
        * (weight_total - inner / (column_norm_value * column_norm_value) * merged_matrix)
    )
    left_factor_gradient = adapter_scale * jnp.einsum(
        "ypz,pvz->pyv", merged_matrix_gradient, right_factor, precision=highest_precision
    )
    right_factor_gradient = adapter_scale * jnp.einsum(
        "emn,mez->enz", left_factor, merged_matrix_gradient, precision=highest_precision
    )
    return (left_factor_gradient, right_factor_gradient, inner / column_norm_value)


def row_pieces_list(
    weight_total,
    merged_matrix,
    column_norm_value,
    column_magnitude,
    left_factor,
    right_factor,
    adapter_scale,
):
    scaled_update = weight_total * (column_magnitude / column_norm_value)
    inner = jnp.sum(weight_total * merged_matrix, axis=0)
    left_factor_part = adapter_scale * jnp.dot(
        scaled_update, right_factor.T, precision=highest_precision
    )
    right_factor_part = adapter_scale * jnp.dot(
        left_factor.T, scaled_update, precision=highest_precision
    )
    return (inner, left_factor_part, right_factor_part)


def general_device(
    inputs,
    lengths,
    prompt_mask,
    partner,
    positions,
    attn_gain,
    mlp_gain,
    attention_input_frozen,
    attention_input_first,
    attention_input_second,
    attention_input_magnitude,
    attention_output_frozen,
    attention_output_first,
    attention_output_second,
    attention_output_magnitude,
    feedforward_input_frozen,
    feedforward_input_first,
    feedforward_input_second,
    feedforward_input_magnitude,
    feedforward_output_frozen,
    feedforward_output_first,
    feedforward_output_second,
    feedforward_output_magnitude,
    grad_out,
):
    micro_count = inputs.shape[0]
    slot_count = inputs.shape[2]
    model_width = inputs.shape[3]
    head_cols = attention_input_frozen.shape[2]
    head_count = head_cols // HEAD_DIM
    unit_count = feedforward_input_frozen.shape[2]
    adapter_scale = ADAPTER_NUMER / ADAPTER_RANK
    score_scale = 1.0 / math.sqrt(HEAD_DIM)
    block_rows = min(512, slot_count)
    block_count = slot_count // block_rows
    attn_scale = attn_gain.astype(jnp.float32)
    mlp_scale = mlp_gain.astype(jnp.float32)
    query_key_value_merged = attention_input_frozen.astype(
        jnp.float32
    ) + adapter_scale * jnp.einsum(
        "kdr,kro->dko", attention_input_first, attention_input_second, precision=highest_precision
    )
    query_key_value_norm = jnp.sqrt(
        jnp.sum(query_key_value_merged * query_key_value_merged, axis=0)
    )
    qkv_weight = (
        (query_key_value_merged * (attention_input_magnitude / query_key_value_norm))
        .astype(jnp.bfloat16)
        .reshape(model_width, 3 * head_cols)
    )
    gate_merged_weight = feedforward_input_frozen.astype(jnp.float32) + adapter_scale * jnp.einsum(
        "kdr,kro->dko",
        feedforward_input_first,
        feedforward_input_second,
        precision=highest_precision,
    )
    gate_column_norm = jnp.sqrt(jnp.sum(gate_merged_weight * gate_merged_weight, axis=0))
    gate_up_weight = (
        (gate_merged_weight * (feedforward_input_magnitude / gate_column_norm))
        .astype(jnp.bfloat16)
        .reshape(model_width, 2 * unit_count)
    )
    output_merged_weight = attention_output_frozen.astype(jnp.float32) + adapter_scale * jnp.dot(
        attention_output_first, attention_output_second, precision=highest_precision
    )
    down_merged_weight = feedforward_output_frozen.astype(jnp.float32) + adapter_scale * jnp.dot(
        feedforward_output_first, feedforward_output_second, precision=highest_precision
    )
    out_square = jnp.sum(output_merged_weight * output_merged_weight, axis=0)
    down_square = jnp.sum(down_merged_weight * down_merged_weight, axis=0)
    output_cross_term = jnp.dot(
        attention_output_first.T, output_merged_weight, precision=highest_precision
    )
    down_cross_term = jnp.dot(
        feedforward_output_first.T, down_merged_weight, precision=highest_precision
    )
    out_square, down_square, output_cross_term, down_cross_term = (
        lax.psum(out_square.astype(jnp.bfloat16), "tensor").astype(jnp.float32),
        lax.psum(down_square.astype(jnp.bfloat16), "tensor").astype(jnp.float32),
        lax.psum(output_cross_term.astype(jnp.bfloat16), "tensor").astype(jnp.float32),
        lax.psum(down_cross_term.astype(jnp.bfloat16), "tensor").astype(jnp.float32),
    )
    output_column_norm = jnp.sqrt(out_square)
    down_column_norm = jnp.sqrt(down_square)
    out_weight = (output_merged_weight * (attention_output_magnitude / output_column_norm)).astype(
        jnp.bfloat16
    )
    down_weight = (down_merged_weight * (feedforward_output_magnitude / down_column_norm)).astype(
        jnp.bfloat16
    )
    grad_qkv = jnp.zeros((model_width, 3 * head_cols), jnp.float32)
    output_projection_gradient = jnp.zeros((head_cols, model_width), jnp.float32)
    grad_gate_up = jnp.zeros((model_width, 2 * unit_count), jnp.float32)
    down_projection_gradient = jnp.zeros((unit_count, model_width), jnp.float32)
    results = []
    input_grads = []
    for micro_at in range(micro_count):
        tokens = inputs[micro_at, 0].astype(jnp.float32)
        length_now = lengths[micro_at, 0]
        partner_row = partner[micro_at, 0]
        cosine, sine_tab = rope_tables(positions[micro_at, 0], HEAD_DIM)
        live_mask = (jnp.arange(slot_count) < length_now).astype(jnp.float32)[:, None]
        attn_rows = rms_scale(tokens)
        normed = (tokens * attn_rows * attn_scale).astype(jnp.bfloat16)
        projected = jnp.dot(normed, qkv_weight, preferred_element_type=jnp.float32).reshape(
            slot_count, 3, head_count, HEAD_DIM
        )
        queries = (projected[:, 0] * cosine + turn_half(projected[:, 0]) * sine_tab).astype(
            jnp.bfloat16
        )
        keys_rot = (projected[:, 1] * cosine + turn_half(projected[:, 1]) * sine_tab).astype(
            jnp.bfloat16
        )
        values_in = projected[:, 2].astype(jnp.bfloat16)
        own_pack = jnp.concatenate(
            [keys_rot.reshape(slot_count, head_cols), values_in.reshape(slot_count, head_cols)],
            axis=1,
        )
        own_flags = prompt_mask[micro_at, 0].astype(jnp.bfloat16)
        empty_pack = (
            jnp.zeros((slot_count, 2 * head_cols), jnp.bfloat16),
            jnp.zeros((slot_count,), jnp.bfloat16),
        )
        far_pack, far_flags = pick_partner(
            partner_row,
            slot_count,
            empty_pack,
            (
                lax.all_gather(own_pack, "dp", axis=0, tiled=True),
                lax.all_gather(own_flags, "dp", axis=0, tiled=True),
            ),
        )
        all_keys = jnp.concatenate(
            [keys_rot, far_pack[:, :head_cols].reshape(slot_count, head_count, HEAD_DIM)], axis=0
        )
        all_values = jnp.concatenate(
            [values_in, far_pack[:, head_cols:].reshape(slot_count, head_count, HEAD_DIM)], axis=0
        )
        far_ok = far_flags > 0

        def block_scores(queries_blk, first_row):
            raw = (
                jnp.einsum(
                    "ihd,jhd->hij", queries_blk, all_keys, preferred_element_type=jnp.float32
                )
                * score_scale
            )
            rows_at = first_row + jnp.arange(block_rows)[:, None]
            own_ok = jnp.arange(slot_count)[None, :] <= rows_at
            allowed = jnp.concatenate(
                [own_ok, jnp.broadcast_to(far_ok[None, :], (block_rows, slot_count))], axis=1
            )
            return jnp.where(allowed[None], raw, masked_score)

        def forward_block(block_at):
            first_row = block_at * block_rows
            scores = block_scores(queries, first_row)
            row_top = jnp.max(scores, axis=-1, keepdims=True)
            exponent = jnp.exp(scores - row_top)
            row_total = jnp.sum(exponent, axis=-1, keepdims=True)
            shares = (exponent / row_total).astype(jnp.bfloat16)
            attended_blk = jnp.einsum(
                "hij,jhd->ihd", shares, all_values, preferred_element_type=jnp.float32
            )
            return (
                attended_blk.reshape(block_rows, head_cols).astype(jnp.bfloat16),
                row_top,
                row_total,
            )

        attended, row_tops, row_totals = lax.map(
            forward_block, jnp.arange(block_count, dtype=jnp.int32)
        )
        attended = attended.reshape(slot_count, head_cols)
        branch = lax.psum(
            jnp.dot(attended, out_weight, preferred_element_type=jnp.float32).astype(jnp.bfloat16),
            "tensor",
        ).astype(jnp.float32)
        middle = tokens + live_mask * branch
        mlp_rows = rms_scale(middle)
        normed_mlp = (middle * mlp_rows * mlp_scale).astype(jnp.bfloat16)
        gate_up = jnp.dot(normed_mlp, gate_up_weight, preferred_element_type=jnp.float32)
        gate_pre = gate_up[:, :unit_count]
        up_pre = gate_up[:, unit_count:]
        gate_sigmoid = jax.nn.sigmoid(gate_pre)
        activated = gate_pre * gate_sigmoid
        hidden = (activated * up_pre).astype(jnp.bfloat16)
        branch_mlp = lax.psum(
            jnp.dot(hidden, down_weight, preferred_element_type=jnp.float32).astype(jnp.bfloat16),
            "tensor",
        ).astype(jnp.float32)
        results.append((middle + live_mask * branch_mlp).astype(jnp.bfloat16))
        upstream = grad_out[micro_at, 0].astype(jnp.float32)
        down_grad = (live_mask * upstream).astype(jnp.bfloat16)
        hidden_grad = contract_cols(down_grad, down_weight)
        down_projection_gradient = down_projection_gradient + contract_rows(hidden, down_grad)
        gate_grad = (
            hidden_grad * up_pre * gate_sigmoid * (1.0 + gate_pre * (1.0 - gate_sigmoid))
        ).astype(jnp.bfloat16)
        up_grad = (hidden_grad * activated).astype(jnp.bfloat16)
        gate_up_grad = jnp.concatenate([gate_grad, up_grad], axis=1)
        grad_gate_up = grad_gate_up + contract_rows(normed_mlp, gate_up_grad)
        mlp_in_grad = lax.psum(
            contract_cols(gate_up_grad, gate_up_weight).astype(jnp.bfloat16), "tensor"
        ).astype(jnp.float32)
        middle_grad = upstream + rms_back(middle, mlp_rows, mlp_scale, mlp_in_grad)
        attn_grad = (live_mask * middle_grad).astype(jnp.bfloat16)
        output_projection_gradient = output_projection_gradient + contract_rows(attended, attn_grad)
        attended_grad = (
            contract_cols(attn_grad, out_weight)
            .astype(jnp.bfloat16)
            .reshape(slot_count, head_count, HEAD_DIM)
        )

        def backward_block(carried, block_at):
            first_row = block_at * block_rows
            row_top = row_tops[block_at]
            row_total = row_totals[block_at]
            scores = block_scores(queries, first_row)
            shares = jnp.exp(scores - row_top) / row_total
            shares_low = shares.astype(jnp.bfloat16)
            share_grad = jnp.einsum(
                "ihd,jhd->hij", attended_grad, all_values, preferred_element_type=jnp.float32
            )
            inner = jnp.sum(shares * share_grad, axis=-1, keepdims=True)
            score_grad = (shares * (share_grad - inner)).astype(jnp.bfloat16)
            query_grad = (
                jnp.einsum("hij,jhd->ihd", score_grad, all_keys, preferred_element_type=jnp.float32)
                * score_scale
            )
            key_part = (
                jnp.einsum("hij,ihd->jhd", score_grad, queries, preferred_element_type=jnp.float32)
                * score_scale
            )
            value_part = jnp.einsum(
                "hij,ihd->jhd", shares_low, attended_grad, preferred_element_type=jnp.float32
            )
            query_grad, key_part, value_part = (query_grad, key_part, value_part)
            return ((carried[0] + key_part, carried[1] + value_part), query_grad)

        key_zero = jnp.zeros((slot_count + slot_count, head_count, HEAD_DIM), jnp.float32)
        (key_grad, value_grad), query_grads = lax.scan(
            backward_block, (key_zero, key_zero), jnp.arange(block_count, dtype=jnp.int32)
        )
        far_grad = jnp.concatenate(
            [
                key_grad[slot_count:].reshape(slot_count, head_cols),
                value_grad[slot_count:].reshape(slot_count, head_cols),
            ],
            axis=1,
        )
        far_low = far_grad.astype(jnp.bfloat16)
        returned = lax.psum_scatter(
            place_far(
                partner_row, far_low.astype(jnp.float32), slot_count * lax.axis_size("dp")
            ).astype(jnp.bfloat16),
            "dp",
            scatter_dimension=0,
            tiled=True,
        ).astype(jnp.float32)
        key_total = key_grad[:slot_count] + returned[:, :head_cols].reshape(
            slot_count, head_count, HEAD_DIM
        )
        value_total = value_grad[:slot_count] + returned[:, head_cols:].reshape(
            slot_count, head_count, HEAD_DIM
        )
        query_total = query_grads.reshape(slot_count, head_count, HEAD_DIM)
        query_back = (query_total * cosine - turn_half(query_total * sine_tab)).astype(jnp.bfloat16)
        key_back = (key_total * cosine - turn_half(key_total * sine_tab)).astype(jnp.bfloat16)
        value_back = value_total.astype(jnp.bfloat16)
        qkv_grad = jnp.concatenate(
            [
                query_back.reshape(slot_count, head_cols),
                key_back.reshape(slot_count, head_cols),
                value_back.reshape(slot_count, head_cols),
            ],
            axis=1,
        )
        grad_qkv = grad_qkv + contract_rows(normed, qkv_grad)
        attn_in_grad = lax.psum(
            contract_cols(qkv_grad, qkv_weight).astype(jnp.bfloat16), "tensor"
        ).astype(jnp.float32)
        input_grads.append(
            (middle_grad + rms_back(tokens, attn_rows, attn_scale, attn_in_grad)).astype(
                jnp.bfloat16
            )
        )
    query_key_value_total = grad_qkv.reshape(model_width, 3, head_cols)
    gate_weight_total = grad_gate_up.reshape(model_width, 2, unit_count)
    qkv_left, qkv_right, qkv_mag = column_gradient_list(
        query_key_value_total,
        query_key_value_merged,
        query_key_value_norm,
        attention_input_magnitude,
        attention_input_first,
        attention_input_second,
        adapter_scale,
    )
    gate_left, gate_right, gate_mag = column_gradient_list(
        gate_weight_total,
        gate_merged_weight,
        gate_column_norm,
        feedforward_input_magnitude,
        feedforward_input_first,
        feedforward_input_second,
        adapter_scale,
    )
    out_inner, output_left_factor, output_right_factor = row_pieces_list(
        output_projection_gradient,
        output_merged_weight,
        output_column_norm,
        attention_output_magnitude,
        attention_output_first,
        attention_output_second,
        adapter_scale,
    )
    down_inner, down_left_factor, down_right_factor = row_pieces_list(
        down_projection_gradient,
        down_merged_weight,
        down_column_norm,
        feedforward_output_magnitude,
        feedforward_output_first,
        feedforward_output_second,
        adapter_scale,
    )
    qkv_left, gate_left, output_right_factor, down_right_factor, out_inner, down_inner = lax.psum(
        (qkv_left, gate_left, output_right_factor, down_right_factor, out_inner, down_inner),
        ("dp", "tensor"),
    )
    qkv_right, qkv_mag, gate_right, gate_mag, output_left_factor, down_left_factor = (
        lax.psum(qkv_right.astype(jnp.bfloat16), "dp").astype(jnp.float32),
        lax.psum(qkv_mag.astype(jnp.bfloat16), "dp").astype(jnp.float32),
        lax.psum(gate_right.astype(jnp.bfloat16), "dp").astype(jnp.float32),
        lax.psum(gate_mag.astype(jnp.bfloat16), "dp").astype(jnp.float32),
        lax.psum(output_left_factor.astype(jnp.bfloat16), "dp").astype(jnp.float32),
        lax.psum(down_left_factor.astype(jnp.bfloat16), "dp").astype(jnp.float32),
    )
    output_norm_factor = (
        attention_output_magnitude
        * out_inner
        / (output_column_norm * output_column_norm * output_column_norm)
    )
    down_norm_factor = (
        feedforward_output_magnitude
        * down_inner
        / (down_column_norm * down_column_norm * down_column_norm)
    )
    output_left_factor = output_left_factor - adapter_scale * jnp.dot(
        output_merged_weight * output_norm_factor,
        attention_output_second.T,
        precision=highest_precision,
    )
    down_left_factor = down_left_factor - adapter_scale * jnp.dot(
        down_merged_weight * down_norm_factor,
        feedforward_output_second.T,
        precision=highest_precision,
    )
    output_right_factor = (
        output_right_factor - adapter_scale * output_cross_term * output_norm_factor
    )
    down_right_factor = down_right_factor - adapter_scale * down_cross_term * down_norm_factor
    out_mag = out_inner / output_column_norm
    down_mag = down_inner / down_column_norm
    layer_out = jnp.stack(results)[:, None]
    layer_grad = jnp.stack(input_grads)[:, None]
    return (
        layer_out,
        layer_grad,
        qkv_left,
        qkv_right,
        qkv_mag,
        output_left_factor,
        output_right_factor,
        out_mag,
        gate_left,
        gate_right,
        gate_mag,
        down_left_factor,
        down_right_factor,
        down_mag,
    )


FAR_SLOTS = 128
LANES = 128
MIB = 1024 * 1024
f32 = jnp.float32
bf16 = jnp.bfloat16


def fits_fast(mesh):
    return mesh.shape["dp"] == 8 and mesh.shape["tensor"] == 4


def split_high_low(value):
    high = value.astype(bf16)
    return high, (value - high.astype(f32)).astype(bf16)


def adapter_product(first_t, second):
    a_high, a_low = split_high_low(first_t)
    b_high, b_low = split_high_low(second)
    left = jnp.concatenate([a_high, a_low, a_high], axis=0)
    right = jnp.concatenate([b_high, b_high, b_low], axis=0)
    return contract_rows(left, right)


def params(mib):
    return pltpu.CompilerParams(vmem_limit_bytes=mib * MIB)


def single(shape):
    zeros = (0,) * len(shape)
    return pl.BlockSpec(shape, lambda *_: zeros, pipeline_mode=pl.Buffered(1))


def micro_rows(micro_at, slots, width):
    return pl.BlockSpec((slots, width), lambda *_: (micro_at, 0), pipeline_mode=pl.Buffered(1))


def micro_tokens(micro_at, slots, width):
    return pl.BlockSpec(
        (None, None, slots, width),
        lambda *_: (micro_at, 0, 0, 0),
        pipeline_mode=pl.Buffered(1),
    )


SCALARS = pl.BlockSpec(memory_space=pltpu.SMEM)
SHORT = pl.CostEstimate(flops=1, bytes_accessed=1, transcendentals=0)


def whole_block(shape):
    zeros = (0,) * len(shape)
    return pl.BlockSpec(shape, lambda *_: zeros)


UNIT_BLOCK = 256
LARGE_MIB = 56


def padded(units):
    return -(-units // UNIT_BLOCK) * UNIT_BLOCK


def adapter_rows(second):
    high, low = split_high_low(second * (ADAPTER_NUMER / ADAPTER_RANK))
    return jnp.concatenate([high, high, low], axis=0)


def adapter_columns(first_t):
    high, low = split_high_low(first_t)
    return jnp.concatenate([high, low, high], axis=0)


def partial_squares(value):
    return jnp.sum((value * value).reshape(value.shape[0] // 8, 8, value.shape[1]), axis=0)


def merge_chunk(base, columns, rows):
    return base.astype(f32) + contract_rows(columns, rows)


def merge_in(frozen, first_t, second, magnitude):
    depth, groups, cols = frozen.shape
    rank = second.shape[1]
    blocks = padded(cols) // UNIT_BLOCK
    total = blocks * groups * UNIT_BLOCK
    row_block = 256
    steps = depth // row_block

    def kernel(w_ref, a_ref, b_ref, m_ref, v_ref, ratio_ref, inverse_ref, wide_ref, r_ref, sq_ref):
        at = pl.program_id(0)

        def pieces():
            for g in range(groups):
                for j in range(blocks):
                    count = min(UNIT_BLOCK, cols - j * UNIT_BLOCK)
                    start = (j * groups + g) * UNIT_BLOCK
                    yield g, j, slice(j * UNIT_BLOCK, j * UNIT_BLOCK + count), start, count

        @pl.when(at == 0)
        def _():
            sq_ref[...] = jnp.zeros_like(sq_ref)
            wide_ref[...] = jnp.zeros_like(wide_ref)
            for g in range(groups):
                r_ref[g] = adapter_rows(b_ref[g])
            for g, j, here, start, count in pieces():
                ranks = slice(g * rank, (g + 1) * rank)
                wide_ref[ranks, start : start + count] = b_ref[g, :, here]

        left = [adapter_columns(a_ref[g]) for g in range(groups)]
        for g, j, here, start, count in pieces():
            v = merge_chunk(w_ref[:, g, here], left[g], r_ref[g, :, here])
            at_g = g * UNIT_BLOCK
            v_ref[j, :, at_g : at_g + count] = v.astype(bf16)
            if count < UNIT_BLOCK:
                v_ref[j, :, at_g + count : at_g + UNIT_BLOCK] = jnp.zeros(
                    (row_block, UNIT_BLOCK - count), bf16
                )
            sq_ref[:, start : start + count] += partial_squares(v)

        @pl.when(at == steps - 1)
        def _():
            ratio_ref[...] = jnp.zeros_like(ratio_ref)
            inverse_ref[...] = jnp.zeros_like(inverse_ref)
            for g, j, here, start, count in pieces():
                there = slice(start, start + count)
                inverse = lax.rsqrt(jnp.sum(sq_ref[:, there], axis=0, keepdims=True))
                inverse_ref[:, there] = inverse
                ratio_ref[:, there] = m_ref[g : g + 1, here] * inverse

    return pl.pallas_call(
        kernel,
        grid=(steps,),
        in_specs=[
            pl.BlockSpec((row_block, groups, cols), lambda i: (i, 0, 0)),
            pl.BlockSpec((groups, rank, row_block), lambda i: (0, 0, i)),
            whole_block((groups, rank, cols)),
            whole_block((groups, cols)),
        ],
        out_specs=[
            pl.BlockSpec((blocks, row_block, groups * UNIT_BLOCK), lambda i: (0, i, 0)),
            whole_block((1, total)),
            whole_block((1, total)),
            whole_block((groups * rank, total)),
        ],
        out_shape=[
            jax.ShapeDtypeStruct((blocks, depth, groups * UNIT_BLOCK), bf16),
            jax.ShapeDtypeStruct((1, total), f32),
            jax.ShapeDtypeStruct((1, total), f32),
            jax.ShapeDtypeStruct((groups * rank, total), f32),
        ],
        scratch_shapes=[
            pltpu.VMEM((groups, 3 * rank, cols), bf16),
            pltpu.VMEM((8, total), f32),
        ],
        compiler_params=params(12),
        cost_estimate=SHORT,
        name="merge_in",
    )(frozen, first_t, second, magnitude)


def merge_out(frozen, first_t, second):
    depth, cols = frozen.shape
    rank = second.shape[0]
    row_block = UNIT_BLOCK
    blocks = padded(depth) // row_block
    chunk = 512

    def kernel(w_ref, a_ref, b_ref, v_ref, total_ref, r_ref, sq_ref):
        at = pl.program_id(0)

        @pl.when(at == 0)
        def _():
            sq_ref[...] = jnp.zeros_like(sq_ref)
            r_ref[...] = adapter_rows(b_ref[...])

        left = adapter_columns(a_ref[...])
        within = at * row_block + lax.broadcasted_iota(jnp.int32, (row_block, 1), 0) < depth
        for j in range(cols // chunk):
            here = slice(j * chunk, (j + 1) * chunk)
            v = jnp.where(within, merge_chunk(w_ref[:, here], left, r_ref[:, here]), 0.0)
            v_ref[:, here] = v.astype(bf16)
            sq_ref[:, here] += partial_squares(v)

        @pl.when(at == blocks - 1)
        def _():
            total_ref[...] = jnp.sum(sq_ref[...], axis=0, keepdims=True)

    return pl.pallas_call(
        kernel,
        grid=(blocks,),
        in_specs=[
            pl.BlockSpec((row_block, cols), lambda i: (i, 0)),
            pl.BlockSpec((rank, row_block), lambda i: (0, i)),
            whole_block((rank, cols)),
        ],
        out_specs=[pl.BlockSpec((row_block, cols), lambda i: (i, 0)), whole_block((1, cols))],
        out_shape=[
            jax.ShapeDtypeStruct((blocks * row_block, cols), bf16),
            jax.ShapeDtypeStruct((1, cols), f32),
        ],
        scratch_shapes=[pltpu.VMEM((3 * rank, cols), bf16), pltpu.VMEM((8, cols), f32)],
        compiler_params=params(10),
        cost_estimate=SHORT,
        name="merge_out",
    )(frozen, first_t, second)


def rotate(values, cosine, sine_signed):
    return values * cosine + pltpu.roll(values, HEAD_DIM // 2, 1) * sine_signed


def rotate_back(values, cosine, sine_signed):
    return values * cosine - pltpu.roll(values, HEAD_DIM // 2, 1) * sine_signed


def merge_project(
    tokens, gain, frozen, first_t, second, magnitude, cosine, sine_signed, flags, slots
):
    count, width = tokens.shape
    cols = frozen.shape[2]
    rank = second.shape[1]
    heads = cols // HEAD_DIM
    chunk_rows, chunk_cols = 256, 256
    micros = count // slots

    def kernel(*refs):
        x_ref, g_ref, w_ref, a_ref, b_ref, m_ref, c_ref, n_ref, f_ref = refs[:9]
        o_ref, v_ref, sq_ref, y_ref, *pack_refs = refs[9:]
        part = pl.program_id(0)

        @pl.when(part == 0)
        def _():
            for m in range(micros):
                pack_refs[m][FAR_SLOTS:, :] = jnp.zeros((16, 2 * cols), bf16)
                pack_refs[m][FAR_SLOTS : FAR_SLOTS + 1, :FAR_SLOTS] = f_ref[m : m + 1].astype(bf16)
            for r in range(0, count, chunk_rows):
                x = x_ref[r : r + chunk_rows].astype(f32)
                o_ref[r : r + chunk_rows] = (x * rms_scale(x) * g_ref[...]).astype(bf16)

        right = adapter_rows(b_ref[...])
        for c in range(0, cols, chunk_cols):
            here = slice(c, c + chunk_cols)
            square = 0.0
            for r in range(0, width, chunk_rows):
                left = adapter_columns(a_ref[:, r : r + chunk_rows])
                v = merge_chunk(w_ref[r : r + chunk_rows, here], left, right[:, here])
                v_ref[r : r + chunk_rows, here] = v.astype(bf16)
                square = square + partial_squares(v)
            square = jnp.sum(square, axis=0, keepdims=True)
            sq_ref[:, here] = square
            ratio = m_ref[:, here] * lax.rsqrt(square)
            total = jnp.dot(o_ref[...], v_ref[:, here], preferred_element_type=f32) * ratio
            for h in range(0, chunk_cols, HEAD_DIM):
                turned = rotate(total[:, h : h + HEAD_DIM], c_ref[...], n_ref[...])
                y_ref[:, c + h : c + h + HEAD_DIM] = jnp.where(
                    part < 2, turned, total[:, h : h + HEAD_DIM]
                ).astype(bf16)

        for kept in (1, 2):

            @pl.when(part == kept)
            def _(first=(kept - 1) * cols):
                for m in range(micros):
                    rows = y_ref[m * slots : m * slots + FAR_SLOTS, :]
                    pack_refs[m][:FAR_SLOTS, first : first + cols] = rows

    return pl.pallas_call(
        kernel,
        grid=(3,),
        in_specs=[
            whole_block((count, width)),
            whole_block((1, width)),
            pl.BlockSpec((None, width, cols), lambda i: (i, 0, 0)),
            pl.BlockSpec((None, rank, width), lambda i: (i, 0, 0)),
            pl.BlockSpec((None, rank, cols), lambda i: (i, 0, 0)),
            pl.BlockSpec((1, cols), lambda i: (0, i)),
            whole_block((count, HEAD_DIM)),
            whole_block((count, HEAD_DIM)),
            whole_block(flags.shape),
        ],
        out_specs=[
            whole_block((count, width)),
            pl.BlockSpec((None, width, cols), lambda i: (i, 0, 0)),
            pl.BlockSpec((1, cols), lambda i: (0, i)),
            pl.BlockSpec((count, cols), lambda i: (0, i)),
        ]
        + [whole_block((FAR_SLOTS + 16, 2 * cols))] * micros,
        out_shape=[
            jax.ShapeDtypeStruct((count, width), bf16),
            jax.ShapeDtypeStruct((3, width, cols), bf16),
            jax.ShapeDtypeStruct((1, 3 * cols), f32),
            jax.ShapeDtypeStruct((count, 3 * cols), bf16),
        ]
        + [jax.ShapeDtypeStruct((FAR_SLOTS + 16, 2 * cols), bf16)] * micros,
        compiler_params=params(22),
        cost_estimate=SHORT,
        name="merge_project",
    )(tokens, gain, frozen, first_t, second, magnitude, cosine, sine_signed, flags)


def head_shares(q, k, far_k, far_ok):
    scale = 1.0 / math.sqrt(HEAD_DIM)
    own = contract_cols(q, k) * scale
    far = contract_cols(q, far_k) * scale
    rows_at = lax.broadcasted_iota(jnp.int32, own.shape, 0)
    slots_at = lax.broadcasted_iota(jnp.int32, own.shape, 1)
    own = jnp.where(slots_at <= rows_at, own, masked_score)
    far = jnp.where(far_ok > 0, far, masked_score)
    scores = jnp.concatenate([own, far], axis=1)
    top = jnp.max(scores, axis=-1, keepdims=True)
    exponent = jnp.exp(scores - top)
    return exponent / jnp.sum(exponent, axis=-1, keepdims=True)


def store_part(value, refs, inner):
    if len(refs) == 1:
        refs[0][...] = value
        return
    half = value.shape[0] // 2

    @pl.when(inner == 1)
    def _():
        refs[0][...] = value[half:]
        refs[1][...] = value[:half]

    @pl.when(inner != 1)
    def _():
        refs[0][...] = value[:half]
        refs[1][...] = value[half:]


def load_total(refs, inner):
    if len(refs) == 1:
        return refs[0][...].astype(f32)
    mine, other = refs[0][...], refs[1][...]
    flip = inner == 1
    first = jnp.where(flip, other, mine)
    last = jnp.where(flip, mine, other)
    return jnp.concatenate([first, last], axis=0).astype(f32)


def part_shapes(slots, width, pieces):
    return [jax.ShapeDtypeStruct((slots // pieces, width), bf16)] * pieces


def attend(inner, projected, far_pack, out_merged, pieces, micro_at, slots):
    cols = projected.shape[1] // 3
    heads = cols // HEAD_DIM
    width = out_merged.shape[1]

    def kernel(i_ref, y_ref, f_ref, w_ref, o_ref, *z_refs):
        far_ok = f_ref[FAR_SLOTS : FAR_SLOTS + 1, :FAR_SLOTS].astype(f32)
        for h in range(heads):
            at = slice(h * HEAD_DIM, (h + 1) * HEAD_DIM)
            far_k = f_ref[:FAR_SLOTS, h * HEAD_DIM : (h + 1) * HEAD_DIM]
            far_v = f_ref[:FAR_SLOTS, cols + h * HEAD_DIM : cols + (h + 1) * HEAD_DIM]
            k = y_ref[:, cols + h * HEAD_DIM : cols + (h + 1) * HEAD_DIM]
            v = y_ref[:, 2 * cols + h * HEAD_DIM : 2 * cols + (h + 1) * HEAD_DIM]
            shares = head_shares(y_ref[:, at], k, far_k, far_ok).astype(bf16)
            values = jnp.concatenate([v, far_v], axis=0)
            o_ref[:, at] = jnp.dot(shares, values, preferred_element_type=f32).astype(bf16)
        part = jnp.dot(o_ref[...], w_ref[...], preferred_element_type=f32).astype(bf16)
        store_part(part, z_refs, i_ref[0])

    return pl.pallas_call(
        kernel,
        grid=(1,),
        in_specs=[
            SCALARS,
            micro_rows(micro_at, slots, 3 * cols),
            single(far_pack.shape),
            single(out_merged.shape),
        ],
        out_specs=[single((slots, cols))] + [single((slots // pieces, width))] * pieces,
        out_shape=[jax.ShapeDtypeStruct((slots, cols), bf16)]
        + part_shapes(slots, width, pieces),
        compiler_params=params(14),
        cost_estimate=SHORT,
        name="attend",
    )(inner, projected, far_pack, out_merged)


def feed_forward(
    scalars,
    branch_sum,
    tokens,
    upstream,
    out_ratio,
    down_ratio,
    gain,
    merged,
    ratio,
    down_merged,
    micro_at,
):
    slots, width = tokens.shape[2:]
    units = down_merged.shape[0]
    block = UNIT_BLOCK
    blocks = units // block
    pieces = len(branch_sum)

    def kernel(*refs):
        n_ref, *refs = refs
        s_refs, refs = refs[:pieces], refs[pieces:]
        x_ref, u_ref, or_ref, dr_ref, g_ref, w_ref, r_ref, wd_ref = refs[:8]
        h_ref, b_ref, d2_ref, hid_ref, dgu_ref, cgu_ref, cd_ref, y_ref = refs[8:16]
        db_refs, (dba_ref, ya_ref) = refs[16:-2], refs[-2:]
        at = pl.program_id(0)

        def live_rows():
            return lax.broadcasted_iota(jnp.int32, (slots, 1), 0) < n_ref[0]

        @pl.when(at == 0)
        def _():
            live = live_rows()
            branch = load_total(s_refs, n_ref[1]) * or_ref[...]
            h = x_ref[...].astype(f32) + jnp.where(live, branch, 0.0)
            h_ref[...] = h
            b_ref[...] = (h * rms_scale(h) * g_ref[...]).astype(bf16)
            d2_ref[...] = jnp.where(live, u_ref[...].astype(f32) * dr_ref[...], 0.0).astype(bf16)
            dba_ref[...] = jnp.zeros_like(dba_ref)
            ya_ref[...] = jnp.zeros_like(ya_ref)

        raw = jnp.dot(b_ref[...], w_ref[...], preferred_element_type=f32)
        dhidden = contract_cols(d2_ref[...], wd_ref[...])
        scaled = raw * r_ref[...]
        gate, up = scaled[:, :block], scaled[:, block:]
        sigmoid = jax.nn.sigmoid(gate)
        activated = gate * sigmoid
        hidden = (activated * up).astype(bf16)
        hid_ref[...] = hidden
        dgate = dhidden * up * sigmoid * (1.0 + gate * (1.0 - sigmoid))
        back = jnp.concatenate([dgate, dhidden * activated], axis=1)
        cgu_ref[...] = jnp.sum(back * raw, axis=0, keepdims=True)
        back = (back * r_ref[...]).astype(bf16)
        dgu_ref[...] = back
        dba_ref[...] += contract_cols(back, w_ref[...])
        ya_ref[...] += jnp.dot(hidden, wd_ref[...], preferred_element_type=f32)

        @pl.when(at == blocks - 1)
        def _():
            store_part(dba_ref[...].astype(bf16), db_refs, n_ref[1])
            y_ref[...] = ya_ref[...].astype(bf16)
            d2 = jnp.where(live_rows(), u_ref[...].astype(f32), 0.0)
            cd_ref[...] = jnp.sum(d2 * ya_ref[...], axis=0, keepdims=True)

    row = single((1, width))
    full = single((slots, width))
    part = single((slots // pieces, width))
    micro = micro_tokens(micro_at, slots, width)
    unit_cols = pl.BlockSpec((slots, block), lambda i: (0, i))
    pair_cols = pl.BlockSpec((slots, 2 * block), lambda i: (0, i))
    pair_row = pl.BlockSpec((1, 2 * block), lambda i: (0, i))
    return pl.pallas_call(
        kernel,
        grid=(blocks,),
        in_specs=[pl.BlockSpec(memory_space=pltpu.SMEM)]
        + [part] * pieces
        + [
            micro,
            micro,
            row,
            row,
            row,
            pl.BlockSpec((None, width, 2 * block), lambda i: (i, 0, 0)),
            pair_row,
            pl.BlockSpec((block, width), lambda i: (i, 0)),
        ],
        out_specs=[full] * 3 + [unit_cols, pair_cols, pair_row, row, full] + [part] * pieces,
        out_shape=[
            jax.ShapeDtypeStruct((slots, width), f32),
            jax.ShapeDtypeStruct((slots, width), bf16),
            jax.ShapeDtypeStruct((slots, width), bf16),
            jax.ShapeDtypeStruct((slots, units), bf16),
            jax.ShapeDtypeStruct((slots, 2 * units), bf16),
            jax.ShapeDtypeStruct((1, 2 * units), f32),
            jax.ShapeDtypeStruct((1, width), f32),
            jax.ShapeDtypeStruct((slots, width), bf16),
        ]
        + part_shapes(slots, width, pieces),
        scratch_shapes=[
            pltpu.VMEM((slots, width), f32),
            pltpu.VMEM((slots, width), f32),
        ],
        compiler_params=params(LARGE_MIB),
        cost_estimate=SHORT,
        name="feed_forward",
    )(
        scalars,
        *branch_sum,
        tokens,
        upstream,
        out_ratio,
        down_ratio,
        gain,
        merged,
        ratio,
        down_merged,
    )


def attend_back(
    scalars,
    db_sum,
    middle,
    upstream,
    branch_sum,
    gain,
    out_ratio,
    out_merged,
    projected,
    far_pack,
    cosine,
    sine_signed,
    micro_at,
):
    slots, width = middle.shape
    cols = projected.shape[1] // 3
    heads = cols // HEAD_DIM
    scale = 1.0 / math.sqrt(HEAD_DIM)
    pieces = len(db_sum)

    def kernel(*refs):
        n_ref, *refs = refs
        e_refs, s_refs, refs = refs[:pieces], refs[pieces : 2 * pieces], refs[2 * pieces :]
        h_ref, u_ref, g_ref, or_ref, w_ref, y_ref, f_ref, c_ref, sn_ref = refs[:9]
        dh_ref, d1_ref, co_ref, dy_ref, far_ref, do_ref = refs[9:]
        live = lax.broadcasted_iota(jnp.int32, (slots, 1), 0) < n_ref[0]
        h = h_ref[...]
        back = rms_back(h, rms_scale(h), g_ref[...], load_total(e_refs, n_ref[1]))
        dh = u_ref[...].astype(f32) + back
        dh_ref[...] = dh
        d1 = jnp.where(live, dh, 0.0)
        co_ref[...] = jnp.sum(d1 * load_total(s_refs, n_ref[1]), axis=0, keepdims=True)
        d1_ref[...] = (d1 * or_ref[...]).astype(bf16)
        do_ref[...] = contract_cols(d1_ref[...], w_ref[...]).astype(bf16)
        far_ok = f_ref[FAR_SLOTS : FAR_SLOTS + 1, :FAR_SLOTS].astype(f32)
        for i in range(heads):
            at = slice(i * HEAD_DIM, (i + 1) * HEAD_DIM)
            k_at = slice(cols + i * HEAD_DIM, cols + (i + 1) * HEAD_DIM)
            v_at = slice(2 * cols + i * HEAD_DIM, 2 * cols + (i + 1) * HEAD_DIM)
            q = y_ref[:, at]
            far_k = f_ref[:FAR_SLOTS, at]
            shares = head_shares(q, y_ref[:, k_at], far_k, far_ok)
            keys = jnp.concatenate([y_ref[:, k_at], far_k], axis=0)
            values = jnp.concatenate([y_ref[:, v_at], f_ref[:FAR_SLOTS, k_at]], axis=0)
            do = do_ref[:, at]
            share_grad = contract_cols(do, values)
            inner = jnp.sum(shares * share_grad, axis=-1, keepdims=True)
            score_grad = (shares * (share_grad - inner)).astype(bf16)
            dq = jnp.dot(score_grad, keys, preferred_element_type=f32) * scale
            dk = contract_rows(score_grad, q) * scale
            dv = contract_rows(shares.astype(bf16), do)
            dy_ref[:, at] = rotate_back(dq, c_ref[...], sn_ref[...])
            dy_ref[:, k_at] = dk[:slots]
            dy_ref[:, v_at] = dv[:slots]
            far_ref[:, at] = dk[slots:].astype(bf16)
            far_ref[:, k_at] = dv[slots:].astype(bf16)

    operands = (
        scalars,
        *db_sum,
        *branch_sum,
        middle,
        upstream,
        gain,
        out_ratio,
        out_merged,
        projected,
        far_pack,
        cosine,
        sine_signed,
    )
    shapes = [
        jax.ShapeDtypeStruct((slots, width), f32),
        jax.ShapeDtypeStruct((slots, width), bf16),
        jax.ShapeDtypeStruct((1, width), f32),
        jax.ShapeDtypeStruct((slots, 3 * cols), f32),
        jax.ShapeDtypeStruct((FAR_SLOTS, 2 * cols), bf16),
    ]
    return pl.pallas_call(
        kernel,
        grid=(1,),
        in_specs=[SCALARS]
        + [single((slots // pieces, width))] * (2 * pieces)
        + [
            single((slots, width)),
            micro_tokens(micro_at, slots, width),
            single((1, width)),
            single((1, width)),
            single(out_merged.shape),
            micro_rows(micro_at, slots, 3 * cols),
            single(far_pack.shape),
            micro_rows(micro_at, slots, HEAD_DIM),
            micro_rows(micro_at, slots, HEAD_DIM),
        ],
        out_specs=[single(shape.shape) for shape in shapes],
        out_shape=shapes,
        scratch_shapes=[pltpu.VMEM((slots, cols), bf16)],
        compiler_params=params(LARGE_MIB),
        cost_estimate=SHORT,
        name="attend_back",
    )(*operands)


def project_back(
    inner, dy, returned, projected, cosine, sine_signed, ratio, merged, pieces, micro_at
):
    slots, total = dy.shape
    cols = total // 3
    heads = cols // HEAD_DIM
    width = merged.shape[1]
    blocks = 4
    step = width // blocks

    def kernel(i_ref, d_ref, r_ref, y_ref, c_ref, sn_ref, s_ref, w_ref, o_ref, cs_ref, *da_refs):
        @pl.when(pl.program_id(0) == 0)
        def _():
            for i in range(3 * heads):
                at = slice(i * HEAD_DIM, (i + 1) * HEAD_DIM)
                d = d_ref[:, at]
                raw = y_ref[:, at].astype(f32)
                if i >= heads:
                    back = slice((i - heads) * HEAD_DIM, (i - heads + 1) * HEAD_DIM)
                    low = d[:FAR_SLOTS] + r_ref[:FAR_SLOTS, back].astype(f32)
                    d = jnp.concatenate([low, d[FAR_SLOTS:]], axis=0)
                if heads <= i < 2 * heads:
                    d = rotate_back(d, c_ref[...], sn_ref[...])
                if i < 2 * heads:
                    raw = rotate_back(raw, c_ref[...], sn_ref[...])
                cs_ref[:, at] = jnp.sum(d * raw, axis=0, keepdims=True)
                o_ref[:, at] = (d * s_ref[:, at]).astype(bf16)

        da = 0.0
        for g in range(3):
            da = da + contract_cols(o_ref[:, g * cols : (g + 1) * cols], w_ref[g])
        store_part(da.astype(bf16), da_refs, i_ref[0])

    return pl.pallas_call(
        kernel,
        grid=(blocks,),
        in_specs=[
            SCALARS,
            single((slots, total)),
            single(returned.shape),
            micro_rows(micro_at, slots, total),
            micro_rows(micro_at, slots, HEAD_DIM),
            micro_rows(micro_at, slots, HEAD_DIM),
            single((1, total)),
            pl.BlockSpec((3, step, cols), lambda i: (0, i, 0)),
        ],
        out_specs=[
            whole_block((slots, total)),
            whole_block((1, total)),
        ]
        + [pl.BlockSpec((slots // pieces, step), lambda i: (0, i))] * pieces,
        out_shape=[
            jax.ShapeDtypeStruct((slots, total), bf16),
            jax.ShapeDtypeStruct((1, total), f32),
        ]
        + part_shapes(slots, width, pieces),
        compiler_params=params(LARGE_MIB),
        cost_estimate=SHORT,
        name="project_back",
    )(inner, dy, returned, projected, cosine, sine_signed, ratio, merged)


LINE_PAIRS = [(0, 1), (1, 0), (2, 3), (3, 2)]
LINE_ACROSS = [(0, 3), (3, 0), (1, 2), (2, 1)]


def tensor_sum(parts, beside=None, first=()):
    if len(parts) == 1:
        return [lax.psum(parts[0], "tensor")], None
    keep, send = parts
    received = lax.ppermute(send, "tensor", LINE_PAIRS)
    if first:
        received = after(received, *first)
    pair = keep + received
    across = lax.ppermute(pair, "tensor", LINE_ACROSS)
    done = None
    if beside is not None:
        done = beside(pair)
        across = after(across, *done)
    total = pair + across
    return [total, lax.ppermute(total, "tensor", LINE_PAIRS)], done


def line_total(value):
    value = value + lax.ppermute(value, "tensor", LINE_PAIRS)
    return value + lax.ppermute(value, "tensor", LINE_ACROSS)


def dp_swap(value, hop):
    return lax.ppermute(value, "dp", [(i, i ^ hop) for i in range(8)])


def dp_share(value, line_rows):
    me = lax.axis_index("dp")
    half = value.shape[1] // 2
    quarter = half // 4
    upper = (me & 1) != 0
    low, high = value[:, :half], value[:, half:]
    value = jnp.where(upper, high, low) + dp_swap(jnp.where(upper, low, high), 1)
    chip = me // 2

    def columns(index):
        return lax.dynamic_slice_in_dim(value, index * quarter, quarter, 1)

    kept = columns(chip).astype(f32)
    for hop in (1, 2, 3):
        kept = kept + dp_swap(columns(chip ^ hop), 2 * hop)
    line = kept[:line_rows].astype(bf16)
    total = line.astype(f32)
    for shift in (1, 2, 3):
        total = total + lax.ppermute(line, "tensor", [(i, (i + shift) % 4) for i in range(4)])
    return jnp.concatenate([total, kept[line_rows:]], axis=0).astype(bf16)


def dp_gather(mine):
    me = lax.axis_index("dp")
    upper = (me & 1) != 0
    chip = me // 2
    quarters = [mine] + [dp_swap(mine, 2 * hop) for hop in (1, 2, 3)]
    value = jnp.concatenate([lax.select_n(chip ^ q, *quarters) for q in range(4)], axis=1)
    other = dp_swap(value, 1)
    value = jnp.concatenate(
        [jnp.where(upper, other, value), jnp.where(upper, value, other)], axis=1
    )
    return value.astype(f32)


def pair_exchange(pack, distance, sibling_distance):
    held = [pack] + [dp_swap(pack, hop) for hop in (2, 4, 6)]

    def pick(index):
        return lax.select_n(index // 2, *held)

    across = dp_swap(pick(sibling_distance & 6), 1)
    return jnp.where(distance % 2 == 1, across, pick(distance & 6)), held


def adapter_in(seen_inputs, sent_grads, merged, tall, wide, share, rank):
    micros = len(sent_grads)
    slots, depth = sent_grads[0].shape[0], seen_inputs[0].shape[1]
    blocks, _, cols = merged.shape
    shared = seen_inputs[0].shape[0] != slots
    if shared:
        seen_inputs = seen_inputs * micros
    ranks = tall.shape[0]
    groups = ranks // rank
    sides = 1 if blocks == groups else groups
    part = cols // sides
    scale = ADAPTER_NUMER / ADAPTER_RANK

    def kernel(*refs):
        x_refs, d_refs, refs = refs[:micros], refs[micros : 2 * micros], refs[2 * micros :]
        v_ref, t_ref, w_ref, s_ref, out_ref, *right_refs = refs[: 5 + sides]
        seen_ref, sent_ref, left_ref, all_ref = refs[5 + sides :]
        at = pl.program_id(0)

        @pl.when(at == 0)
        def _():
            left_ref[...] = jnp.zeros_like(left_ref)
            sent_ref[...] = jnp.zeros_like(sent_ref)
            for m in range(micros):
                seen_ref[m] = contract_cols(x_refs[m][...], t_ref[...]).astype(bf16)

        share = s_ref[...]
        wide = w_ref[...]
        right = -jnp.dot(t_ref[...], v_ref[...], preferred_element_type=f32) * share
        left = -contract_cols((wide * share).astype(bf16), v_ref[...])
        for m in range(micros):
            right = right + contract_rows(seen_ref[m], d_refs[m][...])
            sent_ref[m] += contract_cols(d_refs[m][...], wide.astype(bf16))
        if sides == 1:
            all_ref[...] = scale * right
            mine = pl.ds(pl.multiple_of(at * rank, rank), rank)
            right_refs[0][...] = all_ref[mine, :].astype(bf16)
        else:
            for g in range(sides):
                mine = right[g * rank : (g + 1) * rank, g * part : (g + 1) * part]
                right_refs[g][...] = (scale * mine).astype(bf16)
        left_ref[...] += left

        @pl.when(at == blocks - 1)
        def _():
            total = left_ref[...]
            for m in range(micros):
                total = total + contract_rows(sent_ref[m].astype(bf16), x_refs[m][...])
            out_ref[...] = (scale * total).astype(bf16)

    return pl.pallas_call(
        kernel,
        grid=(blocks,),
        in_specs=[micro_rows(m if shared else 0, slots, depth) for m in range(micros)]
        + [pl.BlockSpec((slots, cols), lambda i: (0, i))] * micros
        + [
            pl.BlockSpec((None, depth, cols), lambda i: (i, 0, 0)),
            single((ranks, depth)),
            pl.BlockSpec((ranks, cols), lambda i: (0, i)),
            pl.BlockSpec((1, cols), lambda i: (0, i)),
        ],
        out_specs=[whole_block((ranks, depth))]
        + [pl.BlockSpec((rank, part), lambda i: (0, i))] * sides,
        out_shape=[jax.ShapeDtypeStruct((ranks, depth), bf16)]
        + [jax.ShapeDtypeStruct((rank, blocks * part), bf16)] * sides,
        scratch_shapes=[
            pltpu.VMEM((micros, slots, ranks), bf16),
            pltpu.VMEM((micros, slots, ranks), f32),
            pltpu.VMEM((ranks, depth), f32),
            pltpu.VMEM((ranks, cols), f32),
        ],
        compiler_params=params(LARGE_MIB),
        cost_estimate=SHORT,
        name="adapter_in",
    )(*seen_inputs, *sent_grads, merged, tall, wide, share)


def adapter_out(seen_inputs, sent_grads, merged, first_t, second, share):
    micros = len(seen_inputs)
    slots, cols = sent_grads[0].shape
    depth = merged.shape[0]
    block = min(depth, UNIT_BLOCK)
    blocks = depth // block
    rank = second.shape[0]
    scale = ADAPTER_NUMER / ADAPTER_RANK

    def kernel(*refs):
        x_refs, d_refs, refs = refs[:micros], refs[micros : 2 * micros], refs[2 * micros :]
        v_ref, a_ref, b_ref, s_ref, left_ref, out_ref, seen_ref, sent_ref, right_ref = refs
        at = pl.program_id(0)
        second = b_ref[...]

        @pl.when(at == 0)
        def _():
            right_ref[...] = jnp.zeros_like(right_ref)
            seen_ref[...] = jnp.zeros_like(seen_ref)
            for m in range(micros):
                sent_ref[m] = contract_cols(d_refs[m][...], second.astype(bf16)).astype(bf16)

        first = a_ref[...].astype(bf16)
        left = -contract_cols((second * s_ref[...]).astype(bf16), v_ref[...])
        for m in range(micros):
            left = left + contract_rows(sent_ref[m], x_refs[m][...])
            seen_ref[m] += contract_cols(x_refs[m][...], first)
        left_ref[...] = (scale * left).astype(bf16)
        right_ref[...] += -jnp.dot(first, v_ref[...], preferred_element_type=f32) * s_ref[...]

        @pl.when(at == blocks - 1)
        def _():
            total = right_ref[...]
            for m in range(micros):
                total = total + contract_rows(seen_ref[m].astype(bf16), d_refs[m][...])
            out_ref[...] = (scale * total).astype(bf16)

    return pl.pallas_call(
        kernel,
        grid=(blocks,),
        in_specs=[pl.BlockSpec((slots, block), lambda i: (0, i))] * micros
        + [single((slots, cols))] * micros
        + [
            pl.BlockSpec((block, cols), lambda i: (i, 0)),
            pl.BlockSpec((rank, block), lambda i: (0, i)),
            single((rank, cols)),
            single((1, cols)),
        ],
        out_specs=[pl.BlockSpec((rank, block), lambda i: (0, i)), whole_block((rank, cols))],
        out_shape=[
            jax.ShapeDtypeStruct((rank, depth), bf16),
            jax.ShapeDtypeStruct((rank, cols), bf16),
        ],
        scratch_shapes=[
            pltpu.VMEM((micros, slots, rank), f32),
            pltpu.VMEM((micros, slots, rank), bf16),
            pltpu.VMEM((rank, cols), f32),
        ],
        compiler_params=params(LARGE_MIB),
        cost_estimate=SHORT,
        name="adapter_out",
    )(*seen_inputs, *sent_grads, merged, first_t, second, share)


def finish_input(scalars, total, tokens, middle_grad, gain, micro_at, micros, earlier):
    slots, width = middle_grad.shape
    pieces = len(total)

    def kernel(*refs):
        i_ref, *refs = refs
        x_ref, d_ref, g_ref = refs[pieces : pieces + 3]
        x = x_ref[...].astype(f32)
        back = rms_back(x, rms_scale(x), g_ref[...], load_total(refs[:pieces], i_ref[1]))
        refs[-1][...] = (d_ref[...] + back).astype(bf16)

    operands = [scalars, *total, tokens, middle_grad, gain]
    specs = [SCALARS] + [single(piece.shape) for piece in total]
    specs += [micro_tokens(micro_at, slots, width), single((slots, width)), single((1, width))]
    return write_micro(kernel, operands, specs, slots, width, micro_at, micros, earlier)


def finish_output(scalars, total, middle, ratio, micro_at, micros, earlier):
    slots, width = middle.shape
    pieces = len(total)

    def kernel(*refs):
        n_ref, *refs = refs
        m_ref, r_ref = refs[pieces : pieces + 2]
        live = lax.broadcasted_iota(jnp.int32, (slots, 1), 0) < n_ref[0]
        branch = load_total(refs[:pieces], n_ref[1]) * r_ref[...]
        refs[-1][...] = (m_ref[...] + jnp.where(live, branch, 0.0)).astype(bf16)

    operands = [scalars, *total, middle, ratio]
    specs = [SCALARS] + [single(operand.shape) for operand in operands[1:]]
    return write_micro(kernel, operands, specs, slots, width, micro_at, micros, earlier)


def write_micro(kernel, operands, specs, slots, width, micro_at, micros, earlier):
    aliases = {}
    if earlier is not None:
        aliases = {len(operands): 0}
        operands = operands + [earlier]
        specs = specs + [pl.BlockSpec(memory_space=pl.ANY)]
    return pl.pallas_call(
        kernel,
        grid=(1,),
        in_specs=specs,
        out_specs=pl.BlockSpec((None, None, slots, width), lambda i: (micro_at, 0, 0, 0)),
        out_shape=jax.ShapeDtypeStruct((micros, 1, slots, width), bf16),
        input_output_aliases=aliases,
        compiler_params=params(16),
        cost_estimate=SHORT,
        name="finish",
    )(*operands)


def after(value, *others):
    return lax.optimization_barrier((value, *others))[0]


def from_blocks(array, groups, units):
    ranks, total = array.shape
    array = array.reshape(ranks, total // (groups * UNIT_BLOCK), groups, UNIT_BLOCK)
    return jnp.transpose(array, (2, 0, 1, 3)).reshape(groups, ranks, total // groups)[..., :units]


def diagonal(second):
    groups, rank, cols = second.shape
    rows = [
        jnp.pad(second[g], ((g * rank, (groups - 1 - g) * rank), (0, 0))) for g in range(groups)
    ]
    return jnp.stack(rows)


def fast_device(
    inputs,
    lengths,
    prompt_mask,
    partner,
    positions,
    attn_gain,
    mlp_gain,
    attention_input_frozen,
    attention_input_first,
    attention_input_second,
    attention_input_magnitude,
    attention_output_frozen,
    attention_output_first,
    attention_output_second,
    attention_output_magnitude,
    feedforward_input_frozen,
    feedforward_input_first,
    feedforward_input_second,
    feedforward_input_magnitude,
    feedforward_output_frozen,
    feedforward_output_first,
    feedforward_output_second,
    feedforward_output_magnitude,
    grad_out,
):
    micros, _, slots, width = inputs.shape
    cols = attention_input_frozen.shape[2]
    units = feedforward_input_frozen.shape[2]
    rank = attention_output_second.shape[0]
    attn_row = attn_gain.astype(f32)[None]
    mlp_row = mlp_gain.astype(f32)[None]
    qkv_first_t = jnp.swapaxes(attention_input_first, 1, 2)
    gate_first_t = jnp.swapaxes(feedforward_input_first, 1, 2)
    out_first_t = attention_output_first.T
    down_first_t = feedforward_output_first.T
    out_magnitude = attention_output_magnitude[None]
    down_magnitude = feedforward_output_magnitude[None]

    me = lax.axis_index("dp")
    distance = partner[:, 0] ^ me
    sibling_distance = lax.ppermute(distance, "dp", [(i, i ^ 1) for i in range(8)])

    indices = jnp.arange(HEAD_DIM // 2, dtype=f32)
    inverse = rope_base ** (-2.0 * indices / HEAD_DIM)
    angles = positions.reshape(micros * slots).astype(f32)[:, None] * inverse[None, :]
    cosine, sine = jnp.cos(angles), jnp.sin(angles)
    cosine = jnp.concatenate([cosine, cosine], axis=1)
    sine_signed = jnp.concatenate([-sine, sine], axis=1)
    tokens = inputs.reshape(micros * slots, width)
    qkv_magnitude = attention_input_magnitude.reshape(1, -1)
    normed, qkv_merged, qkv_square, projected, *packs = merge_project(
        tokens,
        attn_row,
        jnp.swapaxes(attention_input_frozen, 0, 1),
        qkv_first_t,
        attention_input_second,
        qkv_magnitude,
        cosine,
        sine_signed,
        prompt_mask[:, 0, :FAR_SLOTS].astype(f32),
        slots,
    )
    qkv_inverse = lax.rsqrt(qkv_square)
    qkv_ratio = qkv_magnitude * qkv_inverse

    far_packs, held = [], []
    for m in range(micros):
        pack = after(packs[m], *held)
        far_pack, held = pair_exchange(pack, distance[m], sibling_distance[m])
        far_packs.append(far_pack)

    out_merged, out_square = merge_out(
        attention_output_frozen, out_first_t, after(attention_output_second, packs[0])
    )
    down_merged, down_square = merge_out(
        feedforward_output_frozen, down_first_t, after(feedforward_output_second, packs[0])
    )
    squares = line_total(jnp.concatenate([out_square, down_square], axis=0))
    out_inverse, down_inverse = lax.rsqrt(squares[:1]), lax.rsqrt(squares[1:])
    out_ratio = out_magnitude * out_inverse
    down_ratio = down_magnitude * down_inverse
    line_at = lax.axis_index("tensor")
    inner = ((line_at == 1) | (line_at == 2)).astype(jnp.int32)[None]
    scalars = [jnp.concatenate([lengths[m], inner]) for m in range(micros)]

    pieces = (2, 1)
    attended, parts = [], []
    turn = after(inner, squares)
    for m in range(micros):
        seen, *part = attend(turn, projected, far_packs[m], out_merged, pieces[m], m, slots)
        turn = after(inner, seen)
        attended.append(seen)
        parts.append(part)
    gate_rank = 2 * rank

    def merge_gate(pair):
        return merge_in(
            feedforward_input_frozen,
            gate_first_t,
            after(feedforward_input_second, attended[1], pair),
            feedforward_input_magnitude,
        )

    first_sum, found = tensor_sum(parts[0], merge_gate)
    gate_merged, gate_ratio, gate_inverse, gate_wide = found
    branch_sums = [first_sum, tensor_sum(parts[1])[0]]

    middles, normed_mlp, hiddens, gate_grads, gate_inner = [], [], [], [], 0.0
    db_parts, down_parts, down_grads, down_inner = [], [], [], 0.0
    turn = scalars[0]
    for m in range(micros):
        middle, b, d2, hidden, dgu, c_gate, c_down, y, *db = feed_forward(
            turn,
            branch_sums[m],
            inputs,
            grad_out,
            out_ratio,
            down_ratio,
            mlp_row,
            gate_merged,
            gate_ratio,
            down_merged,
            m,
        )
        turn = after(scalars[1], c_down)
        middles.append(middle)
        normed_mlp.append(b)
        hiddens.append(hidden)
        gate_grads.append(dgu)
        gate_inner = gate_inner + c_gate
        down_inner = down_inner + c_down
        down_grads.append(d2)
        db_parts.append(db)
        down_parts.append(y)
    gate_tall = gate_first_t.reshape(gate_rank, width).astype(bf16)

    def adapters_feed_forward(pair):
        inner_now, down_now = after(gate_inner, pair), after(down_inner, pair)
        down_now = line_total(down_now)
        in_found = adapter_in(
            normed_mlp,
            gate_grads,
            gate_merged,
            gate_tall,
            gate_wide,
            inner_now * gate_ratio * gate_inverse * gate_inverse,
            rank,
        )
        out_found = adapter_out(
            hiddens,
            down_grads,
            down_merged,
            jnp.pad(down_first_t, ((0, 0), (0, down_merged.shape[0] - units))),
            feedforward_output_second,
            down_now * down_ratio * down_inverse * down_inverse,
        )
        return [*in_found, *out_found, down_now]

    first_sum, found = tensor_sum(db_parts[0], adapters_feed_forward, [down_inner])
    gate_left, gate_right, up_right, down_left, down_right, down_inner = found
    db_sums = [first_sum, tensor_sum(db_parts[1])[0]]
    gate_mag = from_blocks(gate_inner * gate_inverse, 2, units)[:, 0]
    down_mag = down_inner * down_inverse
    down_parts = [after(y, db_sums[1][0]) for y in down_parts]
    down_sums = [tensor_sum([y])[0] for y in down_parts]

    middle_grads, out_grads, out_inner, qkv_grads, qkv_inner, da_parts = [], [], 0.0, [], 0.0, []
    exchanged = []
    turn = scalars[0]
    for m in range(micros):
        dh, d1, c_out, dy, far_grad = attend_back(
            turn,
            db_sums[m],
            middles[m],
            grad_out,
            branch_sums[m],
            mlp_row,
            out_ratio,
            out_merged,
            projected,
            far_packs[m],
            cosine,
            sine_signed,
            m,
        )
        turn = after(scalars[1], c_out)
        middle_grads.append(dh)
        out_grads.append(d1)
        out_inner = out_inner + c_out
        far_grad = after(far_grad, db_sums[1][0])
        returned, _ = pair_exchange(far_grad, distance[m], sibling_distance[m])
        exchanged.append((dy, returned))
    turn = inner
    for m in range(micros):
        dy, returned = exchanged[m]
        dqkv, c_qkv, *da = project_back(
            turn,
            dy,
            returned,
            projected,
            cosine,
            sine_signed,
            qkv_ratio,
            qkv_merged,
            2,
            m,
        )
        turn = after(inner, c_qkv)
        qkv_grads.append(dqkv)
        qkv_inner = qkv_inner + c_qkv
        da_parts.append(da)
    def adapters_attention(pair):
        out_now, qkv_now = after(out_inner, pair), after(qkv_inner, pair) / qkv_ratio
        out_found = adapter_out(
            attended,
            out_grads,
            out_merged,
            out_first_t,
            attention_output_second,
            out_now * out_ratio * out_inverse * out_inverse,
        )
        in_found = adapter_in(
            [normed],
            qkv_grads,
            qkv_merged,
            qkv_first_t.reshape(3 * rank, width).astype(bf16),
            jnp.concatenate(list(diagonal(attention_input_second)), axis=1),
            qkv_now * qkv_ratio * qkv_inverse * qkv_inverse,
            rank,
        )
        return [*out_found, *in_found, qkv_now]

    found = adapters_attention(qkv_inner)
    out_left, out_right, qkv_left, qkv_right, qkv_inner = found
    low_units = [piece[:, :units] for piece in (gate_right, up_right, down_left)]
    magnitudes = [gate_mag, down_mag, qkv_inner * qkv_inverse, out_inner * out_inverse]

    def wide(piece):
        return jnp.pad(piece.astype(bf16), ((0, 0), (0, width - piece.shape[1])))

    magnitudes = jnp.concatenate([wide(piece) for piece in magnitudes], axis=0)
    magnitudes = jnp.pad(magnitudes, ((0, rank - magnitudes.shape[0]), (0, 0)))
    pieces = [gate_left, down_right, qkv_left, out_right]
    line_rows = 7 * rank
    pieces += [wide(piece) for piece in low_units]
    pieces += [jnp.concatenate([qkv_right, out_left], axis=1), magnitudes]
    share = dp_share(jnp.concatenate(pieces, axis=0), line_rows)
    sums_in = [*down_sums[0], *down_sums[1], share]
    da_sums = [tensor_sum(part, None, sums_in)[0] for part in da_parts]
    totals = dp_gather(after(share, da_sums[1][0]))
    found, at = [], 0
    for piece in pieces:
        found.append(totals[at : at + piece.shape[0]])
        at += piece.shape[0]
    gate_left, down_right, qkv_left, out_right, gate_right, up_right, down_left, rights, mags = found
    gate_left = gate_left.reshape(2, rank, width)
    qkv_left = qkv_left.reshape(3, rank, width)
    gate_right = jnp.stack([gate_right[:, :units], up_right[:, :units]])
    down_left = down_left[:, :units]
    qkv_right = jnp.stack([rights[:, g * cols : (g + 1) * cols] for g in range(3)])
    out_left = rights[:, 3 * cols :]
    gate_mag, down_mag, out_mag = mags[:2, :units], mags[2], mags[4]
    qkv_mag = mags[3, : 3 * cols].reshape(3, cols)

    layer_out, layer_grad = None, None
    for m in range(micros):
        layer_out = finish_output(
            scalars[m], down_sums[m], middles[m], down_ratio, m, micros, layer_out
        )
    for m in range(micros):
        layer_grad = finish_input(
            scalars[m], da_sums[m], inputs, middle_grads[m], attn_row, m, micros, layer_grad
        )
    return (
        layer_out,
        layer_grad,
        jnp.swapaxes(qkv_left, 1, 2),
        qkv_right,
        qkv_mag,
        out_left.T,
        out_right,
        out_mag,
        jnp.swapaxes(gate_left, 1, 2),
        gate_right,
        gate_mag,
        down_left.T,
        down_right,
        down_mag,
    )


def solution(mesh):
    in_specs = (
        P(None, "dp", None, None),
        P(None, "dp"),
        P(None, "dp", None),
        P(None, "dp"),
        P(None, "dp", None),
        P(),
        P(),
        P(None, None, "tensor"),
        P(),
        P(None, None, "tensor"),
        P(None, "tensor"),
        P("tensor", None),
        P("tensor", None),
        P(),
        P(),
        P(None, None, "tensor"),
        P(),
        P(None, None, "tensor"),
        P(None, "tensor"),
        P("tensor", None),
        P("tensor", None),
        P(),
        P(),
        P(None, "dp", None, None),
    )
    out_specs = (
        P(None, "dp", None, None),
        P(None, "dp", None, None),
        P(),
        P(None, None, "tensor"),
        P(None, "tensor"),
        P("tensor", None),
        P(),
        P(),
        P(),
        P(None, None, "tensor"),
        P(None, "tensor"),
        P("tensor", None),
        P(),
        P(),
    )
    device_step = fast_device if fits_fast(mesh) else general_device
    return jax.shard_map(
        device_step, mesh=mesh, in_specs=in_specs, out_specs=out_specs, check_vma=False
    )
```

```python
import math

import jax
import jax.numpy as jnp
from jax import lax
from jax.experimental import pallas as pl
from jax.experimental.pallas import tpu as pltpu
from jax.sharding import PartitionSpec as P

HEAD_DIM = 128
ADAPTER_RANK = 16
ADAPTER_NUMER = 32


epsilon = 1e-05
rope_base = 10000.0
highest_precision = lax.Precision.HIGHEST
masked_score = -1e30


def rms_scale(values):
    return lax.rsqrt(jnp.mean(values * values, axis=-1, keepdims=True) + epsilon)


def rms_back(values, scale_rows, gain_row, gradient):
    scaled_update = gradient * gain_row
    normal = values * scale_rows
    return scale_rows * (
        scaled_update - normal * jnp.mean(scaled_update * normal, axis=-1, keepdims=True)
    )


def turn_half(values):
    middle = values.shape[-1] // 2
    return jnp.concatenate([-values[..., middle:], values[..., :middle]], axis=-1)


def rope_tables(positions, head_size):
    indices = jnp.arange(head_size // 2, dtype=jnp.float32)
    inverse = rope_base ** (-2.0 * indices / head_size)
    angles = positions.astype(jnp.float32)[:, None] * inverse[None, :]
    angles = jnp.concatenate([angles, angles], axis=-1)
    return (jnp.cos(angles)[:, None, :], jnp.sin(angles)[:, None, :])


def contract_rows(left_factor, right_factor):
    return lax.dot_general(
        left_factor, right_factor, (((0,), (0,)), ((), ())), preferred_element_type=jnp.float32
    )


def contract_cols(left_factor, right_factor):
    return lax.dot_general(
        left_factor, right_factor, (((1,), (1,)), ((), ())), preferred_element_type=jnp.float32
    )


def pick_partner(partner_row, far_slots, current, pieces):
    piece_rows = pieces[0].shape[0]
    wanted = partner_row * far_slots + jnp.arange(far_slots, dtype=jnp.int32)
    inside = (wanted >= 0) & (wanted < piece_rows)
    clipped = jnp.clip(wanted, 0, piece_rows - 1)
    packed = jnp.where(inside[:, None], jnp.take(pieces[0], clipped, axis=0), current[0])
    flags = jnp.where(inside, jnp.take(pieces[1], clipped, axis=0), current[1])
    return (packed, flags)


def place_far(partner_row, far_grad, row_count):
    far_slots = far_grad.shape[0]
    owners = jnp.arange(row_count // far_slots, dtype=jnp.int32)
    term = jnp.where((owners == partner_row)[:, None, None], far_grad[None], 0.0)
    return term.reshape(row_count, far_grad.shape[1])


def column_gradient_list(
    weight_total,
    merged_matrix,
    column_norm_value,
    column_magnitude,
    left_factor,
    right_factor,
    adapter_scale,
):
    inner = jnp.sum(weight_total * merged_matrix, axis=0)
    merged_matrix_gradient = (
        column_magnitude
        / column_norm_value
        * (weight_total - inner / (column_norm_value * column_norm_value) * merged_matrix)
    )
    left_factor_gradient = adapter_scale * jnp.einsum(
        "ypz,pvz->pyv", merged_matrix_gradient, right_factor, precision=highest_precision
    )
    right_factor_gradient = adapter_scale * jnp.einsum(
        "emn,mez->enz", left_factor, merged_matrix_gradient, precision=highest_precision
    )
    return (left_factor_gradient, right_factor_gradient, inner / column_norm_value)


def row_pieces_list(
    weight_total,
    merged_matrix,
    column_norm_value,
    column_magnitude,
    left_factor,
    right_factor,
    adapter_scale,
):
    scaled_update = weight_total * (column_magnitude / column_norm_value)
    inner = jnp.sum(weight_total * merged_matrix, axis=0)
    left_factor_part = adapter_scale * jnp.dot(
        scaled_update, right_factor.T, precision=highest_precision
    )
    right_factor_part = adapter_scale * jnp.dot(
        left_factor.T, scaled_update, precision=highest_precision
    )
    return (inner, left_factor_part, right_factor_part)


def general_device(
    inputs,
    lengths,
    prompt_mask,
    partner,
    positions,
    attn_gain,
    mlp_gain,
    attention_input_frozen,
    attention_input_first,
    attention_input_second,
    attention_input_magnitude,
    attention_output_frozen,
    attention_output_first,
    attention_output_second,
    attention_output_magnitude,
    feedforward_input_frozen,
    feedforward_input_first,
    feedforward_input_second,
    feedforward_input_magnitude,
    feedforward_output_frozen,
    feedforward_output_first,
    feedforward_output_second,
    feedforward_output_magnitude,
    grad_out,
):
    micro_count = inputs.shape[0]
    slot_count = inputs.shape[2]
    model_width = inputs.shape[3]
    head_cols = attention_input_frozen.shape[2]
    head_count = head_cols // HEAD_DIM
    unit_count = feedforward_input_frozen.shape[2]
    adapter_scale = ADAPTER_NUMER / ADAPTER_RANK
    score_scale = 1.0 / math.sqrt(HEAD_DIM)
    block_rows = min(512, slot_count)
    block_count = slot_count // block_rows
    attn_scale = attn_gain.astype(jnp.float32)
    mlp_scale = mlp_gain.astype(jnp.float32)
    query_key_value_merged = attention_input_frozen.astype(
        jnp.float32
    ) + adapter_scale * jnp.einsum(
        "kdr,kro->dko", attention_input_first, attention_input_second, precision=highest_precision
    )
    query_key_value_norm = jnp.sqrt(
        jnp.sum(query_key_value_merged * query_key_value_merged, axis=0)
    )
    qkv_weight = (
        (query_key_value_merged * (attention_input_magnitude / query_key_value_norm))
        .astype(jnp.bfloat16)
        .reshape(model_width, 3 * head_cols)
    )
    gate_merged_weight = feedforward_input_frozen.astype(jnp.float32) + adapter_scale * jnp.einsum(
        "kdr,kro->dko",
        feedforward_input_first,
        feedforward_input_second,
        precision=highest_precision,
    )
    gate_column_norm = jnp.sqrt(jnp.sum(gate_merged_weight * gate_merged_weight, axis=0))
    gate_up_weight = (
        (gate_merged_weight * (feedforward_input_magnitude / gate_column_norm))
        .astype(jnp.bfloat16)
        .reshape(model_width, 2 * unit_count)
    )
    output_merged_weight = attention_output_frozen.astype(jnp.float32) + adapter_scale * jnp.dot(
        attention_output_first, attention_output_second, precision=highest_precision
    )
    down_merged_weight = feedforward_output_frozen.astype(jnp.float32) + adapter_scale * jnp.dot(
        feedforward_output_first, feedforward_output_second, precision=highest_precision
    )
    out_square = jnp.sum(output_merged_weight * output_merged_weight, axis=0)
    down_square = jnp.sum(down_merged_weight * down_merged_weight, axis=0)
    output_cross_term = jnp.dot(
        attention_output_first.T, output_merged_weight, precision=highest_precision
    )
    down_cross_term = jnp.dot(
        feedforward_output_first.T, down_merged_weight, precision=highest_precision
    )
    out_square, down_square, output_cross_term, down_cross_term = (
        lax.psum(out_square.astype(jnp.bfloat16), "tensor").astype(jnp.float32),
        lax.psum(down_square.astype(jnp.bfloat16), "tensor").astype(jnp.float32),
        lax.psum(output_cross_term.astype(jnp.bfloat16), "tensor").astype(jnp.float32),
        lax.psum(down_cross_term.astype(jnp.bfloat16), "tensor").astype(jnp.float32),
    )
    output_column_norm = jnp.sqrt(out_square)
    down_column_norm = jnp.sqrt(down_square)
    out_weight = (output_merged_weight * (attention_output_magnitude / output_column_norm)).astype(
        jnp.bfloat16
    )
    down_weight = (down_merged_weight * (feedforward_output_magnitude / down_column_norm)).astype(
        jnp.bfloat16
    )
    grad_qkv = jnp.zeros((model_width, 3 * head_cols), jnp.float32)
    output_projection_gradient = jnp.zeros((head_cols, model_width), jnp.float32)
    grad_gate_up = jnp.zeros((model_width, 2 * unit_count), jnp.float32)
    down_projection_gradient = jnp.zeros((unit_count, model_width), jnp.float32)
    results = []
    input_grads = []
    for micro_at in range(micro_count):
        tokens = inputs[micro_at, 0].astype(jnp.float32)
        length_now = lengths[micro_at, 0]
        partner_row = partner[micro_at, 0]
        cosine, sine_tab = rope_tables(positions[micro_at, 0], HEAD_DIM)
        live_mask = (jnp.arange(slot_count) < length_now).astype(jnp.float32)[:, None]
        attn_rows = rms_scale(tokens)
        normed = (tokens * attn_rows * attn_scale).astype(jnp.bfloat16)
        projected = jnp.dot(normed, qkv_weight, preferred_element_type=jnp.float32).reshape(
            slot_count, 3, head_count, HEAD_DIM
        )
        queries = (projected[:, 0] * cosine + turn_half(projected[:, 0]) * sine_tab).astype(
            jnp.bfloat16
        )
        keys_rot = (projected[:, 1] * cosine + turn_half(projected[:, 1]) * sine_tab).astype(
            jnp.bfloat16
        )
        values_in = projected[:, 2].astype(jnp.bfloat16)
        own_pack = jnp.concatenate(
            [keys_rot.reshape(slot_count, head_cols), values_in.reshape(slot_count, head_cols)],
            axis=1,
        )
        own_flags = prompt_mask[micro_at, 0].astype(jnp.bfloat16)
        empty_pack = (
            jnp.zeros((slot_count, 2 * head_cols), jnp.bfloat16),
            jnp.zeros((slot_count,), jnp.bfloat16),
        )
        far_pack, far_flags = pick_partner(
            partner_row,
            slot_count,
            empty_pack,
            (
                lax.all_gather(own_pack, "dp", axis=0, tiled=True),
                lax.all_gather(own_flags, "dp", axis=0, tiled=True),
            ),
        )
        all_keys = jnp.concatenate(
            [keys_rot, far_pack[:, :head_cols].reshape(slot_count, head_count, HEAD_DIM)], axis=0
        )
        all_values = jnp.concatenate(
            [values_in, far_pack[:, head_cols:].reshape(slot_count, head_count, HEAD_DIM)], axis=0
        )
        far_ok = far_flags > 0

        def block_scores(queries_blk, first_row):
            raw = (
                jnp.einsum(
                    "ihd,jhd->hij", queries_blk, all_keys, preferred_element_type=jnp.float32
                )
                * score_scale
            )
            rows_at = first_row + jnp.arange(block_rows)[:, None]
            own_ok = jnp.arange(slot_count)[None, :] <= rows_at
            allowed = jnp.concatenate(
                [own_ok, jnp.broadcast_to(far_ok[None, :], (block_rows, slot_count))], axis=1
            )
            return jnp.where(allowed[None], raw, masked_score)

        def forward_block(block_at):
            first_row = block_at * block_rows
            scores = block_scores(queries, first_row)
            row_top = jnp.max(scores, axis=-1, keepdims=True)
            exponent = jnp.exp(scores - row_top)
            row_total = jnp.sum(exponent, axis=-1, keepdims=True)
            shares = (exponent / row_total).astype(jnp.bfloat16)
            attended_blk = jnp.einsum(
                "hij,jhd->ihd", shares, all_values, preferred_element_type=jnp.float32
            )
            return (
                attended_blk.reshape(block_rows, head_cols).astype(jnp.bfloat16),
                row_top,
                row_total,
            )

        attended, row_tops, row_totals = lax.map(
            forward_block, jnp.arange(block_count, dtype=jnp.int32)
        )
        attended = attended.reshape(slot_count, head_cols)
        branch = lax.psum(
            jnp.dot(attended, out_weight, preferred_element_type=jnp.float32).astype(jnp.bfloat16),
            "tensor",
        ).astype(jnp.float32)
        middle = tokens + live_mask * branch
        mlp_rows = rms_scale(middle)
        normed_mlp = (middle * mlp_rows * mlp_scale).astype(jnp.bfloat16)
        gate_up = jnp.dot(normed_mlp, gate_up_weight, preferred_element_type=jnp.float32)
        gate_pre = gate_up[:, :unit_count]
        up_pre = gate_up[:, unit_count:]
        gate_sigmoid = jax.nn.sigmoid(gate_pre)
        activated = gate_pre * gate_sigmoid
        hidden = (activated * up_pre).astype(jnp.bfloat16)
        branch_mlp = lax.psum(
            jnp.dot(hidden, down_weight, preferred_element_type=jnp.float32).astype(jnp.bfloat16),
            "tensor",
        ).astype(jnp.float32)
        results.append((middle + live_mask * branch_mlp).astype(jnp.bfloat16))
        upstream = grad_out[micro_at, 0].astype(jnp.float32)
        down_grad = (live_mask * upstream).astype(jnp.bfloat16)
        hidden_grad = contract_cols(down_grad, down_weight)
        down_projection_gradient = down_projection_gradient + contract_rows(hidden, down_grad)
        gate_grad = (
            hidden_grad * up_pre * gate_sigmoid * (1.0 + gate_pre * (1.0 - gate_sigmoid))
        ).astype(jnp.bfloat16)
        up_grad = (hidden_grad * activated).astype(jnp.bfloat16)
        gate_up_grad = jnp.concatenate([gate_grad, up_grad], axis=1)
        grad_gate_up = grad_gate_up + contract_rows(normed_mlp, gate_up_grad)
        mlp_in_grad = lax.psum(
            contract_cols(gate_up_grad, gate_up_weight).astype(jnp.bfloat16), "tensor"
        ).astype(jnp.float32)
        middle_grad = upstream + rms_back(middle, mlp_rows, mlp_scale, mlp_in_grad)
        attn_grad = (live_mask * middle_grad).astype(jnp.bfloat16)
        output_projection_gradient = output_projection_gradient + contract_rows(attended, attn_grad)
        attended_grad = (
            contract_cols(attn_grad, out_weight)
            .astype(jnp.bfloat16)
            .reshape(slot_count, head_count, HEAD_DIM)
        )

        def backward_block(carried, block_at):
            first_row = block_at * block_rows
            row_top = row_tops[block_at]
            row_total = row_totals[block_at]
            scores = block_scores(queries, first_row)
            shares = jnp.exp(scores - row_top) / row_total
            shares_low = shares.astype(jnp.bfloat16)
            share_grad = jnp.einsum(
                "ihd,jhd->hij", attended_grad, all_values, preferred_element_type=jnp.float32
            )
            inner = jnp.sum(shares * share_grad, axis=-1, keepdims=True)
            score_grad = (shares * (share_grad - inner)).astype(jnp.bfloat16)
            query_grad = (
                jnp.einsum("hij,jhd->ihd", score_grad, all_keys, preferred_element_type=jnp.float32)
                * score_scale
            )
            key_part = (
                jnp.einsum("hij,ihd->jhd", score_grad, queries, preferred_element_type=jnp.float32)
                * score_scale
            )
            value_part = jnp.einsum(
                "hij,ihd->jhd", shares_low, attended_grad, preferred_element_type=jnp.float32
            )
            query_grad, key_part, value_part = (query_grad, key_part, value_part)
            return ((carried[0] + key_part, carried[1] + value_part), query_grad)

        key_zero = jnp.zeros((slot_count + slot_count, head_count, HEAD_DIM), jnp.float32)
        (key_grad, value_grad), query_grads = lax.scan(
            backward_block, (key_zero, key_zero), jnp.arange(block_count, dtype=jnp.int32)
        )
        far_grad = jnp.concatenate(
            [
                key_grad[slot_count:].reshape(slot_count, head_cols),
                value_grad[slot_count:].reshape(slot_count, head_cols),
            ],
            axis=1,
        )
        far_low = far_grad.astype(jnp.bfloat16)
        returned = lax.psum_scatter(
            place_far(
                partner_row, far_low.astype(jnp.float32), slot_count * lax.axis_size("dp")
            ).astype(jnp.bfloat16),
            "dp",
            scatter_dimension=0,
            tiled=True,
        ).astype(jnp.float32)
        key_total = key_grad[:slot_count] + returned[:, :head_cols].reshape(
            slot_count, head_count, HEAD_DIM
        )
        value_total = value_grad[:slot_count] + returned[:, head_cols:].reshape(
            slot_count, head_count, HEAD_DIM
        )
        query_total = query_grads.reshape(slot_count, head_count, HEAD_DIM)
        query_back = (query_total * cosine - turn_half(query_total * sine_tab)).astype(jnp.bfloat16)
        key_back = (key_total * cosine - turn_half(key_total * sine_tab)).astype(jnp.bfloat16)
        value_back = value_total.astype(jnp.bfloat16)
        qkv_grad = jnp.concatenate(
            [
                query_back.reshape(slot_count, head_cols),
                key_back.reshape(slot_count, head_cols),
                value_back.reshape(slot_count, head_cols),
            ],
            axis=1,
        )
        grad_qkv = grad_qkv + contract_rows(normed, qkv_grad)
        attn_in_grad = lax.psum(
            contract_cols(qkv_grad, qkv_weight).astype(jnp.bfloat16), "tensor"
        ).astype(jnp.float32)
        input_grads.append(
            (middle_grad + rms_back(tokens, attn_rows, attn_scale, attn_in_grad)).astype(
                jnp.bfloat16
            )
        )
    query_key_value_total = grad_qkv.reshape(model_width, 3, head_cols)
    gate_weight_total = grad_gate_up.reshape(model_width, 2, unit_count)
    qkv_left, qkv_right, qkv_mag = column_gradient_list(
        query_key_value_total,
        query_key_value_merged,
        query_key_value_norm,
        attention_input_magnitude,
        attention_input_first,
        attention_input_second,
        adapter_scale,
    )
    gate_left, gate_right, gate_mag = column_gradient_list(
        gate_weight_total,
        gate_merged_weight,
        gate_column_norm,
        feedforward_input_magnitude,
        feedforward_input_first,
        feedforward_input_second,
        adapter_scale,
    )
    out_inner, output_left_factor, output_right_factor = row_pieces_list(
        output_projection_gradient,
        output_merged_weight,
        output_column_norm,
        attention_output_magnitude,
        attention_output_first,
        attention_output_second,
        adapter_scale,
    )
    down_inner, down_left_factor, down_right_factor = row_pieces_list(
        down_projection_gradient,
        down_merged_weight,
        down_column_norm,
        feedforward_output_magnitude,
        feedforward_output_first,
        feedforward_output_second,
        adapter_scale,
    )
    qkv_left, gate_left, output_right_factor, down_right_factor, out_inner, down_inner = lax.psum(
        (qkv_left, gate_left, output_right_factor, down_right_factor, out_inner, down_inner),
        ("dp", "tensor"),
    )
    qkv_right, qkv_mag, gate_right, gate_mag, output_left_factor, down_left_factor = (
        lax.psum(qkv_right.astype(jnp.bfloat16), "dp").astype(jnp.float32),
        lax.psum(qkv_mag.astype(jnp.bfloat16), "dp").astype(jnp.float32),
        lax.psum(gate_right.astype(jnp.bfloat16), "dp").astype(jnp.float32),
        lax.psum(gate_mag.astype(jnp.bfloat16), "dp").astype(jnp.float32),
        lax.psum(output_left_factor.astype(jnp.bfloat16), "dp").astype(jnp.float32),
        lax.psum(down_left_factor.astype(jnp.bfloat16), "dp").astype(jnp.float32),
    )
    output_norm_factor = (
        attention_output_magnitude
        * out_inner
        / (output_column_norm * output_column_norm * output_column_norm)
    )
    down_norm_factor = (
        feedforward_output_magnitude
        * down_inner
        / (down_column_norm * down_column_norm * down_column_norm)
    )
    output_left_factor = output_left_factor - adapter_scale * jnp.dot(
        output_merged_weight * output_norm_factor,
        attention_output_second.T,
        precision=highest_precision,
    )
    down_left_factor = down_left_factor - adapter_scale * jnp.dot(
        down_merged_weight * down_norm_factor,
        feedforward_output_second.T,
        precision=highest_precision,
    )
    output_right_factor = (
        output_right_factor - adapter_scale * output_cross_term * output_norm_factor
    )
    down_right_factor = down_right_factor - adapter_scale * down_cross_term * down_norm_factor
    out_mag = out_inner / output_column_norm
    down_mag = down_inner / down_column_norm
    layer_out = jnp.stack(results)[:, None]
    layer_grad = jnp.stack(input_grads)[:, None]
    return (
        layer_out,
        layer_grad,
        qkv_left,
        qkv_right,
        qkv_mag,
        output_left_factor,
        output_right_factor,
        out_mag,
        gate_left,
        gate_right,
        gate_mag,
        down_left_factor,
        down_right_factor,
        down_mag,
    )


FAR_SLOTS = 128
LANES = 128
MIB = 1024 * 1024
f32 = jnp.float32
bf16 = jnp.bfloat16


def fits_fast(mesh):
    return mesh.shape["dp"] == 8 and mesh.shape["tensor"] == 4


def split_high_low(value):
    high = value.astype(bf16)
    return high, (value - high.astype(f32)).astype(bf16)


def adapter_product(first_t, second):
    a_high, a_low = split_high_low(first_t)
    b_high, b_low = split_high_low(second)
    left = jnp.concatenate([a_high, a_low, a_high], axis=0)
    right = jnp.concatenate([b_high, b_high, b_low], axis=0)
    return contract_rows(left, right)


def params(mib):
    return pltpu.CompilerParams(vmem_limit_bytes=mib * MIB)


def single(shape):
    zeros = (0,) * len(shape)
    return pl.BlockSpec(shape, lambda *_: zeros, pipeline_mode=pl.Buffered(1))


def micro_rows(micro_at, slots, width):
    return pl.BlockSpec((slots, width), lambda *_: (micro_at, 0), pipeline_mode=pl.Buffered(1))


def micro_tokens(micro_at, slots, width):
    return pl.BlockSpec(
        (None, None, slots, width),
        lambda *_: (micro_at, 0, 0, 0),
        pipeline_mode=pl.Buffered(1),
    )


SCALARS = pl.BlockSpec(memory_space=pltpu.SMEM)
SHORT = pl.CostEstimate(flops=1, bytes_accessed=1, transcendentals=0)


def whole_block(shape):
    zeros = (0,) * len(shape)
    return pl.BlockSpec(shape, lambda *_: zeros)


UNIT_BLOCK = 256
LARGE_MIB = 56


def padded(units):
    return -(-units // UNIT_BLOCK) * UNIT_BLOCK


def adapter_rows(second):
    high, low = split_high_low(second * (ADAPTER_NUMER / ADAPTER_RANK))
    return jnp.concatenate([high, high, low], axis=0)


def adapter_columns(first_t):
    high, low = split_high_low(first_t)
    return jnp.concatenate([high, low, high], axis=0)


def partial_squares(value):
    return jnp.sum((value * value).reshape(value.shape[0] // 8, 8, value.shape[1]), axis=0)


def merge_chunk(base, columns, rows):
    return base.astype(f32) + contract_rows(columns, rows)


def merge_in(frozen, first_t, second, magnitude):
    depth, groups, cols = frozen.shape
    rank = second.shape[1]
    blocks = padded(cols) // UNIT_BLOCK
    total = blocks * groups * UNIT_BLOCK
    row_block = 256
    steps = depth // row_block

    def kernel(w_ref, a_ref, b_ref, m_ref, v_ref, ratio_ref, inverse_ref, wide_ref, r_ref, sq_ref):
        at = pl.program_id(0)

        def pieces():
            for g in range(groups):
                for j in range(blocks):
                    count = min(UNIT_BLOCK, cols - j * UNIT_BLOCK)
                    start = (j * groups + g) * UNIT_BLOCK
                    yield g, j, slice(j * UNIT_BLOCK, j * UNIT_BLOCK + count), start, count

        @pl.when(at == 0)
        def _():
            sq_ref[...] = jnp.zeros_like(sq_ref)
            wide_ref[...] = jnp.zeros_like(wide_ref)
            for g in range(groups):
                r_ref[g] = adapter_rows(b_ref[g])
            for g, j, here, start, count in pieces():
                ranks = slice(g * rank, (g + 1) * rank)
                wide_ref[ranks, start : start + count] = b_ref[g, :, here]

        left = [adapter_columns(a_ref[g]) for g in range(groups)]
        for g, j, here, start, count in pieces():
            v = merge_chunk(w_ref[:, g, here], left[g], r_ref[g, :, here])
            at_g = g * UNIT_BLOCK
            v_ref[j, :, at_g : at_g + count] = v.astype(bf16)
            if count < UNIT_BLOCK:
                v_ref[j, :, at_g + count : at_g + UNIT_BLOCK] = jnp.zeros(
                    (row_block, UNIT_BLOCK - count), bf16
                )
            sq_ref[:, start : start + count] += partial_squares(v)

        @pl.when(at == steps - 1)
        def _():
            ratio_ref[...] = jnp.zeros_like(ratio_ref)
            inverse_ref[...] = jnp.zeros_like(inverse_ref)
            for g, j, here, start, count in pieces():
                there = slice(start, start + count)
                inverse = lax.rsqrt(jnp.sum(sq_ref[:, there], axis=0, keepdims=True))
                inverse_ref[:, there] = inverse
                ratio_ref[:, there] = m_ref[g : g + 1, here] * inverse

    return pl.pallas_call(
        kernel,
        grid=(steps,),
        in_specs=[
            pl.BlockSpec((row_block, groups, cols), lambda i: (i, 0, 0)),
            pl.BlockSpec((groups, rank, row_block), lambda i: (0, 0, i)),
            whole_block((groups, rank, cols)),
            whole_block((groups, cols)),
        ],
        out_specs=[
            pl.BlockSpec((blocks, row_block, groups * UNIT_BLOCK), lambda i: (0, i, 0)),
            whole_block((1, total)),
            whole_block((1, total)),
            whole_block((groups * rank, total)),
        ],
        out_shape=[
            jax.ShapeDtypeStruct((blocks, depth, groups * UNIT_BLOCK), bf16),
            jax.ShapeDtypeStruct((1, total), f32),
            jax.ShapeDtypeStruct((1, total), f32),
            jax.ShapeDtypeStruct((groups * rank, total), f32),
        ],
        scratch_shapes=[
            pltpu.VMEM((groups, 3 * rank, cols), bf16),
            pltpu.VMEM((8, total), f32),
        ],
        compiler_params=params(LARGE_MIB),
        cost_estimate=SHORT,
        name="merge_in",
    )(frozen, first_t, second, magnitude)


def merge_out(frozen, first_t, second):
    depth, cols = frozen.shape
    rank = second.shape[0]
    row_block = UNIT_BLOCK
    blocks = padded(depth) // row_block
    chunk = 512

    def kernel(w_ref, a_ref, b_ref, v_ref, total_ref, r_ref, sq_ref):
        at = pl.program_id(0)

        @pl.when(at == 0)
        def _():
            sq_ref[...] = jnp.zeros_like(sq_ref)
            r_ref[...] = adapter_rows(b_ref[...])

        left = adapter_columns(a_ref[...])
        within = at * row_block + lax.broadcasted_iota(jnp.int32, (row_block, 1), 0) < depth
        for j in range(cols // chunk):
            here = slice(j * chunk, (j + 1) * chunk)
            v = jnp.where(within, merge_chunk(w_ref[:, here], left, r_ref[:, here]), 0.0)
            v_ref[:, here] = v.astype(bf16)
            sq_ref[:, here] += partial_squares(v)

        @pl.when(at == blocks - 1)
        def _():
            total_ref[...] = jnp.sum(sq_ref[...], axis=0, keepdims=True)

    return pl.pallas_call(
        kernel,
        grid=(blocks,),
        in_specs=[
            pl.BlockSpec((row_block, cols), lambda i: (i, 0)),
            pl.BlockSpec((rank, row_block), lambda i: (0, i)),
            whole_block((rank, cols)),
        ],
        out_specs=[pl.BlockSpec((row_block, cols), lambda i: (i, 0)), whole_block((1, cols))],
        out_shape=[
            jax.ShapeDtypeStruct((blocks * row_block, cols), bf16),
            jax.ShapeDtypeStruct((1, cols), f32),
        ],
        scratch_shapes=[pltpu.VMEM((3 * rank, cols), bf16), pltpu.VMEM((8, cols), f32)],
        compiler_params=params(10),
        cost_estimate=SHORT,
        name="merge_out",
    )(frozen, first_t, second)


def rotate(values, cosine, sine_signed):
    return values * cosine + pltpu.roll(values, HEAD_DIM // 2, 1) * sine_signed


def rotate_back(values, cosine, sine_signed):
    return values * cosine - pltpu.roll(values, HEAD_DIM // 2, 1) * sine_signed


def merge_project(
    tokens, gain, frozen, first_t, second, magnitude, cosine, sine_signed, flags, slots
):
    count, width = tokens.shape
    cols = frozen.shape[2]
    rank = second.shape[1]
    heads = cols // HEAD_DIM
    chunk_rows, chunk_cols = 256, 256
    micros = count // slots

    def kernel(*refs):
        x_ref, g_ref, w_ref, a_ref, b_ref, m_ref, c_ref, n_ref, f_ref = refs[:9]
        o_ref, v_ref, sq_ref, y_ref, *pack_refs = refs[9:]
        part = pl.program_id(0)

        @pl.when(part == 0)
        def _():
            for m in range(micros):
                pack_refs[m][FAR_SLOTS:, :] = jnp.zeros((16, 2 * cols), bf16)
                pack_refs[m][FAR_SLOTS : FAR_SLOTS + 1, :FAR_SLOTS] = f_ref[m : m + 1].astype(bf16)
            for r in range(0, count, chunk_rows):
                x = x_ref[r : r + chunk_rows].astype(f32)
                o_ref[r : r + chunk_rows] = (x * rms_scale(x) * g_ref[...]).astype(bf16)

        right = adapter_rows(b_ref[...])
        for c in range(0, cols, chunk_cols):
            here = slice(c, c + chunk_cols)
            square = 0.0
            for r in range(0, width, chunk_rows):
                left = adapter_columns(a_ref[:, r : r + chunk_rows])
                v = merge_chunk(w_ref[r : r + chunk_rows, here], left, right[:, here])
                v_ref[r : r + chunk_rows, here] = v.astype(bf16)
                square = square + partial_squares(v)
            square = jnp.sum(square, axis=0, keepdims=True)
            sq_ref[:, here] = square
            ratio = m_ref[:, here] * lax.rsqrt(square)
            total = jnp.dot(o_ref[...], v_ref[:, here], preferred_element_type=f32) * ratio
            for h in range(0, chunk_cols, HEAD_DIM):
                turned = rotate(total[:, h : h + HEAD_DIM], c_ref[...], n_ref[...])
                y_ref[:, c + h : c + h + HEAD_DIM] = jnp.where(
                    part < 2, turned, total[:, h : h + HEAD_DIM]
                ).astype(bf16)

        for kept in (1, 2):

            @pl.when(part == kept)
            def _(first=(kept - 1) * cols):
                for m in range(micros):
                    rows = y_ref[m * slots : m * slots + FAR_SLOTS, :]
                    pack_refs[m][:FAR_SLOTS, first : first + cols] = rows

    return pl.pallas_call(
        kernel,
        grid=(3,),
        in_specs=[
            whole_block((count, width)),
            whole_block((1, width)),
            pl.BlockSpec((None, width, cols), lambda i: (i, 0, 0)),
            pl.BlockSpec((None, rank, width), lambda i: (i, 0, 0)),
            pl.BlockSpec((None, rank, cols), lambda i: (i, 0, 0)),
            pl.BlockSpec((1, cols), lambda i: (0, i)),
            whole_block((count, HEAD_DIM)),
            whole_block((count, HEAD_DIM)),
            whole_block(flags.shape),
        ],
        out_specs=[
            whole_block((count, width)),
            pl.BlockSpec((None, width, cols), lambda i: (i, 0, 0)),
            pl.BlockSpec((1, cols), lambda i: (0, i)),
            pl.BlockSpec((count, cols), lambda i: (0, i)),
        ]
        + [whole_block((FAR_SLOTS + 16, 2 * cols))] * micros,
        out_shape=[
            jax.ShapeDtypeStruct((count, width), bf16),
            jax.ShapeDtypeStruct((3, width, cols), bf16),
            jax.ShapeDtypeStruct((1, 3 * cols), f32),
            jax.ShapeDtypeStruct((count, 3 * cols), bf16),
        ]
        + [jax.ShapeDtypeStruct((FAR_SLOTS + 16, 2 * cols), bf16)] * micros,
        compiler_params=params(LARGE_MIB),
        cost_estimate=SHORT,
        name="merge_project",
    )(tokens, gain, frozen, first_t, second, magnitude, cosine, sine_signed, flags)


def head_shares(q, k, far_k, far_ok):
    scale = 1.0 / math.sqrt(HEAD_DIM)
    own = contract_cols(q, k) * scale
    far = contract_cols(q, far_k) * scale
    rows_at = lax.broadcasted_iota(jnp.int32, own.shape, 0)
    slots_at = lax.broadcasted_iota(jnp.int32, own.shape, 1)
    own = jnp.where(slots_at <= rows_at, own, masked_score)
    far = jnp.where(far_ok > 0, far, masked_score)
    scores = jnp.concatenate([own, far], axis=1)
    top = jnp.max(scores, axis=-1, keepdims=True)
    exponent = jnp.exp(scores - top)
    return exponent / jnp.sum(exponent, axis=-1, keepdims=True)


def store_part(value, refs, inner):
    if len(refs) == 1:
        refs[0][...] = value
        return
    half = value.shape[0] // 2

    @pl.when(inner == 1)
    def _():
        refs[0][...] = value[half:]
        refs[1][...] = value[:half]

    @pl.when(inner != 1)
    def _():
        refs[0][...] = value[:half]
        refs[1][...] = value[half:]


def load_total(refs, inner):
    if len(refs) == 1:
        return refs[0][...].astype(f32)
    mine, other = refs[0][...], refs[1][...]
    flip = inner == 1
    first = jnp.where(flip, other, mine)
    last = jnp.where(flip, mine, other)
    return jnp.concatenate([first, last], axis=0).astype(f32)


def part_shapes(slots, width, pieces):
    return [jax.ShapeDtypeStruct((slots // pieces, width), bf16)] * pieces


def attend(inner, projected, far_pack, out_merged, pieces, micro_at, slots):
    cols = projected.shape[1] // 3
    heads = cols // HEAD_DIM
    width = out_merged.shape[1]

    def kernel(i_ref, y_ref, f_ref, w_ref, o_ref, *z_refs):
        far_ok = f_ref[FAR_SLOTS : FAR_SLOTS + 1, :FAR_SLOTS].astype(f32)
        for h in range(heads):
            at = slice(h * HEAD_DIM, (h + 1) * HEAD_DIM)
            far_k = f_ref[:FAR_SLOTS, h * HEAD_DIM : (h + 1) * HEAD_DIM]
            far_v = f_ref[:FAR_SLOTS, cols + h * HEAD_DIM : cols + (h + 1) * HEAD_DIM]
            k = y_ref[:, cols + h * HEAD_DIM : cols + (h + 1) * HEAD_DIM]
            v = y_ref[:, 2 * cols + h * HEAD_DIM : 2 * cols + (h + 1) * HEAD_DIM]
            shares = head_shares(y_ref[:, at], k, far_k, far_ok).astype(bf16)
            values = jnp.concatenate([v, far_v], axis=0)
            o_ref[:, at] = jnp.dot(shares, values, preferred_element_type=f32).astype(bf16)
        part = jnp.dot(o_ref[...], w_ref[...], preferred_element_type=f32).astype(bf16)
        store_part(part, z_refs, i_ref[0])

    return pl.pallas_call(
        kernel,
        grid=(1,),
        in_specs=[
            SCALARS,
            micro_rows(micro_at, slots, 3 * cols),
            single(far_pack.shape),
            single(out_merged.shape),
        ],
        out_specs=[single((slots, cols))] + [single((slots // pieces, width))] * pieces,
        out_shape=[jax.ShapeDtypeStruct((slots, cols), bf16)]
        + part_shapes(slots, width, pieces),
        compiler_params=params(14),
        cost_estimate=SHORT,
        name="attend",
    )(inner, projected, far_pack, out_merged)


def feed_forward(
    scalars,
    branch_sum,
    tokens,
    upstream,
    out_ratio,
    down_ratio,
    gain,
    merged,
    ratio,
    down_merged,
    micro_at,
    db_pieces,
    y_pieces,
):
    slots, width = tokens.shape[2:]
    units = down_merged.shape[0]
    block = UNIT_BLOCK
    blocks = units // block
    pieces = len(branch_sum)
    chunk = 512

    def kernel(*refs):
        n_ref, *refs = refs
        s_refs, refs = refs[:pieces], refs[pieces:]
        x_ref, u_ref, or_ref, dr_ref, g_ref, w_hbm, r_ref, wd_hbm = refs[:8]
        outs, refs = refs[8:13], refs[13:]
        cgu_ref, cd_ref, *refs = refs
        db_refs, y_refs = refs[:db_pieces], refs[db_pieces : db_pieces + y_pieces]
        refs = refs[db_pieces + y_pieces :]
        w_ref, wd_ref, h_ref, b_ref, d2_ref, hid_ref, dgu_ref, db_ref, y_ref = refs[:9]
        in_sems, out_sems = refs[9:]
        loads = []
        for j in range(blocks):
            gate_up = slice(j * 2 * block, (j + 1) * 2 * block)
            rows = slice(j * block, (j + 1) * block)
            loads.append(
                (
                    pltpu.make_async_copy(w_hbm.at[j], w_ref.at[:, gate_up], in_sems.at[0, j]),
                    pltpu.make_async_copy(wd_hbm.at[rows], wd_ref.at[rows], in_sems.at[1, j]),
                )
            )
            for load in loads[-1]:
                load.start()
        held = (h_ref, b_ref, d2_ref, hid_ref, dgu_ref)
        stores = [
            pltpu.make_async_copy(ref, out, out_sems.at[i])
            for i, (ref, out) in enumerate(zip(held, outs))
        ]
        live = lax.broadcasted_iota(jnp.int32, (slots, 1), 0) < n_ref[0]
        branch = load_total(s_refs, n_ref[1]) * or_ref[...]
        h = x_ref[...].astype(f32) + jnp.where(live, branch, 0.0)
        h_ref[...] = h
        b_ref[...] = (h * rms_scale(h) * g_ref[...]).astype(bf16)
        d2_ref[...] = jnp.where(live, u_ref[...].astype(f32) * dr_ref[...], 0.0).astype(bf16)
        for store in stores[:3]:
            store.start()
        for j in range(blocks):
            gate_up = slice(j * 2 * block, (j + 1) * 2 * block)
            rows = slice(j * block, (j + 1) * block)
            for load in loads[j]:
                load.wait()
            raw = jnp.dot(b_ref[...], w_ref[:, gate_up], preferred_element_type=f32)
            dhidden = contract_cols(d2_ref[...], wd_ref[rows])
            scaled = raw * r_ref[:, gate_up]
            gate, up = scaled[:, :block], scaled[:, block:]
            sigmoid = jax.nn.sigmoid(gate)
            activated = gate * sigmoid
            hid_ref[:, rows] = (activated * up).astype(bf16)
            dgate = dhidden * up * sigmoid * (1.0 + gate * (1.0 - sigmoid))
            back = jnp.concatenate([dgate, dhidden * activated], axis=1)
            cgu_ref[:, gate_up] = jnp.sum(back * raw, axis=0, keepdims=True)
            dgu_ref[:, gate_up] = (back * r_ref[:, gate_up]).astype(bf16)
        for store in stores[3:]:
            store.start()
        for start in range(0, width, chunk):
            here = slice(start, start + chunk)
            db_ref[:, here] = contract_cols(dgu_ref[...], w_ref[here, :]).astype(bf16)
            y = jnp.dot(hid_ref[...], wd_ref[:, here], preferred_element_type=f32)
            y_ref[:, here] = y.astype(bf16)
            d2 = jnp.where(live, u_ref[:, here].astype(f32), 0.0)
            cd_ref[:, here] = jnp.sum(d2 * y, axis=0, keepdims=True)
        store_part(db_ref[...], db_refs, n_ref[1])
        store_part(y_ref[...], y_refs, n_ref[1])
        for store in stores:
            store.wait()

    row = single((1, width))
    micro = micro_tokens(micro_at, slots, width)
    anywhere = pl.BlockSpec(memory_space=pl.ANY)
    held = [
        ((slots, width), f32),
        ((slots, width), bf16),
        ((slots, width), bf16),
        ((slots, units), bf16),
        ((slots, 2 * units), bf16),
    ]
    return pl.pallas_call(
        kernel,
        grid=(1,),
        in_specs=[SCALARS]
        + [single(piece.shape) for piece in branch_sum]
        + [micro, micro, row, row, row, anywhere, single((1, 2 * units)), anywhere],
        out_specs=[anywhere] * 5
        + [single((1, 2 * units)), row]
        + [single((slots // db_pieces, width))] * db_pieces
        + [single((slots // y_pieces, width))] * y_pieces,
        out_shape=[jax.ShapeDtypeStruct(*shape) for shape in held]
        + [
            jax.ShapeDtypeStruct((1, 2 * units), f32),
            jax.ShapeDtypeStruct((1, width), f32),
        ]
        + part_shapes(slots, width, db_pieces)
        + part_shapes(slots, width, y_pieces),
        scratch_shapes=[
            pltpu.VMEM((width, 2 * units), bf16),
            pltpu.VMEM((units, width), bf16),
        ]
        + [pltpu.VMEM(*shape) for shape in held]
        + [pltpu.VMEM((slots, width), bf16)] * 2
        + [pltpu.SemaphoreType.DMA((2, blocks)), pltpu.SemaphoreType.DMA((5,))],
        compiler_params=params(LARGE_MIB),
        cost_estimate=SHORT,
        name="feed_forward",
    )(
        scalars,
        *branch_sum,
        tokens,
        upstream,
        out_ratio,
        down_ratio,
        gain,
        merged,
        ratio,
        down_merged,
    )


def attend_back(
    scalars,
    db_sum,
    middle,
    upstream,
    branch_sum,
    gain,
    out_ratio,
    out_merged,
    projected,
    far_pack,
    cosine,
    sine_signed,
    micro_at,
):
    slots, width = middle.shape
    cols = projected.shape[1] // 3
    heads = cols // HEAD_DIM
    scale = 1.0 / math.sqrt(HEAD_DIM)
    pieces = len(db_sum)

    def kernel(*refs):
        n_ref, *refs = refs
        e_refs, s_refs, refs = refs[:pieces], refs[pieces : 2 * pieces], refs[2 * pieces :]
        h_ref, u_ref, g_ref, or_ref, w_ref, y_ref, f_ref, c_ref, sn_ref = refs[:9]
        dh_ref, d1_ref, co_ref, dy_ref, far_ref, do_ref = refs[9:]
        live = lax.broadcasted_iota(jnp.int32, (slots, 1), 0) < n_ref[0]
        h = h_ref[...]
        back = rms_back(h, rms_scale(h), g_ref[...], load_total(e_refs, n_ref[1]))
        dh = u_ref[...].astype(f32) + back
        dh_ref[...] = dh
        d1 = jnp.where(live, dh, 0.0)
        co_ref[...] = jnp.sum(d1 * load_total(s_refs, n_ref[1]), axis=0, keepdims=True)
        d1_ref[...] = (d1 * or_ref[...]).astype(bf16)
        do_ref[...] = contract_cols(d1_ref[...], w_ref[...]).astype(bf16)
        far_ok = f_ref[FAR_SLOTS : FAR_SLOTS + 1, :FAR_SLOTS].astype(f32)
        for i in range(heads):
            at = slice(i * HEAD_DIM, (i + 1) * HEAD_DIM)
            k_at = slice(cols + i * HEAD_DIM, cols + (i + 1) * HEAD_DIM)
            v_at = slice(2 * cols + i * HEAD_DIM, 2 * cols + (i + 1) * HEAD_DIM)
            q = y_ref[:, at]
            far_k = f_ref[:FAR_SLOTS, at]
            shares = head_shares(q, y_ref[:, k_at], far_k, far_ok)
            keys = jnp.concatenate([y_ref[:, k_at], far_k], axis=0)
            values = jnp.concatenate([y_ref[:, v_at], f_ref[:FAR_SLOTS, k_at]], axis=0)
            do = do_ref[:, at]
            share_grad = contract_cols(do, values)
            inner = jnp.sum(shares * share_grad, axis=-1, keepdims=True)
            score_grad = (shares * (share_grad - inner)).astype(bf16)
            dq = jnp.dot(score_grad, keys, preferred_element_type=f32) * scale
            dk = contract_rows(score_grad, q) * scale
            dv = contract_rows(shares.astype(bf16), do)
            dy_ref[:, at] = rotate_back(dq, c_ref[...], sn_ref[...])
            dy_ref[:, k_at] = dk[:slots]
            dy_ref[:, v_at] = dv[:slots]
            far_ref[:, at] = dk[slots:].astype(bf16)
            far_ref[:, k_at] = dv[slots:].astype(bf16)

    operands = (
        scalars,
        *db_sum,
        *branch_sum,
        middle,
        upstream,
        gain,
        out_ratio,
        out_merged,
        projected,
        far_pack,
        cosine,
        sine_signed,
    )
    shapes = [
        jax.ShapeDtypeStruct((slots, width), f32),
        jax.ShapeDtypeStruct((slots, width), bf16),
        jax.ShapeDtypeStruct((1, width), f32),
        jax.ShapeDtypeStruct((slots, 3 * cols), f32),
        jax.ShapeDtypeStruct((FAR_SLOTS, 2 * cols), bf16),
    ]
    return pl.pallas_call(
        kernel,
        grid=(1,),
        in_specs=[SCALARS]
        + [single((slots // pieces, width))] * (2 * pieces)
        + [
            single((slots, width)),
            micro_tokens(micro_at, slots, width),
            single((1, width)),
            single((1, width)),
            single(out_merged.shape),
            micro_rows(micro_at, slots, 3 * cols),
            single(far_pack.shape),
            micro_rows(micro_at, slots, HEAD_DIM),
            micro_rows(micro_at, slots, HEAD_DIM),
        ],
        out_specs=[single(shape.shape) for shape in shapes],
        out_shape=shapes,
        scratch_shapes=[pltpu.VMEM((slots, cols), bf16)],
        compiler_params=params(LARGE_MIB),
        cost_estimate=SHORT,
        name="attend_back",
    )(*operands)


def project_back(
    inner, dy, returned, projected, cosine, sine_signed, ratio, merged, pieces, micro_at
):
    slots, total = dy.shape
    cols = total // 3
    heads = cols // HEAD_DIM
    width = merged.shape[1]
    blocks = 4
    step = width // blocks

    def kernel(i_ref, d_ref, r_ref, y_ref, c_ref, sn_ref, s_ref, w_ref, o_ref, cs_ref, *da_refs):
        @pl.when(pl.program_id(0) == 0)
        def _():
            for i in range(3 * heads):
                at = slice(i * HEAD_DIM, (i + 1) * HEAD_DIM)
                d = d_ref[:, at]
                raw = y_ref[:, at].astype(f32)
                if i >= heads:
                    back = slice((i - heads) * HEAD_DIM, (i - heads + 1) * HEAD_DIM)
                    low = d[:FAR_SLOTS] + r_ref[:FAR_SLOTS, back].astype(f32)
                    d = jnp.concatenate([low, d[FAR_SLOTS:]], axis=0)
                if heads <= i < 2 * heads:
                    d = rotate_back(d, c_ref[...], sn_ref[...])
                if i < 2 * heads:
                    raw = rotate_back(raw, c_ref[...], sn_ref[...])
                cs_ref[:, at] = jnp.sum(d * raw, axis=0, keepdims=True)
                o_ref[:, at] = (d * s_ref[:, at]).astype(bf16)

        da = 0.0
        for g in range(3):
            da = da + contract_cols(o_ref[:, g * cols : (g + 1) * cols], w_ref[g])
        store_part(da.astype(bf16), da_refs, i_ref[0])

    return pl.pallas_call(
        kernel,
        grid=(blocks,),
        in_specs=[
            SCALARS,
            single((slots, total)),
            single(returned.shape),
            micro_rows(micro_at, slots, total),
            micro_rows(micro_at, slots, HEAD_DIM),
            micro_rows(micro_at, slots, HEAD_DIM),
            single((1, total)),
            pl.BlockSpec((3, step, cols), lambda i: (0, i, 0)),
        ],
        out_specs=[
            whole_block((slots, total)),
            whole_block((1, total)),
        ]
        + [pl.BlockSpec((slots // pieces, step), lambda i: (0, i))] * pieces,
        out_shape=[
            jax.ShapeDtypeStruct((slots, total), bf16),
            jax.ShapeDtypeStruct((1, total), f32),
        ]
        + part_shapes(slots, width, pieces),
        compiler_params=params(LARGE_MIB),
        cost_estimate=SHORT,
        name="project_back",
    )(inner, dy, returned, projected, cosine, sine_signed, ratio, merged)


LINE_PAIRS = [(0, 1), (1, 0), (2, 3), (3, 2)]
LINE_ACROSS = [(0, 3), (3, 0), (1, 2), (2, 1)]


def tensor_sum(parts, beside=None, first=()):
    if len(parts) == 1:
        return [lax.psum(parts[0], "tensor")], None
    keep, send = parts
    received = lax.ppermute(send, "tensor", LINE_PAIRS)
    if first:
        received = after(received, *first)
    pair = keep + received
    across = lax.ppermute(pair, "tensor", LINE_ACROSS)
    done = None
    if beside is not None:
        done = beside(pair)
        across = after(across, *done)
    total = pair + across
    return [total, lax.ppermute(total, "tensor", LINE_PAIRS)], done


def line_total(value):
    total = value
    for shift in (1, 2, 3):
        pairs = [(i, (i + shift) % 4) for i in range(4)]
        total = total + lax.ppermute(value, "tensor", pairs)
    return total


def dp_swap(value, hop):
    return lax.ppermute(value, "dp", [(i, i ^ hop) for i in range(8)])


def dp_share(value, line_rows):
    me = lax.axis_index("dp")
    half = value.shape[1] // 2
    quarter = half // 4
    upper = (me & 1) != 0
    low, high = value[:, :half], value[:, half:]
    value = jnp.where(upper, high, low) + dp_swap(jnp.where(upper, low, high), 1)
    chip = me // 2

    def columns(index):
        return lax.dynamic_slice_in_dim(value, index * quarter, quarter, 1)

    kept = columns(chip).astype(f32)
    for hop in (1, 2, 3):
        kept = kept + dp_swap(columns(chip ^ hop), 2 * hop)
    line = kept[:line_rows].astype(bf16)
    total = line.astype(f32)
    for shift in (1, 2, 3):
        total = total + lax.ppermute(line, "tensor", [(i, (i + shift) % 4) for i in range(4)])
    return jnp.concatenate([total, kept[line_rows:]], axis=0).astype(bf16)


def dp_gather(mine):
    me = lax.axis_index("dp")
    upper = (me & 1) != 0
    chip = me // 2
    quarters = [mine] + [dp_swap(mine, 2 * hop) for hop in (1, 2, 3)]
    value = jnp.concatenate([lax.select_n(chip ^ q, *quarters) for q in range(4)], axis=1)
    other = dp_swap(value, 1)
    value = jnp.concatenate(
        [jnp.where(upper, other, value), jnp.where(upper, value, other)], axis=1
    )
    return value.astype(f32)


def pair_exchange(pack, distance, sibling_distance):
    held = [pack] + [dp_swap(pack, hop) for hop in (2, 4, 6)]

    def pick(index):
        return lax.select_n(index // 2, *held)

    across = dp_swap(pick(sibling_distance & 6), 1)
    return jnp.where(distance % 2 == 1, across, pick(distance & 6)), held


def adapter_in(seen_inputs, sent_grads, merged, tall, wide, share, rank):
    micros = len(sent_grads)
    slots, depth = sent_grads[0].shape[0], seen_inputs[0].shape[1]
    blocks, _, cols = merged.shape
    shared = seen_inputs[0].shape[0] != slots
    if shared:
        seen_inputs = seen_inputs * micros
    ranks = tall.shape[0]
    groups = ranks // rank
    sides = 1 if blocks == groups else groups
    part = cols // sides
    scale = ADAPTER_NUMER / ADAPTER_RANK

    def kernel(*refs):
        x_refs, d_refs, refs = refs[:micros], refs[micros : 2 * micros], refs[2 * micros :]
        v_ref, t_ref, w_ref, s_ref, out_ref, *right_refs = refs[: 5 + sides]
        seen_ref, sent_ref, left_ref, all_ref = refs[5 + sides :]
        at = pl.program_id(0)

        @pl.when(at == 0)
        def _():
            left_ref[...] = jnp.zeros_like(left_ref)
            sent_ref[...] = jnp.zeros_like(sent_ref)
            for m in range(micros):
                seen_ref[m] = contract_cols(x_refs[m][...], t_ref[...]).astype(bf16)

        share = s_ref[...]
        wide = w_ref[...]
        right = -jnp.dot(t_ref[...], v_ref[...], preferred_element_type=f32) * share
        left = -contract_cols((wide * share).astype(bf16), v_ref[...])
        for m in range(micros):
            right = right + contract_rows(seen_ref[m], d_refs[m][...])
            sent_ref[m] += contract_cols(d_refs[m][...], wide.astype(bf16))
        if sides == 1:
            all_ref[...] = scale * right
            mine = pl.ds(pl.multiple_of(at * rank, rank), rank)
            right_refs[0][...] = all_ref[mine, :].astype(bf16)
        else:
            for g in range(sides):
                mine = right[g * rank : (g + 1) * rank, g * part : (g + 1) * part]
                right_refs[g][...] = (scale * mine).astype(bf16)
        left_ref[...] += left

        @pl.when(at == blocks - 1)
        def _():
            total = left_ref[...]
            for m in range(micros):
                total = total + contract_rows(sent_ref[m].astype(bf16), x_refs[m][...])
            out_ref[...] = (scale * total).astype(bf16)

    return pl.pallas_call(
        kernel,
        grid=(blocks,),
        in_specs=[micro_rows(m if shared else 0, slots, depth) for m in range(micros)]
        + [pl.BlockSpec((slots, cols), lambda i: (0, i))] * micros
        + [
            pl.BlockSpec((None, depth, cols), lambda i: (i, 0, 0)),
            single((ranks, depth)),
            pl.BlockSpec((ranks, cols), lambda i: (0, i)),
            pl.BlockSpec((1, cols), lambda i: (0, i)),
        ],
        out_specs=[whole_block((ranks, depth))]
        + [pl.BlockSpec((rank, part), lambda i: (0, i))] * sides,
        out_shape=[jax.ShapeDtypeStruct((ranks, depth), bf16)]
        + [jax.ShapeDtypeStruct((rank, blocks * part), bf16)] * sides,
        scratch_shapes=[
            pltpu.VMEM((micros, slots, ranks), bf16),
            pltpu.VMEM((micros, slots, ranks), f32),
            pltpu.VMEM((ranks, depth), f32),
            pltpu.VMEM((ranks, cols), f32),
        ],
        compiler_params=params(LARGE_MIB),
        cost_estimate=SHORT,
        name="adapter_in",
    )(*seen_inputs, *sent_grads, merged, tall, wide, share)


def adapter_out(seen_inputs, sent_grads, merged, first_t, second, share):
    micros = len(seen_inputs)
    slots, cols = sent_grads[0].shape
    depth = merged.shape[0]
    block = min(depth, UNIT_BLOCK)
    blocks = depth // block
    rank = second.shape[0]
    scale = ADAPTER_NUMER / ADAPTER_RANK

    def kernel(*refs):
        x_refs, d_refs, refs = refs[:micros], refs[micros : 2 * micros], refs[2 * micros :]
        v_ref, a_ref, b_ref, s_ref, left_ref, out_ref, seen_ref, sent_ref, right_ref = refs
        at = pl.program_id(0)
        second = b_ref[...]

        @pl.when(at == 0)
        def _():
            right_ref[...] = jnp.zeros_like(right_ref)
            seen_ref[...] = jnp.zeros_like(seen_ref)
            for m in range(micros):
                sent_ref[m] = contract_cols(d_refs[m][...], second.astype(bf16)).astype(bf16)

        first = a_ref[...].astype(bf16)
        left = -contract_cols((second * s_ref[...]).astype(bf16), v_ref[...])
        for m in range(micros):
            left = left + contract_rows(sent_ref[m], x_refs[m][...])
            seen_ref[m] += contract_cols(x_refs[m][...], first)
        left_ref[...] = (scale * left).astype(bf16)
        right_ref[...] += -jnp.dot(first, v_ref[...], preferred_element_type=f32) * s_ref[...]

        @pl.when(at == blocks - 1)
        def _():
            total = right_ref[...]
            for m in range(micros):
                total = total + contract_rows(seen_ref[m].astype(bf16), d_refs[m][...])
            out_ref[...] = (scale * total).astype(bf16)

    return pl.pallas_call(
        kernel,
        grid=(blocks,),
        in_specs=[pl.BlockSpec((slots, block), lambda i: (0, i))] * micros
        + [single((slots, cols))] * micros
        + [
            pl.BlockSpec((block, cols), lambda i: (i, 0)),
            pl.BlockSpec((rank, block), lambda i: (0, i)),
            single((rank, cols)),
            single((1, cols)),
        ],
        out_specs=[pl.BlockSpec((rank, block), lambda i: (0, i)), whole_block((rank, cols))],
        out_shape=[
            jax.ShapeDtypeStruct((rank, depth), bf16),
            jax.ShapeDtypeStruct((rank, cols), bf16),
        ],
        scratch_shapes=[
            pltpu.VMEM((micros, slots, rank), f32),
            pltpu.VMEM((micros, slots, rank), bf16),
            pltpu.VMEM((rank, cols), f32),
        ],
        compiler_params=params(LARGE_MIB),
        cost_estimate=SHORT,
        name="adapter_out",
    )(*seen_inputs, *sent_grads, merged, first_t, second, share)


def finish_input(scalars, total, tokens, middle_grad, gain, micro_at, micros, earlier):
    slots, width = middle_grad.shape
    pieces = len(total)

    def kernel(*refs):
        i_ref, *refs = refs
        x_ref, d_ref, g_ref = refs[pieces : pieces + 3]
        x = x_ref[...].astype(f32)
        back = rms_back(x, rms_scale(x), g_ref[...], load_total(refs[:pieces], i_ref[1]))
        refs[-1][...] = (d_ref[...] + back).astype(bf16)

    operands = [scalars, *total, tokens, middle_grad, gain]
    specs = [SCALARS] + [single(piece.shape) for piece in total]
    specs += [micro_tokens(micro_at, slots, width), single((slots, width)), single((1, width))]
    return write_micro(kernel, operands, specs, slots, width, micro_at, micros, earlier)


def finish_output(scalars, total, middle, ratio, micro_at, micros, earlier):
    slots, width = middle.shape
    pieces = len(total)

    def kernel(*refs):
        n_ref, *refs = refs
        m_ref, r_ref = refs[pieces : pieces + 2]
        live = lax.broadcasted_iota(jnp.int32, (slots, 1), 0) < n_ref[0]
        branch = load_total(refs[:pieces], n_ref[1]) * r_ref[...]
        refs[-1][...] = (m_ref[...] + jnp.where(live, branch, 0.0)).astype(bf16)

    operands = [scalars, *total, middle, ratio]
    specs = [SCALARS] + [single(operand.shape) for operand in operands[1:]]
    return write_micro(kernel, operands, specs, slots, width, micro_at, micros, earlier)


def write_micro(kernel, operands, specs, slots, width, micro_at, micros, earlier):
    aliases = {}
    if earlier is not None:
        aliases = {len(operands): 0}
        operands = operands + [earlier]
        specs = specs + [pl.BlockSpec(memory_space=pl.ANY)]
    return pl.pallas_call(
        kernel,
        grid=(1,),
        in_specs=specs,
        out_specs=pl.BlockSpec((None, None, slots, width), lambda i: (micro_at, 0, 0, 0)),
        out_shape=jax.ShapeDtypeStruct((micros, 1, slots, width), bf16),
        input_output_aliases=aliases,
        compiler_params=params(16),
        cost_estimate=SHORT,
        name="finish",
    )(*operands)


def after(value, *others):
    return lax.optimization_barrier((value, *others))[0]


def from_blocks(array, groups, units):
    ranks, total = array.shape
    array = array.reshape(ranks, total // (groups * UNIT_BLOCK), groups, UNIT_BLOCK)
    return jnp.transpose(array, (2, 0, 1, 3)).reshape(groups, ranks, total // groups)[..., :units]


def diagonal(second):
    groups, rank, cols = second.shape
    rows = [
        jnp.pad(second[g], ((g * rank, (groups - 1 - g) * rank), (0, 0))) for g in range(groups)
    ]
    return jnp.stack(rows)


def fast_device(
    inputs,
    lengths,
    prompt_mask,
    partner,
    positions,
    attn_gain,
    mlp_gain,
    attention_input_frozen,
    attention_input_first,
    attention_input_second,
    attention_input_magnitude,
    attention_output_frozen,
    attention_output_first,
    attention_output_second,
    attention_output_magnitude,
    feedforward_input_frozen,
    feedforward_input_first,
    feedforward_input_second,
    feedforward_input_magnitude,
    feedforward_output_frozen,
    feedforward_output_first,
    feedforward_output_second,
    feedforward_output_magnitude,
    grad_out,
):
    micros, _, slots, width = inputs.shape
    cols = attention_input_frozen.shape[2]
    units = feedforward_input_frozen.shape[2]
    rank = attention_output_second.shape[0]
    attn_row = attn_gain.astype(f32)[None]
    mlp_row = mlp_gain.astype(f32)[None]
    qkv_first_t = jnp.swapaxes(attention_input_first, 1, 2)
    gate_first_t = jnp.swapaxes(feedforward_input_first, 1, 2)
    out_first_t = attention_output_first.T
    down_first_t = feedforward_output_first.T
    out_magnitude = attention_output_magnitude[None]
    down_magnitude = feedforward_output_magnitude[None]

    me = lax.axis_index("dp")
    distance = partner[:, 0] ^ me
    sibling_distance = lax.ppermute(distance, "dp", [(i, i ^ 1) for i in range(8)])

    indices = jnp.arange(HEAD_DIM // 2, dtype=f32)
    inverse = rope_base ** (-2.0 * indices / HEAD_DIM)
    angles = positions.reshape(micros * slots).astype(f32)[:, None] * inverse[None, :]
    cosine, sine = jnp.cos(angles), jnp.sin(angles)
    cosine = jnp.concatenate([cosine, cosine], axis=1)
    sine_signed = jnp.concatenate([-sine, sine], axis=1)
    tokens = inputs.reshape(micros * slots, width)
    qkv_magnitude = attention_input_magnitude.reshape(1, -1)
    normed, qkv_merged, qkv_square, projected, *packs = merge_project(
        tokens,
        attn_row,
        jnp.swapaxes(attention_input_frozen, 0, 1),
        qkv_first_t,
        attention_input_second,
        qkv_magnitude,
        cosine,
        sine_signed,
        prompt_mask[:, 0, :FAR_SLOTS].astype(f32),
        slots,
    )
    qkv_inverse = lax.rsqrt(qkv_square)
    qkv_ratio = qkv_magnitude * qkv_inverse

    far_packs, held = [], []
    for m in range(micros):
        pack = after(packs[m], *held)
        far_pack, held = pair_exchange(pack, distance[m], sibling_distance[m])
        far_packs.append(far_pack)

    out_merged, out_square = merge_out(
        attention_output_frozen, out_first_t, after(attention_output_second, packs[0])
    )
    down_merged, down_square = merge_out(
        feedforward_output_frozen, down_first_t, after(feedforward_output_second, packs[0])
    )
    line_at = lax.axis_index("tensor")
    inner = ((line_at == 1) | (line_at == 2)).astype(jnp.int32)[None]
    scalars = [jnp.concatenate([lengths[m], inner]) for m in range(micros)]

    pieces = (2, 1)
    attended, parts = [], []
    turn = after(inner, down_square)
    for m in range(micros):
        seen, *part = attend(turn, projected, far_packs[m], out_merged, pieces[m], m, slots)
        turn = after(inner, seen)
        attended.append(seen)
        parts.append(part)
    squares = jnp.concatenate([out_square, down_square], axis=0)
    squares = line_total(after(squares, attended[1]))
    out_inverse, down_inverse = lax.rsqrt(squares[:1]), lax.rsqrt(squares[1:])
    out_ratio = out_magnitude * out_inverse
    down_ratio = down_magnitude * down_inverse
    gate_rank = 2 * rank

    def merge_gate(pair):
        return merge_in(
            feedforward_input_frozen,
            gate_first_t,
            after(feedforward_input_second, attended[1], pair),
            feedforward_input_magnitude,
        )

    first_sum, found = tensor_sum(parts[0], merge_gate)
    gate_merged, gate_ratio, gate_inverse, gate_wide = found
    branch_sums = [first_sum, tensor_sum(parts[1])[0]]

    middles, normed_mlp, hiddens, gate_grads, gate_inner = [], [], [], [], 0.0
    db_parts, down_parts, down_grads, down_inner = [], [], [], 0.0
    turn = scalars[0]
    for m in range(micros):
        middle, b, d2, hidden, dgu, c_gate, c_down, *sums = feed_forward(
            turn,
            branch_sums[m],
            inputs,
            grad_out,
            out_ratio,
            down_ratio,
            mlp_row,
            gate_merged,
            gate_ratio,
            down_merged,
            m,
            pieces[m],
            1 + m,
        )
        db, y = sums[: pieces[m]], sums[pieces[m] :]
        turn = after(scalars[1], c_down)
        middles.append(middle)
        normed_mlp.append(b)
        hiddens.append(hidden)
        gate_grads.append(dgu)
        gate_inner = gate_inner + c_gate
        down_inner = down_inner + c_down
        down_grads.append(d2)
        db_parts.append(db)
        down_parts.append(y)
    gate_tall = gate_first_t.reshape(gate_rank, width).astype(bf16)

    def adapters_feed_forward(pair):
        inner_now, down_now = after(gate_inner, pair), after(down_inner, pair)
        down_now = line_total(down_now)
        in_found = adapter_in(
            normed_mlp,
            gate_grads,
            gate_merged,
            gate_tall,
            gate_wide,
            inner_now * gate_ratio * gate_inverse * gate_inverse,
            rank,
        )
        out_found = adapter_out(
            hiddens,
            down_grads,
            down_merged,
            jnp.pad(down_first_t, ((0, 0), (0, down_merged.shape[0] - units))),
            feedforward_output_second,
            down_now * down_ratio * down_inverse * down_inverse,
        )
        return [*in_found, *out_found, down_now]

    first_sum, found = tensor_sum(db_parts[0], adapters_feed_forward, [down_inner])
    gate_left, gate_right, up_right, down_left, down_right, down_inner = found
    db_sums = [first_sum, tensor_sum(db_parts[1])[0]]
    gate_mag = from_blocks(gate_inner * gate_inverse, 2, units)[:, 0]
    down_mag = down_inner * down_inverse
    down_parts[0] = [after(down_parts[0][0], db_sums[1][0])]
    down_sums = [tensor_sum(part)[0] for part in down_parts]

    middle_grads, out_grads, out_inner, qkv_grads, qkv_inner, da_parts = [], [], 0.0, [], 0.0, []
    exchanged = []
    turn = scalars[0]
    for m in range(micros):
        dh, d1, c_out, dy, far_grad = attend_back(
            turn,
            db_sums[m],
            middles[m],
            grad_out,
            branch_sums[m],
            mlp_row,
            out_ratio,
            out_merged,
            projected,
            far_packs[m],
            cosine,
            sine_signed,
            m,
        )
        turn = after(scalars[1], c_out)
        middle_grads.append(dh)
        out_grads.append(d1)
        out_inner = out_inner + c_out
        returned, _ = pair_exchange(far_grad, distance[m], sibling_distance[m])
        exchanged.append((dy, returned))
    turn = inner
    for m in range(micros):
        dy, returned = exchanged[m]
        dqkv, c_qkv, *da = project_back(
            turn,
            dy,
            returned,
            projected,
            cosine,
            sine_signed,
            qkv_ratio,
            qkv_merged,
            2 - m,
            m,
        )
        turn = after(inner, c_qkv)
        qkv_grads.append(dqkv)
        qkv_inner = qkv_inner + c_qkv
        da_parts.append(da)
    def adapters_attention(pair):
        out_now, qkv_now = after(out_inner, pair), after(qkv_inner, pair) / qkv_ratio
        out_found = adapter_out(
            attended,
            out_grads,
            out_merged,
            out_first_t,
            attention_output_second,
            out_now * out_ratio * out_inverse * out_inverse,
        )
        in_found = adapter_in(
            [normed],
            qkv_grads,
            qkv_merged,
            qkv_first_t.reshape(3 * rank, width).astype(bf16),
            jnp.concatenate(list(diagonal(attention_input_second)), axis=1),
            qkv_now * qkv_ratio * qkv_inverse * qkv_inverse,
            rank,
        )
        return [*out_found, *in_found, qkv_now]

    found = adapters_attention(qkv_inner)
    out_left, out_right, qkv_left, qkv_right, qkv_inner = found
    low_units = [piece[:, :units] for piece in (gate_right, up_right, down_left)]
    magnitudes = [gate_mag, down_mag, qkv_inner * qkv_inverse, out_inner * out_inverse]

    def wide(piece):
        return jnp.pad(piece.astype(bf16), ((0, 0), (0, width - piece.shape[1])))

    magnitudes = jnp.concatenate([wide(piece) for piece in magnitudes], axis=0)
    magnitudes = jnp.pad(magnitudes, ((0, rank - magnitudes.shape[0]), (0, 0)))
    pieces = [gate_left, down_right, qkv_left, out_right]
    line_rows = 7 * rank
    pieces += [wide(piece) for piece in low_units]
    pieces += [jnp.concatenate([qkv_right, out_left], axis=1), magnitudes]
    share = dp_share(jnp.concatenate(pieces, axis=0), line_rows)
    da_last = after(da_parts[1][0], *down_sums[0])
    da_sums = [tensor_sum(da_parts[0])[0], tensor_sum([da_last])[0]]
    totals = dp_gather(after(share, da_sums[0][1], da_sums[1][0]))
    found, at = [], 0
    for piece in pieces:
        found.append(totals[at : at + piece.shape[0]])
        at += piece.shape[0]
    gate_left, down_right, qkv_left, out_right, gate_right, up_right, down_left, rights, mags = found
    gate_left = gate_left.reshape(2, rank, width)
    qkv_left = qkv_left.reshape(3, rank, width)
    gate_right = jnp.stack([gate_right[:, :units], up_right[:, :units]])
    down_left = down_left[:, :units]
    qkv_right = jnp.stack([rights[:, g * cols : (g + 1) * cols] for g in range(3)])
    out_left = rights[:, 3 * cols :]
    gate_mag, down_mag, out_mag = mags[:2, :units], mags[2], mags[4]
    qkv_mag = mags[3, : 3 * cols].reshape(3, cols)

    layer_out, layer_grad = None, None
    for m in range(micros):
        layer_out = finish_output(
            scalars[m], down_sums[m], middles[m], down_ratio, m, micros, layer_out
        )
    for m in range(micros):
        layer_grad = finish_input(
            scalars[m], da_sums[m], inputs, middle_grads[m], attn_row, m, micros, layer_grad
        )
    return (
        layer_out,
        layer_grad,
        jnp.swapaxes(qkv_left, 1, 2),
        qkv_right,
        qkv_mag,
        out_left.T,
        out_right,
        out_mag,
        jnp.swapaxes(gate_left, 1, 2),
        gate_right,
        gate_mag,
        down_left.T,
        down_right,
        down_mag,
    )


def solution(mesh):
    in_specs = (
        P(None, "dp", None, None),
        P(None, "dp"),
        P(None, "dp", None),
        P(None, "dp"),
        P(None, "dp", None),
        P(),
        P(),
        P(None, None, "tensor"),
        P(),
        P(None, None, "tensor"),
        P(None, "tensor"),
        P("tensor", None),
        P("tensor", None),
        P(),
        P(),
        P(None, None, "tensor"),
        P(),
        P(None, None, "tensor"),
        P(None, "tensor"),
        P("tensor", None),
        P("tensor", None),
        P(),
        P(),
        P(None, "dp", None, None),
    )
    out_specs = (
        P(None, "dp", None, None),
        P(None, "dp", None, None),
        P(),
        P(None, None, "tensor"),
        P(None, "tensor"),
        P("tensor", None),
        P(),
        P(),
        P(),
        P(None, None, "tensor"),
        P(None, "tensor"),
        P("tensor", None),
        P(),
        P(),
    )
    device_step = fast_device if fits_fast(mesh) else general_device
    return jax.shard_map(
        device_step, mesh=mesh, in_specs=in_specs, out_specs=out_specs, check_vma=False
    )
```

```python
import math

import jax
import jax.numpy as jnp
from jax import lax
from jax.experimental import pallas as pl
from jax.experimental.pallas import tpu as pltpu
from jax.sharding import PartitionSpec as P

HEAD_DIM = 128
ADAPTER_RANK = 16
ADAPTER_NUMER = 32


epsilon = 1e-05
rope_base = 10000.0
highest_precision = lax.Precision.HIGHEST
masked_score = -1e30


def rms_scale(values):
    return lax.rsqrt(jnp.mean(values * values, axis=-1, keepdims=True) + epsilon)


def rms_back(values, scale_rows, gain_row, gradient):
    scaled_update = gradient * gain_row
    normal = values * scale_rows
    return scale_rows * (
        scaled_update - normal * jnp.mean(scaled_update * normal, axis=-1, keepdims=True)
    )


def turn_half(values):
    middle = values.shape[-1] // 2
    return jnp.concatenate([-values[..., middle:], values[..., :middle]], axis=-1)


def rope_tables(positions, head_size):
    indices = jnp.arange(head_size // 2, dtype=jnp.float32)
    inverse = rope_base ** (-2.0 * indices / head_size)
    angles = positions.astype(jnp.float32)[:, None] * inverse[None, :]
    angles = jnp.concatenate([angles, angles], axis=-1)
    return (jnp.cos(angles)[:, None, :], jnp.sin(angles)[:, None, :])


def contract_rows(left_factor, right_factor):
    return lax.dot_general(
        left_factor, right_factor, (((0,), (0,)), ((), ())), preferred_element_type=jnp.float32
    )


def contract_cols(left_factor, right_factor):
    return lax.dot_general(
        left_factor, right_factor, (((1,), (1,)), ((), ())), preferred_element_type=jnp.float32
    )


def pick_partner(partner_row, far_slots, current, pieces):
    piece_rows = pieces[0].shape[0]
    wanted = partner_row * far_slots + jnp.arange(far_slots, dtype=jnp.int32)
    inside = (wanted >= 0) & (wanted < piece_rows)
    clipped = jnp.clip(wanted, 0, piece_rows - 1)
    packed = jnp.where(inside[:, None], jnp.take(pieces[0], clipped, axis=0), current[0])
    flags = jnp.where(inside, jnp.take(pieces[1], clipped, axis=0), current[1])
    return (packed, flags)


def place_far(partner_row, far_grad, row_count):
    far_slots = far_grad.shape[0]
    owners = jnp.arange(row_count // far_slots, dtype=jnp.int32)
    term = jnp.where((owners == partner_row)[:, None, None], far_grad[None], 0.0)
    return term.reshape(row_count, far_grad.shape[1])


def column_gradient_list(
    weight_total,
    merged_matrix,
    column_norm_value,
    column_magnitude,
    left_factor,
    right_factor,
    adapter_scale,
):
    inner = jnp.sum(weight_total * merged_matrix, axis=0)
    merged_matrix_gradient = (
        column_magnitude
        / column_norm_value
        * (weight_total - inner / (column_norm_value * column_norm_value) * merged_matrix)
    )
    left_factor_gradient = adapter_scale * jnp.einsum(
        "ypz,pvz->pyv", merged_matrix_gradient, right_factor, precision=highest_precision
    )
    right_factor_gradient = adapter_scale * jnp.einsum(
        "emn,mez->enz", left_factor, merged_matrix_gradient, precision=highest_precision
    )
    return (left_factor_gradient, right_factor_gradient, inner / column_norm_value)


def row_pieces_list(
    weight_total,
    merged_matrix,
    column_norm_value,
    column_magnitude,
    left_factor,
    right_factor,
    adapter_scale,
):
    scaled_update = weight_total * (column_magnitude / column_norm_value)
    inner = jnp.sum(weight_total * merged_matrix, axis=0)
    left_factor_part = adapter_scale * jnp.dot(
        scaled_update, right_factor.T, precision=highest_precision
    )
    right_factor_part = adapter_scale * jnp.dot(
        left_factor.T, scaled_update, precision=highest_precision
    )
    return (inner, left_factor_part, right_factor_part)


def general_device(
    inputs,
    lengths,
    prompt_mask,
    partner,
    positions,
    attn_gain,
    mlp_gain,
    attention_input_frozen,
    attention_input_first,
    attention_input_second,
    attention_input_magnitude,
    attention_output_frozen,
    attention_output_first,
    attention_output_second,
    attention_output_magnitude,
    feedforward_input_frozen,
    feedforward_input_first,
    feedforward_input_second,
    feedforward_input_magnitude,
    feedforward_output_frozen,
    feedforward_output_first,
    feedforward_output_second,
    feedforward_output_magnitude,
    grad_out,
):
    micro_count = inputs.shape[0]
    slot_count = inputs.shape[2]
    model_width = inputs.shape[3]
    head_cols = attention_input_frozen.shape[2]
    head_count = head_cols // HEAD_DIM
    unit_count = feedforward_input_frozen.shape[2]
    adapter_scale = ADAPTER_NUMER / ADAPTER_RANK
    score_scale = 1.0 / math.sqrt(HEAD_DIM)
    block_rows = min(512, slot_count)
    block_count = slot_count // block_rows
    attn_scale = attn_gain.astype(jnp.float32)
    mlp_scale = mlp_gain.astype(jnp.float32)
    query_key_value_merged = attention_input_frozen.astype(
        jnp.float32
    ) + adapter_scale * jnp.einsum(
        "kdr,kro->dko", attention_input_first, attention_input_second, precision=highest_precision
    )
    query_key_value_norm = jnp.sqrt(
        jnp.sum(query_key_value_merged * query_key_value_merged, axis=0)
    )
    qkv_weight = (
        (query_key_value_merged * (attention_input_magnitude / query_key_value_norm))
        .astype(jnp.bfloat16)
        .reshape(model_width, 3 * head_cols)
    )
    gate_merged_weight = feedforward_input_frozen.astype(jnp.float32) + adapter_scale * jnp.einsum(
        "kdr,kro->dko",
        feedforward_input_first,
        feedforward_input_second,
        precision=highest_precision,
    )
    gate_column_norm = jnp.sqrt(jnp.sum(gate_merged_weight * gate_merged_weight, axis=0))
    gate_up_weight = (
        (gate_merged_weight * (feedforward_input_magnitude / gate_column_norm))
        .astype(jnp.bfloat16)
        .reshape(model_width, 2 * unit_count)
    )
    output_merged_weight = attention_output_frozen.astype(jnp.float32) + adapter_scale * jnp.dot(
        attention_output_first, attention_output_second, precision=highest_precision
    )
    down_merged_weight = feedforward_output_frozen.astype(jnp.float32) + adapter_scale * jnp.dot(
        feedforward_output_first, feedforward_output_second, precision=highest_precision
    )
    out_square = jnp.sum(output_merged_weight * output_merged_weight, axis=0)
    down_square = jnp.sum(down_merged_weight * down_merged_weight, axis=0)
    output_cross_term = jnp.dot(
        attention_output_first.T, output_merged_weight, precision=highest_precision
    )
    down_cross_term = jnp.dot(
        feedforward_output_first.T, down_merged_weight, precision=highest_precision
    )
    out_square, down_square, output_cross_term, down_cross_term = (
        lax.psum(out_square.astype(jnp.bfloat16), "tensor").astype(jnp.float32),
        lax.psum(down_square.astype(jnp.bfloat16), "tensor").astype(jnp.float32),
        lax.psum(output_cross_term.astype(jnp.bfloat16), "tensor").astype(jnp.float32),
        lax.psum(down_cross_term.astype(jnp.bfloat16), "tensor").astype(jnp.float32),
    )
    output_column_norm = jnp.sqrt(out_square)
    down_column_norm = jnp.sqrt(down_square)
    out_weight = (output_merged_weight * (attention_output_magnitude / output_column_norm)).astype(
        jnp.bfloat16
    )
    down_weight = (down_merged_weight * (feedforward_output_magnitude / down_column_norm)).astype(
        jnp.bfloat16
    )
    grad_qkv = jnp.zeros((model_width, 3 * head_cols), jnp.float32)
    output_projection_gradient = jnp.zeros((head_cols, model_width), jnp.float32)
    grad_gate_up = jnp.zeros((model_width, 2 * unit_count), jnp.float32)
    down_projection_gradient = jnp.zeros((unit_count, model_width), jnp.float32)
    results = []
    input_grads = []
    for micro_at in range(micro_count):
        tokens = inputs[micro_at, 0].astype(jnp.float32)
        length_now = lengths[micro_at, 0]
        partner_row = partner[micro_at, 0]
        cosine, sine_tab = rope_tables(positions[micro_at, 0], HEAD_DIM)
        live_mask = (jnp.arange(slot_count) < length_now).astype(jnp.float32)[:, None]
        attn_rows = rms_scale(tokens)
        normed = (tokens * attn_rows * attn_scale).astype(jnp.bfloat16)
        projected = jnp.dot(normed, qkv_weight, preferred_element_type=jnp.float32).reshape(
            slot_count, 3, head_count, HEAD_DIM
        )
        queries = (projected[:, 0] * cosine + turn_half(projected[:, 0]) * sine_tab).astype(
            jnp.bfloat16
        )
        keys_rot = (projected[:, 1] * cosine + turn_half(projected[:, 1]) * sine_tab).astype(
            jnp.bfloat16
        )
        values_in = projected[:, 2].astype(jnp.bfloat16)
        own_pack = jnp.concatenate(
            [keys_rot.reshape(slot_count, head_cols), values_in.reshape(slot_count, head_cols)],
            axis=1,
        )
        own_flags = prompt_mask[micro_at, 0].astype(jnp.bfloat16)
        empty_pack = (
            jnp.zeros((slot_count, 2 * head_cols), jnp.bfloat16),
            jnp.zeros((slot_count,), jnp.bfloat16),
        )
        far_pack, far_flags = pick_partner(
            partner_row,
            slot_count,
            empty_pack,
            (
                lax.all_gather(own_pack, "dp", axis=0, tiled=True),
                lax.all_gather(own_flags, "dp", axis=0, tiled=True),
            ),
        )
        all_keys = jnp.concatenate(
            [keys_rot, far_pack[:, :head_cols].reshape(slot_count, head_count, HEAD_DIM)], axis=0
        )
        all_values = jnp.concatenate(
            [values_in, far_pack[:, head_cols:].reshape(slot_count, head_count, HEAD_DIM)], axis=0
        )
        far_ok = far_flags > 0

        def block_scores(queries_blk, first_row):
            raw = (
                jnp.einsum(
                    "ihd,jhd->hij", queries_blk, all_keys, preferred_element_type=jnp.float32
                )
                * score_scale
            )
            rows_at = first_row + jnp.arange(block_rows)[:, None]
            own_ok = jnp.arange(slot_count)[None, :] <= rows_at
            allowed = jnp.concatenate(
                [own_ok, jnp.broadcast_to(far_ok[None, :], (block_rows, slot_count))], axis=1
            )
            return jnp.where(allowed[None], raw, masked_score)

        def forward_block(block_at):
            first_row = block_at * block_rows
            scores = block_scores(queries, first_row)
            row_top = jnp.max(scores, axis=-1, keepdims=True)
            exponent = jnp.exp(scores - row_top)
            row_total = jnp.sum(exponent, axis=-1, keepdims=True)
            shares = (exponent / row_total).astype(jnp.bfloat16)
            attended_blk = jnp.einsum(
                "hij,jhd->ihd", shares, all_values, preferred_element_type=jnp.float32
            )
            return (
                attended_blk.reshape(block_rows, head_cols).astype(jnp.bfloat16),
                row_top,
                row_total,
            )

        attended, row_tops, row_totals = lax.map(
            forward_block, jnp.arange(block_count, dtype=jnp.int32)
        )
        attended = attended.reshape(slot_count, head_cols)
        branch = lax.psum(
            jnp.dot(attended, out_weight, preferred_element_type=jnp.float32).astype(jnp.bfloat16),
            "tensor",
        ).astype(jnp.float32)
        middle = tokens + live_mask * branch
        mlp_rows = rms_scale(middle)
        normed_mlp = (middle * mlp_rows * mlp_scale).astype(jnp.bfloat16)
        gate_up = jnp.dot(normed_mlp, gate_up_weight, preferred_element_type=jnp.float32)
        gate_pre = gate_up[:, :unit_count]
        up_pre = gate_up[:, unit_count:]
        gate_sigmoid = jax.nn.sigmoid(gate_pre)
        activated = gate_pre * gate_sigmoid
        hidden = (activated * up_pre).astype(jnp.bfloat16)
        branch_mlp = lax.psum(
            jnp.dot(hidden, down_weight, preferred_element_type=jnp.float32).astype(jnp.bfloat16),
            "tensor",
        ).astype(jnp.float32)
        results.append((middle + live_mask * branch_mlp).astype(jnp.bfloat16))
        upstream = grad_out[micro_at, 0].astype(jnp.float32)
        down_grad = (live_mask * upstream).astype(jnp.bfloat16)
        hidden_grad = contract_cols(down_grad, down_weight)
        down_projection_gradient = down_projection_gradient + contract_rows(hidden, down_grad)
        gate_grad = (
            hidden_grad * up_pre * gate_sigmoid * (1.0 + gate_pre * (1.0 - gate_sigmoid))
        ).astype(jnp.bfloat16)
        up_grad = (hidden_grad * activated).astype(jnp.bfloat16)
        gate_up_grad = jnp.concatenate([gate_grad, up_grad], axis=1)
        grad_gate_up = grad_gate_up + contract_rows(normed_mlp, gate_up_grad)
        mlp_in_grad = lax.psum(
            contract_cols(gate_up_grad, gate_up_weight).astype(jnp.bfloat16), "tensor"
        ).astype(jnp.float32)
        middle_grad = upstream + rms_back(middle, mlp_rows, mlp_scale, mlp_in_grad)
        attn_grad = (live_mask * middle_grad).astype(jnp.bfloat16)
        output_projection_gradient = output_projection_gradient + contract_rows(attended, attn_grad)
        attended_grad = (
            contract_cols(attn_grad, out_weight)
            .astype(jnp.bfloat16)
            .reshape(slot_count, head_count, HEAD_DIM)
        )

        def backward_block(carried, block_at):
            first_row = block_at * block_rows
            row_top = row_tops[block_at]
            row_total = row_totals[block_at]
            scores = block_scores(queries, first_row)
            shares = jnp.exp(scores - row_top) / row_total
            shares_low = shares.astype(jnp.bfloat16)
            share_grad = jnp.einsum(
                "ihd,jhd->hij", attended_grad, all_values, preferred_element_type=jnp.float32
            )
            inner = jnp.sum(shares * share_grad, axis=-1, keepdims=True)
            score_grad = (shares * (share_grad - inner)).astype(jnp.bfloat16)
            query_grad = (
                jnp.einsum("hij,jhd->ihd", score_grad, all_keys, preferred_element_type=jnp.float32)
                * score_scale
            )
            key_part = (
                jnp.einsum("hij,ihd->jhd", score_grad, queries, preferred_element_type=jnp.float32)
                * score_scale
            )
            value_part = jnp.einsum(
                "hij,ihd->jhd", shares_low, attended_grad, preferred_element_type=jnp.float32
            )
            query_grad, key_part, value_part = (query_grad, key_part, value_part)
            return ((carried[0] + key_part, carried[1] + value_part), query_grad)

        key_zero = jnp.zeros((slot_count + slot_count, head_count, HEAD_DIM), jnp.float32)
        (key_grad, value_grad), query_grads = lax.scan(
            backward_block, (key_zero, key_zero), jnp.arange(block_count, dtype=jnp.int32)
        )
        far_grad = jnp.concatenate(
            [
                key_grad[slot_count:].reshape(slot_count, head_cols),
                value_grad[slot_count:].reshape(slot_count, head_cols),
            ],
            axis=1,
        )
        far_low = far_grad.astype(jnp.bfloat16)
        returned = lax.psum_scatter(
            place_far(
                partner_row, far_low.astype(jnp.float32), slot_count * lax.axis_size("dp")
            ).astype(jnp.bfloat16),
            "dp",
            scatter_dimension=0,
            tiled=True,
        ).astype(jnp.float32)
        key_total = key_grad[:slot_count] + returned[:, :head_cols].reshape(
            slot_count, head_count, HEAD_DIM
        )
        value_total = value_grad[:slot_count] + returned[:, head_cols:].reshape(
            slot_count, head_count, HEAD_DIM
        )
        query_total = query_grads.reshape(slot_count, head_count, HEAD_DIM)
        query_back = (query_total * cosine - turn_half(query_total * sine_tab)).astype(jnp.bfloat16)
        key_back = (key_total * cosine - turn_half(key_total * sine_tab)).astype(jnp.bfloat16)
        value_back = value_total.astype(jnp.bfloat16)
        qkv_grad = jnp.concatenate(
            [
                query_back.reshape(slot_count, head_cols),
                key_back.reshape(slot_count, head_cols),
                value_back.reshape(slot_count, head_cols),
            ],
            axis=1,
        )
        grad_qkv = grad_qkv + contract_rows(normed, qkv_grad)
        attn_in_grad = lax.psum(
            contract_cols(qkv_grad, qkv_weight).astype(jnp.bfloat16), "tensor"
        ).astype(jnp.float32)
        input_grads.append(
            (middle_grad + rms_back(tokens, attn_rows, attn_scale, attn_in_grad)).astype(
                jnp.bfloat16
            )
        )
    query_key_value_total = grad_qkv.reshape(model_width, 3, head_cols)
    gate_weight_total = grad_gate_up.reshape(model_width, 2, unit_count)
    qkv_left, qkv_right, qkv_mag = column_gradient_list(
        query_key_value_total,
        query_key_value_merged,
        query_key_value_norm,
        attention_input_magnitude,
        attention_input_first,
        attention_input_second,
        adapter_scale,
    )
    gate_left, gate_right, gate_mag = column_gradient_list(
        gate_weight_total,
        gate_merged_weight,
        gate_column_norm,
        feedforward_input_magnitude,
        feedforward_input_first,
        feedforward_input_second,
        adapter_scale,
    )
    out_inner, output_left_factor, output_right_factor = row_pieces_list(
        output_projection_gradient,
        output_merged_weight,
        output_column_norm,
        attention_output_magnitude,
        attention_output_first,
        attention_output_second,
        adapter_scale,
    )
    down_inner, down_left_factor, down_right_factor = row_pieces_list(
        down_projection_gradient,
        down_merged_weight,
        down_column_norm,
        feedforward_output_magnitude,
        feedforward_output_first,
        feedforward_output_second,
        adapter_scale,
    )
    qkv_left, gate_left, output_right_factor, down_right_factor, out_inner, down_inner = lax.psum(
        (qkv_left, gate_left, output_right_factor, down_right_factor, out_inner, down_inner),
        ("dp", "tensor"),
    )
    qkv_right, qkv_mag, gate_right, gate_mag, output_left_factor, down_left_factor = (
        lax.psum(qkv_right.astype(jnp.bfloat16), "dp").astype(jnp.float32),
        lax.psum(qkv_mag.astype(jnp.bfloat16), "dp").astype(jnp.float32),
        lax.psum(gate_right.astype(jnp.bfloat16), "dp").astype(jnp.float32),
        lax.psum(gate_mag.astype(jnp.bfloat16), "dp").astype(jnp.float32),
        lax.psum(output_left_factor.astype(jnp.bfloat16), "dp").astype(jnp.float32),
        lax.psum(down_left_factor.astype(jnp.bfloat16), "dp").astype(jnp.float32),
    )
    output_norm_factor = (
        attention_output_magnitude
        * out_inner
        / (output_column_norm * output_column_norm * output_column_norm)
    )
    down_norm_factor = (
        feedforward_output_magnitude
        * down_inner
        / (down_column_norm * down_column_norm * down_column_norm)
    )
    output_left_factor = output_left_factor - adapter_scale * jnp.dot(
        output_merged_weight * output_norm_factor,
        attention_output_second.T,
        precision=highest_precision,
    )
    down_left_factor = down_left_factor - adapter_scale * jnp.dot(
        down_merged_weight * down_norm_factor,
        feedforward_output_second.T,
        precision=highest_precision,
    )
    output_right_factor = (
        output_right_factor - adapter_scale * output_cross_term * output_norm_factor
    )
    down_right_factor = down_right_factor - adapter_scale * down_cross_term * down_norm_factor
    out_mag = out_inner / output_column_norm
    down_mag = down_inner / down_column_norm
    layer_out = jnp.stack(results)[:, None]
    layer_grad = jnp.stack(input_grads)[:, None]
    return (
        layer_out,
        layer_grad,
        qkv_left,
        qkv_right,
        qkv_mag,
        output_left_factor,
        output_right_factor,
        out_mag,
        gate_left,
        gate_right,
        gate_mag,
        down_left_factor,
        down_right_factor,
        down_mag,
    )


FAR_SLOTS = 128
LANES = 128
MIB = 1024 * 1024
f32 = jnp.float32
bf16 = jnp.bfloat16


def fits_fast(mesh):
    return mesh.shape["dp"] == 8 and mesh.shape["tensor"] == 4


def split_high_low(value):
    high = value.astype(bf16)
    return high, (value - high.astype(f32)).astype(bf16)


def adapter_product(first_t, second):
    a_high, a_low = split_high_low(first_t)
    b_high, b_low = split_high_low(second)
    left = jnp.concatenate([a_high, a_low, a_high], axis=0)
    right = jnp.concatenate([b_high, b_high, b_low], axis=0)
    return contract_rows(left, right)


def params(mib):
    return pltpu.CompilerParams(vmem_limit_bytes=mib * MIB)


def single(shape):
    zeros = (0,) * len(shape)
    return pl.BlockSpec(shape, lambda *_: zeros, pipeline_mode=pl.Buffered(1))


def micro_rows(micro_at, slots, width):
    return pl.BlockSpec((slots, width), lambda *_: (micro_at, 0), pipeline_mode=pl.Buffered(1))


def micro_tokens(micro_at, slots, width):
    return pl.BlockSpec(
        (None, None, slots, width),
        lambda *_: (micro_at, 0, 0, 0),
        pipeline_mode=pl.Buffered(1),
    )


SCALARS = pl.BlockSpec(memory_space=pltpu.SMEM)
SHORT = pl.CostEstimate(flops=1, bytes_accessed=1, transcendentals=0)


def whole_block(shape):
    zeros = (0,) * len(shape)
    return pl.BlockSpec(shape, lambda *_: zeros)


UNIT_BLOCK = 256
LARGE_MIB = 56


def padded(units):
    return -(-units // UNIT_BLOCK) * UNIT_BLOCK


def adapter_rows(second):
    high, low = split_high_low(second * (ADAPTER_NUMER / ADAPTER_RANK))
    return jnp.concatenate([high, high, low], axis=0)


def adapter_columns(first_t):
    high, low = split_high_low(first_t)
    return jnp.concatenate([high, low, high], axis=0)


def partial_squares(value):
    return jnp.sum((value * value).reshape(value.shape[0] // 8, 8, value.shape[1]), axis=0)


def merge_chunk(base, columns, rows):
    return base.astype(f32) + contract_rows(columns, rows)


def merge_in(frozen, first_t, second, magnitude):
    depth, groups, cols = frozen.shape
    rank = second.shape[1]
    blocks = padded(cols) // UNIT_BLOCK
    total = blocks * groups * UNIT_BLOCK
    row_block = 256
    steps = depth // row_block

    def kernel(w_ref, a_ref, b_ref, m_ref, v_ref, ratio_ref, inverse_ref, wide_ref, r_ref, sq_ref):
        at = pl.program_id(0)

        def pieces():
            for g in range(groups):
                for j in range(blocks):
                    count = min(UNIT_BLOCK, cols - j * UNIT_BLOCK)
                    start = (j * groups + g) * UNIT_BLOCK
                    yield g, j, slice(j * UNIT_BLOCK, j * UNIT_BLOCK + count), start, count

        @pl.when(at == 0)
        def _():
            sq_ref[...] = jnp.zeros_like(sq_ref)
            wide_ref[...] = jnp.zeros_like(wide_ref)
            for g in range(groups):
                r_ref[g] = adapter_rows(b_ref[g])
            for g, j, here, start, count in pieces():
                ranks = slice(g * rank, (g + 1) * rank)
                wide_ref[ranks, start : start + count] = b_ref[g, :, here]

        left = [adapter_columns(a_ref[g]) for g in range(groups)]
        for g, j, here, start, count in pieces():
            v = merge_chunk(w_ref[:, g, here], left[g], r_ref[g, :, here])
            at_g = g * UNIT_BLOCK
            v_ref[j, :, at_g : at_g + count] = v.astype(bf16)
            if count < UNIT_BLOCK:
                v_ref[j, :, at_g + count : at_g + UNIT_BLOCK] = jnp.zeros(
                    (row_block, UNIT_BLOCK - count), bf16
                )
            sq_ref[:, start : start + count] += partial_squares(v)

        @pl.when(at == steps - 1)
        def _():
            ratio_ref[...] = jnp.zeros_like(ratio_ref)
            inverse_ref[...] = jnp.zeros_like(inverse_ref)
            for g, j, here, start, count in pieces():
                there = slice(start, start + count)
                inverse = lax.rsqrt(jnp.sum(sq_ref[:, there], axis=0, keepdims=True))
                inverse_ref[:, there] = inverse
                ratio_ref[:, there] = m_ref[g : g + 1, here] * inverse

    return pl.pallas_call(
        kernel,
        grid=(steps,),
        in_specs=[
            pl.BlockSpec((row_block, groups, cols), lambda i: (i, 0, 0)),
            pl.BlockSpec((groups, rank, row_block), lambda i: (0, 0, i)),
            whole_block((groups, rank, cols)),
            whole_block((groups, cols)),
        ],
        out_specs=[
            pl.BlockSpec((blocks, row_block, groups * UNIT_BLOCK), lambda i: (0, i, 0)),
            whole_block((1, total)),
            whole_block((1, total)),
            whole_block((groups * rank, total)),
        ],
        out_shape=[
            jax.ShapeDtypeStruct((blocks, depth, groups * UNIT_BLOCK), bf16),
            jax.ShapeDtypeStruct((1, total), f32),
            jax.ShapeDtypeStruct((1, total), f32),
            jax.ShapeDtypeStruct((groups * rank, total), f32),
        ],
        scratch_shapes=[
            pltpu.VMEM((groups, 3 * rank, cols), bf16),
            pltpu.VMEM((8, total), f32),
        ],
        compiler_params=params(LARGE_MIB),
        cost_estimate=SHORT,
        name="merge_in",
    )(frozen, first_t, second, magnitude)


def merge_out(frozen, first_t, second):
    depth, cols = frozen.shape
    rank = second.shape[0]
    row_block = UNIT_BLOCK
    blocks = padded(depth) // row_block
    chunk = 512

    def kernel(w_ref, a_ref, b_ref, v_ref, total_ref, r_ref, sq_ref):
        at = pl.program_id(0)

        @pl.when(at == 0)
        def _():
            sq_ref[...] = jnp.zeros_like(sq_ref)
            r_ref[...] = adapter_rows(b_ref[...])

        left = adapter_columns(a_ref[...])
        within = at * row_block + lax.broadcasted_iota(jnp.int32, (row_block, 1), 0) < depth
        for j in range(cols // chunk):
            here = slice(j * chunk, (j + 1) * chunk)
            v = jnp.where(within, merge_chunk(w_ref[:, here], left, r_ref[:, here]), 0.0)
            v_ref[:, here] = v.astype(bf16)
            sq_ref[:, here] += partial_squares(v)

        @pl.when(at == blocks - 1)
        def _():
            total_ref[...] = jnp.sum(sq_ref[...], axis=0, keepdims=True)

    return pl.pallas_call(
        kernel,
        grid=(blocks,),
        in_specs=[
            pl.BlockSpec((row_block, cols), lambda i: (i, 0)),
            pl.BlockSpec((rank, row_block), lambda i: (0, i)),
            whole_block((rank, cols)),
        ],
        out_specs=[pl.BlockSpec((row_block, cols), lambda i: (i, 0)), whole_block((1, cols))],
        out_shape=[
            jax.ShapeDtypeStruct((blocks * row_block, cols), bf16),
            jax.ShapeDtypeStruct((1, cols), f32),
        ],
        scratch_shapes=[pltpu.VMEM((3 * rank, cols), bf16), pltpu.VMEM((8, cols), f32)],
        compiler_params=params(10),
        cost_estimate=SHORT,
        name="merge_out",
    )(frozen, first_t, second)


def rotate(values, cosine, sine_signed):
    return values * cosine + pltpu.roll(values, HEAD_DIM // 2, 1) * sine_signed


def rotate_back(values, cosine, sine_signed):
    return values * cosine - pltpu.roll(values, HEAD_DIM // 2, 1) * sine_signed


def merge_project(
    tokens, gain, frozen, first_t, second, magnitude, cosine, sine_signed, flags, slots
):
    count, width = tokens.shape
    cols = frozen.shape[2]
    rank = second.shape[1]
    heads = cols // HEAD_DIM
    chunk_rows, chunk_cols = 256, 256
    micros = count // slots

    def kernel(*refs):
        x_ref, g_ref, w_ref, a_ref, b_ref, m_ref, c_ref, n_ref, f_ref = refs[:9]
        o_ref, v_ref, sq_ref, y_ref, *pack_refs = refs[9:]
        part = pl.program_id(0)

        @pl.when(part == 0)
        def _():
            for m in range(micros):
                pack_refs[m][FAR_SLOTS:, :] = jnp.zeros((16, 2 * cols), bf16)
                pack_refs[m][FAR_SLOTS : FAR_SLOTS + 1, :FAR_SLOTS] = f_ref[m : m + 1].astype(bf16)
            for r in range(0, count, chunk_rows):
                x = x_ref[r : r + chunk_rows].astype(f32)
                o_ref[r : r + chunk_rows] = (x * rms_scale(x) * g_ref[...]).astype(bf16)

        right = adapter_rows(b_ref[...])
        for c in range(0, cols, chunk_cols):
            here = slice(c, c + chunk_cols)
            square = 0.0
            for r in range(0, width, chunk_rows):
                left = adapter_columns(a_ref[:, r : r + chunk_rows])
                v = merge_chunk(w_ref[r : r + chunk_rows, here], left, right[:, here])
                v_ref[r : r + chunk_rows, here] = v.astype(bf16)
                square = square + partial_squares(v)
            square = jnp.sum(square, axis=0, keepdims=True)
            sq_ref[:, here] = square
            ratio = m_ref[:, here] * lax.rsqrt(square)
            total = jnp.dot(o_ref[...], v_ref[:, here], preferred_element_type=f32) * ratio
            for h in range(0, chunk_cols, HEAD_DIM):
                turned = rotate(total[:, h : h + HEAD_DIM], c_ref[...], n_ref[...])
                y_ref[:, c + h : c + h + HEAD_DIM] = jnp.where(
                    part < 2, turned, total[:, h : h + HEAD_DIM]
                ).astype(bf16)

        for kept in (1, 2):

            @pl.when(part == kept)
            def _(first=(kept - 1) * cols):
                for m in range(micros):
                    rows = y_ref[m * slots : m * slots + FAR_SLOTS, :]
                    pack_refs[m][:FAR_SLOTS, first : first + cols] = rows

    return pl.pallas_call(
        kernel,
        grid=(3,),
        in_specs=[
            whole_block((count, width)),
            whole_block((1, width)),
            pl.BlockSpec((None, width, cols), lambda i: (i, 0, 0)),
            pl.BlockSpec((None, rank, width), lambda i: (i, 0, 0)),
            pl.BlockSpec((None, rank, cols), lambda i: (i, 0, 0)),
            pl.BlockSpec((1, cols), lambda i: (0, i)),
            whole_block((count, HEAD_DIM)),
            whole_block((count, HEAD_DIM)),
            whole_block(flags.shape),
        ],
        out_specs=[
            whole_block((count, width)),
            pl.BlockSpec((None, width, cols), lambda i: (i, 0, 0)),
            pl.BlockSpec((1, cols), lambda i: (0, i)),
            pl.BlockSpec((count, cols), lambda i: (0, i)),
        ]
        + [whole_block((FAR_SLOTS + 16, 2 * cols))] * micros,
        out_shape=[
            jax.ShapeDtypeStruct((count, width), bf16),
            jax.ShapeDtypeStruct((3, width, cols), bf16),
            jax.ShapeDtypeStruct((1, 3 * cols), f32),
            jax.ShapeDtypeStruct((count, 3 * cols), bf16),
        ]
        + [jax.ShapeDtypeStruct((FAR_SLOTS + 16, 2 * cols), bf16)] * micros,
        compiler_params=params(LARGE_MIB),
        cost_estimate=SHORT,
        name="merge_project",
    )(tokens, gain, frozen, first_t, second, magnitude, cosine, sine_signed, flags)


def head_shares(q, k, far_k, far_ok):
    scale = 1.0 / math.sqrt(HEAD_DIM)
    own = contract_cols(q, k) * scale
    far = contract_cols(q, far_k) * scale
    rows_at = lax.broadcasted_iota(jnp.int32, own.shape, 0)
    slots_at = lax.broadcasted_iota(jnp.int32, own.shape, 1)
    own = jnp.where(slots_at <= rows_at, own, masked_score)
    far = jnp.where(far_ok > 0, far, masked_score)
    scores = jnp.concatenate([own, far], axis=1)
    top = jnp.max(scores, axis=-1, keepdims=True)
    exponent = jnp.exp(scores - top)
    return exponent / jnp.sum(exponent, axis=-1, keepdims=True)


def store_part(value, refs, inner):
    if len(refs) == 1:
        refs[0][...] = value
        return
    half = value.shape[0] // 2

    @pl.when(inner == 1)
    def _():
        refs[0][...] = value[half:]
        refs[1][...] = value[:half]

    @pl.when(inner != 1)
    def _():
        refs[0][...] = value[:half]
        refs[1][...] = value[half:]


def load_total(refs, inner):
    if len(refs) == 1:
        return refs[0][...].astype(f32)
    mine, other = refs[0][...], refs[1][...]
    flip = inner == 1
    first = jnp.where(flip, other, mine)
    last = jnp.where(flip, mine, other)
    return jnp.concatenate([first, last], axis=0).astype(f32)


def part_shapes(slots, width, pieces):
    return [jax.ShapeDtypeStruct((slots // pieces, width), bf16)] * pieces


def attend(inner, projected, far_pack, out_merged, pieces, micro_at, slots):
    cols = projected.shape[1] // 3
    heads = cols // HEAD_DIM
    width = out_merged.shape[1]

    def kernel(i_ref, y_ref, f_ref, w_ref, o_ref, *z_refs):
        far_ok = f_ref[FAR_SLOTS : FAR_SLOTS + 1, :FAR_SLOTS].astype(f32)
        for h in range(heads):
            at = slice(h * HEAD_DIM, (h + 1) * HEAD_DIM)
            far_k = f_ref[:FAR_SLOTS, h * HEAD_DIM : (h + 1) * HEAD_DIM]
            far_v = f_ref[:FAR_SLOTS, cols + h * HEAD_DIM : cols + (h + 1) * HEAD_DIM]
            k = y_ref[:, cols + h * HEAD_DIM : cols + (h + 1) * HEAD_DIM]
            v = y_ref[:, 2 * cols + h * HEAD_DIM : 2 * cols + (h + 1) * HEAD_DIM]
            shares = head_shares(y_ref[:, at], k, far_k, far_ok).astype(bf16)
            values = jnp.concatenate([v, far_v], axis=0)
            o_ref[:, at] = jnp.dot(shares, values, preferred_element_type=f32).astype(bf16)
        part = jnp.dot(o_ref[...], w_ref[...], preferred_element_type=f32).astype(bf16)
        store_part(part, z_refs, i_ref[0])

    return pl.pallas_call(
        kernel,
        grid=(1,),
        in_specs=[
            SCALARS,
            micro_rows(micro_at, slots, 3 * cols),
            single(far_pack.shape),
            single(out_merged.shape),
        ],
        out_specs=[single((slots, cols))] + [single((slots // pieces, width))] * pieces,
        out_shape=[jax.ShapeDtypeStruct((slots, cols), bf16)]
        + part_shapes(slots, width, pieces),
        compiler_params=params(14),
        cost_estimate=SHORT,
        name="attend",
    )(inner, projected, far_pack, out_merged)


def feed_forward(
    scalars,
    branch_sum,
    tokens,
    upstream,
    out_ratio,
    down_ratio,
    gain,
    merged,
    ratio,
    down_merged,
    micro_at,
    db_pieces,
    y_pieces,
):
    slots, width = tokens.shape[2:]
    units = down_merged.shape[0]
    block = UNIT_BLOCK
    blocks = units // block
    pieces = len(branch_sum)
    chunk = 512

    def kernel(*refs):
        n_ref, *refs = refs
        s_refs, refs = refs[:pieces], refs[pieces:]
        x_ref, u_ref, or_ref, dr_ref, g_ref, w_hbm, r_ref, wd_hbm = refs[:8]
        outs, refs = refs[8:13], refs[13:]
        cgu_ref, cd_ref, *refs = refs
        db_refs, y_refs = refs[:db_pieces], refs[db_pieces : db_pieces + y_pieces]
        refs = refs[db_pieces + y_pieces :]
        w_ref, wd_ref, h_ref, b_ref, d2_ref, hid_ref, dgu_ref, db_ref, y_ref = refs[:9]
        in_sems, out_sems = refs[9:]
        loads = []
        for j in range(blocks):
            gate_up = slice(j * 2 * block, (j + 1) * 2 * block)
            rows = slice(j * block, (j + 1) * block)
            loads.append(
                (
                    pltpu.make_async_copy(w_hbm.at[j], w_ref.at[:, gate_up], in_sems.at[0, j]),
                    pltpu.make_async_copy(wd_hbm.at[rows], wd_ref.at[rows], in_sems.at[1, j]),
                )
            )
            for load in loads[-1]:
                load.start()
        held = (h_ref, b_ref, d2_ref, hid_ref, dgu_ref)
        stores = [
            pltpu.make_async_copy(ref, out, out_sems.at[i])
            for i, (ref, out) in enumerate(zip(held, outs))
        ]
        live = lax.broadcasted_iota(jnp.int32, (slots, 1), 0) < n_ref[0]
        branch = load_total(s_refs, n_ref[1]) * or_ref[...]
        h = x_ref[...].astype(f32) + jnp.where(live, branch, 0.0)
        h_ref[...] = h
        b_ref[...] = (h * rms_scale(h) * g_ref[...]).astype(bf16)
        d2_ref[...] = jnp.where(live, u_ref[...].astype(f32) * dr_ref[...], 0.0).astype(bf16)
        for store in stores[:3]:
            store.start()
        for j in range(blocks):
            gate_up = slice(j * 2 * block, (j + 1) * 2 * block)
            rows = slice(j * block, (j + 1) * block)
            for load in loads[j]:
                load.wait()
            raw = jnp.dot(b_ref[...], w_ref[:, gate_up], preferred_element_type=f32)
            dhidden = contract_cols(d2_ref[...], wd_ref[rows])
            scaled = raw * r_ref[:, gate_up]
            gate, up = scaled[:, :block], scaled[:, block:]
            sigmoid = jax.nn.sigmoid(gate)
            activated = gate * sigmoid
            hid_ref[:, rows] = (activated * up).astype(bf16)
            dgate = dhidden * up * sigmoid * (1.0 + gate * (1.0 - sigmoid))
            back = jnp.concatenate([dgate, dhidden * activated], axis=1)
            cgu_ref[:, gate_up] = jnp.sum(back * raw, axis=0, keepdims=True)
            dgu_ref[:, gate_up] = (back * r_ref[:, gate_up]).astype(bf16)
        for store in stores[3:]:
            store.start()
        for start in range(0, width, chunk):
            here = slice(start, start + chunk)
            db_ref[:, here] = contract_cols(dgu_ref[...], w_ref[here, :]).astype(bf16)
            y = jnp.dot(hid_ref[...], wd_ref[:, here], preferred_element_type=f32)
            y_ref[:, here] = y.astype(bf16)
            d2 = jnp.where(live, u_ref[:, here].astype(f32), 0.0)
            cd_ref[:, here] = jnp.sum(d2 * y, axis=0, keepdims=True)
        store_part(db_ref[...], db_refs, n_ref[1])
        store_part(y_ref[...], y_refs, n_ref[1])
        for store in stores:
            store.wait()

    row = single((1, width))
    micro = micro_tokens(micro_at, slots, width)
    anywhere = pl.BlockSpec(memory_space=pl.ANY)
    held = [
        ((slots, width), f32),
        ((slots, width), bf16),
        ((slots, width), bf16),
        ((slots, units), bf16),
        ((slots, 2 * units), bf16),
    ]
    return pl.pallas_call(
        kernel,
        grid=(1,),
        in_specs=[SCALARS]
        + [single(piece.shape) for piece in branch_sum]
        + [micro, micro, row, row, row, anywhere, single((1, 2 * units)), anywhere],
        out_specs=[anywhere] * 5
        + [single((1, 2 * units)), row]
        + [single((slots // db_pieces, width))] * db_pieces
        + [single((slots // y_pieces, width))] * y_pieces,
        out_shape=[jax.ShapeDtypeStruct(*shape) for shape in held]
        + [
            jax.ShapeDtypeStruct((1, 2 * units), f32),
            jax.ShapeDtypeStruct((1, width), f32),
        ]
        + part_shapes(slots, width, db_pieces)
        + part_shapes(slots, width, y_pieces),
        scratch_shapes=[
            pltpu.VMEM((width, 2 * units), bf16),
            pltpu.VMEM((units, width), bf16),
        ]
        + [pltpu.VMEM(*shape) for shape in held]
        + [pltpu.VMEM((slots, width), bf16)] * 2
        + [pltpu.SemaphoreType.DMA((2, blocks)), pltpu.SemaphoreType.DMA((5,))],
        compiler_params=params(LARGE_MIB),
        cost_estimate=SHORT,
        name="feed_forward",
    )(
        scalars,
        *branch_sum,
        tokens,
        upstream,
        out_ratio,
        down_ratio,
        gain,
        merged,
        ratio,
        down_merged,
    )


def attend_back(
    scalars,
    db_sum,
    middle,
    upstream,
    branch_sum,
    gain,
    out_ratio,
    out_merged,
    projected,
    far_pack,
    cosine,
    sine_signed,
    micro_at,
):
    slots, width = middle.shape
    cols = projected.shape[1] // 3
    heads = cols // HEAD_DIM
    scale = 1.0 / math.sqrt(HEAD_DIM)
    pieces = len(db_sum)

    def kernel(*refs):
        n_ref, *refs = refs
        e_refs, s_refs, refs = refs[:pieces], refs[pieces : 2 * pieces], refs[2 * pieces :]
        h_ref, u_ref, g_ref, or_ref, w_ref, y_ref, f_ref, c_ref, sn_ref = refs[:9]
        dh_ref, d1_ref, co_ref, dy_ref, far_ref, do_ref = refs[9:]
        live = lax.broadcasted_iota(jnp.int32, (slots, 1), 0) < n_ref[0]
        h = h_ref[...]
        back = rms_back(h, rms_scale(h), g_ref[...], load_total(e_refs, n_ref[1]))
        dh = u_ref[...].astype(f32) + back
        dh_ref[...] = dh
        d1 = jnp.where(live, dh, 0.0)
        co_ref[...] = jnp.sum(d1 * load_total(s_refs, n_ref[1]), axis=0, keepdims=True)
        d1_ref[...] = (d1 * or_ref[...]).astype(bf16)
        do_ref[...] = contract_cols(d1_ref[...], w_ref[...]).astype(bf16)
        far_ok = f_ref[FAR_SLOTS : FAR_SLOTS + 1, :FAR_SLOTS].astype(f32)
        for i in range(heads):
            at = slice(i * HEAD_DIM, (i + 1) * HEAD_DIM)
            k_at = slice(cols + i * HEAD_DIM, cols + (i + 1) * HEAD_DIM)
            v_at = slice(2 * cols + i * HEAD_DIM, 2 * cols + (i + 1) * HEAD_DIM)
            q = y_ref[:, at]
            far_k = f_ref[:FAR_SLOTS, at]
            shares = head_shares(q, y_ref[:, k_at], far_k, far_ok)
            keys = jnp.concatenate([y_ref[:, k_at], far_k], axis=0)
            values = jnp.concatenate([y_ref[:, v_at], f_ref[:FAR_SLOTS, k_at]], axis=0)
            do = do_ref[:, at]
            share_grad = contract_cols(do, values)
            inner = jnp.sum(shares * share_grad, axis=-1, keepdims=True)
            score_grad = (shares * (share_grad - inner)).astype(bf16)
            dq = jnp.dot(score_grad, keys, preferred_element_type=f32) * scale
            dk = contract_rows(score_grad, q) * scale
            dv = contract_rows(shares.astype(bf16), do)
            dy_ref[:, at] = rotate_back(dq, c_ref[...], sn_ref[...])
            dy_ref[:, k_at] = dk[:slots]
            dy_ref[:, v_at] = dv[:slots]
            far_ref[:, at] = dk[slots:].astype(bf16)
            far_ref[:, k_at] = dv[slots:].astype(bf16)

    operands = (
        scalars,
        *db_sum,
        *branch_sum,
        middle,
        upstream,
        gain,
        out_ratio,
        out_merged,
        projected,
        far_pack,
        cosine,
        sine_signed,
    )
    shapes = [
        jax.ShapeDtypeStruct((slots, width), f32),
        jax.ShapeDtypeStruct((slots, width), bf16),
        jax.ShapeDtypeStruct((1, width), f32),
        jax.ShapeDtypeStruct((slots, 3 * cols), f32),
        jax.ShapeDtypeStruct((FAR_SLOTS, 2 * cols), bf16),
    ]
    return pl.pallas_call(
        kernel,
        grid=(1,),
        in_specs=[SCALARS]
        + [single((slots // pieces, width))] * (2 * pieces)
        + [
            single((slots, width)),
            micro_tokens(micro_at, slots, width),
            single((1, width)),
            single((1, width)),
            single(out_merged.shape),
            micro_rows(micro_at, slots, 3 * cols),
            single(far_pack.shape),
            micro_rows(micro_at, slots, HEAD_DIM),
            micro_rows(micro_at, slots, HEAD_DIM),
        ],
        out_specs=[single(shape.shape) for shape in shapes],
        out_shape=shapes,
        scratch_shapes=[pltpu.VMEM((slots, cols), bf16)],
        compiler_params=params(LARGE_MIB),
        cost_estimate=SHORT,
        name="attend_back",
    )(*operands)


def project_back(
    inner, dy, returned, projected, cosine, sine_signed, ratio, merged, pieces, micro_at
):
    slots, total = dy.shape
    cols = total // 3
    heads = cols // HEAD_DIM
    width = merged.shape[1]
    blocks = 4
    step = width // blocks

    def kernel(i_ref, d_ref, r_ref, y_ref, c_ref, sn_ref, s_ref, w_ref, o_ref, cs_ref, *da_refs):
        @pl.when(pl.program_id(0) == 0)
        def _():
            for i in range(3 * heads):
                at = slice(i * HEAD_DIM, (i + 1) * HEAD_DIM)
                d = d_ref[:, at]
                raw = y_ref[:, at].astype(f32)
                if i >= heads:
                    back = slice((i - heads) * HEAD_DIM, (i - heads + 1) * HEAD_DIM)
                    low = d[:FAR_SLOTS] + r_ref[:FAR_SLOTS, back].astype(f32)
                    d = jnp.concatenate([low, d[FAR_SLOTS:]], axis=0)
                if heads <= i < 2 * heads:
                    d = rotate_back(d, c_ref[...], sn_ref[...])
                if i < 2 * heads:
                    raw = rotate_back(raw, c_ref[...], sn_ref[...])
                cs_ref[:, at] = jnp.sum(d * raw, axis=0, keepdims=True)
                o_ref[:, at] = (d * s_ref[:, at]).astype(bf16)

        da = 0.0
        for g in range(3):
            da = da + contract_cols(o_ref[:, g * cols : (g + 1) * cols], w_ref[g])
        store_part(da.astype(bf16), da_refs, i_ref[0])

    return pl.pallas_call(
        kernel,
        grid=(blocks,),
        in_specs=[
            SCALARS,
            single((slots, total)),
            single(returned.shape),
            micro_rows(micro_at, slots, total),
            micro_rows(micro_at, slots, HEAD_DIM),
            micro_rows(micro_at, slots, HEAD_DIM),
            single((1, total)),
            pl.BlockSpec((3, step, cols), lambda i: (0, i, 0)),
        ],
        out_specs=[
            whole_block((slots, total)),
            whole_block((1, total)),
        ]
        + [pl.BlockSpec((slots // pieces, step), lambda i: (0, i))] * pieces,
        out_shape=[
            jax.ShapeDtypeStruct((slots, total), bf16),
            jax.ShapeDtypeStruct((1, total), f32),
        ]
        + part_shapes(slots, width, pieces),
        compiler_params=params(LARGE_MIB),
        cost_estimate=SHORT,
        name="project_back",
    )(inner, dy, returned, projected, cosine, sine_signed, ratio, merged)


LINE_PAIRS = [(0, 1), (1, 0), (2, 3), (3, 2)]
LINE_ACROSS = [(0, 3), (3, 0), (1, 2), (2, 1)]


def tensor_sum(parts, beside=None, first=()):
    if len(parts) == 1:
        return [lax.psum(parts[0], "tensor")], None
    keep, send = parts
    received = lax.ppermute(send, "tensor", LINE_PAIRS)
    if first:
        received = after(received, *first)
    pair = keep + received
    across = lax.ppermute(pair, "tensor", LINE_ACROSS)
    done = None
    if beside is not None:
        done = beside(pair)
        across = after(across, *done)
    total = pair + across
    return [total, lax.ppermute(total, "tensor", LINE_PAIRS)], done


def line_total(value):
    total = value
    for shift in (1, 2, 3):
        pairs = [(i, (i + shift) % 4) for i in range(4)]
        total = total + lax.ppermute(value, "tensor", pairs)
    return total


def dp_swap(value, hop):
    return lax.ppermute(value, "dp", [(i, i ^ hop) for i in range(8)])


def dp_share(value, line_rows):
    me = lax.axis_index("dp")
    half = value.shape[1] // 2
    quarter = half // 4
    upper = (me & 1) != 0
    low, high = value[:, :half], value[:, half:]
    value = jnp.where(upper, high, low) + dp_swap(jnp.where(upper, low, high), 1)
    chip = me // 2

    def columns(index):
        return lax.dynamic_slice_in_dim(value, index * quarter, quarter, 1)

    kept = columns(chip).astype(f32)
    for hop in (1, 2, 3):
        kept = kept + dp_swap(columns(chip ^ hop), 2 * hop)
    line = kept[:line_rows].astype(bf16)
    total = line.astype(f32)
    for shift in (1, 2, 3):
        total = total + lax.ppermute(line, "tensor", [(i, (i + shift) % 4) for i in range(4)])
    return jnp.concatenate([total, kept[line_rows:]], axis=0).astype(bf16)


def dp_gather(mine):
    me = lax.axis_index("dp")
    upper = (me & 1) != 0
    chip = me // 2
    quarters = [mine] + [dp_swap(mine, 2 * hop) for hop in (1, 2, 3)]
    value = jnp.concatenate([lax.select_n(chip ^ q, *quarters) for q in range(4)], axis=1)
    other = dp_swap(value, 1)
    value = jnp.concatenate(
        [jnp.where(upper, other, value), jnp.where(upper, value, other)], axis=1
    )
    return value.astype(f32)


def pair_exchange(pack, distance, sibling_distance):
    held = [pack] + [dp_swap(pack, hop) for hop in (2, 4, 6)]

    def pick(index):
        return lax.select_n(index // 2, *held)

    across = dp_swap(pick(sibling_distance & 6), 1)
    return jnp.where(distance % 2 == 1, across, pick(distance & 6)), held


def adapter_in(seen_inputs, sent_grads, merged, tall, wide, share, rank):
    micros = len(sent_grads)
    slots, depth = sent_grads[0].shape[0], seen_inputs[0].shape[1]
    blocks, _, cols = merged.shape
    shared = seen_inputs[0].shape[0] != slots
    if shared:
        seen_inputs = seen_inputs * micros
    ranks = tall.shape[0]
    groups = ranks // rank
    sides = 1 if blocks == groups else groups
    part = cols // sides
    scale = ADAPTER_NUMER / ADAPTER_RANK

    def kernel(*refs):
        x_refs, d_refs, refs = refs[:micros], refs[micros : 2 * micros], refs[2 * micros :]
        v_ref, t_ref, w_ref, s_ref, out_ref, *right_refs = refs[: 5 + sides]
        seen_ref, sent_ref, left_ref, all_ref = refs[5 + sides :]
        at = pl.program_id(0)

        @pl.when(at == 0)
        def _():
            left_ref[...] = jnp.zeros_like(left_ref)
            sent_ref[...] = jnp.zeros_like(sent_ref)
            for m in range(micros):
                seen_ref[m] = contract_cols(x_refs[m][...], t_ref[...]).astype(bf16)

        share = s_ref[...]
        wide = w_ref[...]
        right = -jnp.dot(t_ref[...], v_ref[...], preferred_element_type=f32) * share
        left = -contract_cols((wide * share).astype(bf16), v_ref[...])
        for m in range(micros):
            right = right + contract_rows(seen_ref[m], d_refs[m][...])
            sent_ref[m] += contract_cols(d_refs[m][...], wide.astype(bf16))
        if sides == 1:
            all_ref[...] = scale * right
            mine = pl.ds(pl.multiple_of(at * rank, rank), rank)
            right_refs[0][...] = all_ref[mine, :].astype(bf16)
        else:
            for g in range(sides):
                mine = right[g * rank : (g + 1) * rank, g * part : (g + 1) * part]
                right_refs[g][...] = (scale * mine).astype(bf16)
        left_ref[...] += left

        @pl.when(at == blocks - 1)
        def _():
            total = left_ref[...]
            for m in range(micros):
                total = total + contract_rows(sent_ref[m].astype(bf16), x_refs[m][...])
            out_ref[...] = (scale * total).astype(bf16)

    return pl.pallas_call(
        kernel,
        grid=(blocks,),
        in_specs=[micro_rows(m if shared else 0, slots, depth) for m in range(micros)]
        + [pl.BlockSpec((slots, cols), lambda i: (0, i))] * micros
        + [
            pl.BlockSpec((None, depth, cols), lambda i: (i, 0, 0)),
            single((ranks, depth)),
            pl.BlockSpec((ranks, cols), lambda i: (0, i)),
            pl.BlockSpec((1, cols), lambda i: (0, i)),
        ],
        out_specs=[whole_block((ranks, depth))]
        + [pl.BlockSpec((rank, part), lambda i: (0, i))] * sides,
        out_shape=[jax.ShapeDtypeStruct((ranks, depth), bf16)]
        + [jax.ShapeDtypeStruct((rank, blocks * part), bf16)] * sides,
        scratch_shapes=[
            pltpu.VMEM((micros, slots, ranks), bf16),
            pltpu.VMEM((micros, slots, ranks), f32),
            pltpu.VMEM((ranks, depth), f32),
            pltpu.VMEM((ranks, cols), f32),
        ],
        compiler_params=params(LARGE_MIB),
        cost_estimate=SHORT,
        name="adapter_in",
    )(*seen_inputs, *sent_grads, merged, tall, wide, share)


def adapter_out(seen_inputs, sent_grads, merged, first_t, second, share):
    micros = len(seen_inputs)
    slots, cols = sent_grads[0].shape
    depth = merged.shape[0]
    block = min(depth, UNIT_BLOCK)
    blocks = depth // block
    rank = second.shape[0]
    scale = ADAPTER_NUMER / ADAPTER_RANK

    def kernel(*refs):
        x_refs, d_refs, refs = refs[:micros], refs[micros : 2 * micros], refs[2 * micros :]
        v_ref, a_ref, b_ref, s_ref, left_ref, out_ref, seen_ref, sent_ref, right_ref = refs
        at = pl.program_id(0)
        second = b_ref[...]

        @pl.when(at == 0)
        def _():
            right_ref[...] = jnp.zeros_like(right_ref)
            seen_ref[...] = jnp.zeros_like(seen_ref)
            for m in range(micros):
                sent_ref[m] = contract_cols(d_refs[m][...], second.astype(bf16)).astype(bf16)

        first = a_ref[...].astype(bf16)
        left = -contract_cols((second * s_ref[...]).astype(bf16), v_ref[...])
        for m in range(micros):
            left = left + contract_rows(sent_ref[m], x_refs[m][...])
            seen_ref[m] += contract_cols(x_refs[m][...], first)
        left_ref[...] = (scale * left).astype(bf16)
        right_ref[...] += -jnp.dot(first, v_ref[...], preferred_element_type=f32) * s_ref[...]

        @pl.when(at == blocks - 1)
        def _():
            total = right_ref[...]
            for m in range(micros):
                total = total + contract_rows(seen_ref[m].astype(bf16), d_refs[m][...])
            out_ref[...] = (scale * total).astype(bf16)

    return pl.pallas_call(
        kernel,
        grid=(blocks,),
        in_specs=[pl.BlockSpec((slots, block), lambda i: (0, i))] * micros
        + [single((slots, cols))] * micros
        + [
            pl.BlockSpec((block, cols), lambda i: (i, 0)),
            pl.BlockSpec((rank, block), lambda i: (0, i)),
            single((rank, cols)),
            single((1, cols)),
        ],
        out_specs=[pl.BlockSpec((rank, block), lambda i: (0, i)), whole_block((rank, cols))],
        out_shape=[
            jax.ShapeDtypeStruct((rank, depth), bf16),
            jax.ShapeDtypeStruct((rank, cols), bf16),
        ],
        scratch_shapes=[
            pltpu.VMEM((micros, slots, rank), f32),
            pltpu.VMEM((micros, slots, rank), bf16),
            pltpu.VMEM((rank, cols), f32),
        ],
        compiler_params=params(LARGE_MIB),
        cost_estimate=SHORT,
        name="adapter_out",
    )(*seen_inputs, *sent_grads, merged, first_t, second, share)


def finish_input(scalars, total, tokens, middle_grad, gain, micro_at, micros, earlier):
    slots, width = middle_grad.shape
    pieces = len(total)

    def kernel(*refs):
        i_ref, *refs = refs
        x_ref, d_ref, g_ref = refs[pieces : pieces + 3]
        x = x_ref[...].astype(f32)
        back = rms_back(x, rms_scale(x), g_ref[...], load_total(refs[:pieces], i_ref[1]))
        refs[-1][...] = (d_ref[...] + back).astype(bf16)

    operands = [scalars, *total, tokens, middle_grad, gain]
    specs = [SCALARS] + [single(piece.shape) for piece in total]
    specs += [micro_tokens(micro_at, slots, width), single((slots, width)), single((1, width))]
    return write_micro(kernel, operands, specs, slots, width, micro_at, micros, earlier)


def finish_output(scalars, total, middle, ratio, micro_at, micros, earlier):
    slots, width = middle.shape
    pieces = len(total)

    def kernel(*refs):
        n_ref, *refs = refs
        m_ref, r_ref = refs[pieces : pieces + 2]
        live = lax.broadcasted_iota(jnp.int32, (slots, 1), 0) < n_ref[0]
        branch = load_total(refs[:pieces], n_ref[1]) * r_ref[...]
        refs[-1][...] = (m_ref[...] + jnp.where(live, branch, 0.0)).astype(bf16)

    operands = [scalars, *total, middle, ratio]
    specs = [SCALARS] + [single(operand.shape) for operand in operands[1:]]
    return write_micro(kernel, operands, specs, slots, width, micro_at, micros, earlier)


def write_micro(kernel, operands, specs, slots, width, micro_at, micros, earlier):
    aliases = {}
    if earlier is not None:
        aliases = {len(operands): 0}
        operands = operands + [earlier]
        specs = specs + [pl.BlockSpec(memory_space=pl.ANY)]
    return pl.pallas_call(
        kernel,
        grid=(1,),
        in_specs=specs,
        out_specs=pl.BlockSpec((None, None, slots, width), lambda i: (micro_at, 0, 0, 0)),
        out_shape=jax.ShapeDtypeStruct((micros, 1, slots, width), bf16),
        input_output_aliases=aliases,
        compiler_params=params(16),
        cost_estimate=SHORT,
        name="finish",
    )(*operands)


def after(value, *others):
    return lax.optimization_barrier((value, *others))[0]


def from_blocks(array, groups, units):
    ranks, total = array.shape
    array = array.reshape(ranks, total // (groups * UNIT_BLOCK), groups, UNIT_BLOCK)
    return jnp.transpose(array, (2, 0, 1, 3)).reshape(groups, ranks, total // groups)[..., :units]


def diagonal(second):
    groups, rank, cols = second.shape
    rows = [
        jnp.pad(second[g], ((g * rank, (groups - 1 - g) * rank), (0, 0))) for g in range(groups)
    ]
    return jnp.stack(rows)


def fast_device(
    inputs,
    lengths,
    prompt_mask,
    partner,
    positions,
    attn_gain,
    mlp_gain,
    attention_input_frozen,
    attention_input_first,
    attention_input_second,
    attention_input_magnitude,
    attention_output_frozen,
    attention_output_first,
    attention_output_second,
    attention_output_magnitude,
    feedforward_input_frozen,
    feedforward_input_first,
    feedforward_input_second,
    feedforward_input_magnitude,
    feedforward_output_frozen,
    feedforward_output_first,
    feedforward_output_second,
    feedforward_output_magnitude,
    grad_out,
):
    micros, _, slots, width = inputs.shape
    cols = attention_input_frozen.shape[2]
    units = feedforward_input_frozen.shape[2]
    rank = attention_output_second.shape[0]
    attn_row = attn_gain.astype(f32)[None]
    mlp_row = mlp_gain.astype(f32)[None]
    qkv_first_t = jnp.swapaxes(attention_input_first, 1, 2)
    gate_first_t = jnp.swapaxes(feedforward_input_first, 1, 2)
    out_first_t = attention_output_first.T
    down_first_t = feedforward_output_first.T
    out_magnitude = attention_output_magnitude[None]
    down_magnitude = feedforward_output_magnitude[None]

    me = lax.axis_index("dp")
    distance = partner[:, 0] ^ me
    sibling_distance = lax.ppermute(distance, "dp", [(i, i ^ 1) for i in range(8)])

    indices = jnp.arange(HEAD_DIM // 2, dtype=f32)
    inverse = rope_base ** (-2.0 * indices / HEAD_DIM)
    angles = positions.reshape(micros * slots).astype(f32)[:, None] * inverse[None, :]
    cosine, sine = jnp.cos(angles), jnp.sin(angles)
    cosine = jnp.concatenate([cosine, cosine], axis=1)
    sine_signed = jnp.concatenate([-sine, sine], axis=1)
    tokens = inputs.reshape(micros * slots, width)
    qkv_magnitude = attention_input_magnitude.reshape(1, -1)
    normed, qkv_merged, qkv_square, projected, *packs = merge_project(
        tokens,
        attn_row,
        jnp.swapaxes(attention_input_frozen, 0, 1),
        qkv_first_t,
        attention_input_second,
        qkv_magnitude,
        cosine,
        sine_signed,
        prompt_mask[:, 0, :FAR_SLOTS].astype(f32),
        slots,
    )
    qkv_inverse = lax.rsqrt(qkv_square)
    qkv_ratio = qkv_magnitude * qkv_inverse

    far_packs, held = [], []
    for m in range(micros):
        pack = after(packs[m], *held)
        far_pack, held = pair_exchange(pack, distance[m], sibling_distance[m])
        far_packs.append(far_pack)

    out_merged, out_square = merge_out(
        attention_output_frozen, out_first_t, after(attention_output_second, packs[0])
    )
    down_merged, down_square = merge_out(
        feedforward_output_frozen, down_first_t, after(feedforward_output_second, packs[0])
    )
    line_at = lax.axis_index("tensor")
    inner = ((line_at == 1) | (line_at == 2)).astype(jnp.int32)[None]
    scalars = [jnp.concatenate([lengths[m], inner]) for m in range(micros)]

    pieces = (2, 1)
    attended, parts = [], []
    turn = after(inner, down_square)
    for m in range(micros):
        seen, *part = attend(turn, projected, far_packs[m], out_merged, pieces[m], m, slots)
        turn = after(inner, seen)
        attended.append(seen)
        parts.append(part)
    squares = jnp.concatenate([out_square, down_square], axis=0)
    squares = line_total(after(squares, attended[1]))
    out_inverse, down_inverse = lax.rsqrt(squares[:1]), lax.rsqrt(squares[1:])
    out_ratio = out_magnitude * out_inverse
    down_ratio = down_magnitude * down_inverse
    gate_rank = 2 * rank

    def merge_gate(pair):
        return merge_in(
            feedforward_input_frozen,
            gate_first_t,
            after(feedforward_input_second, attended[1], pair),
            feedforward_input_magnitude,
        )

    first_sum, found = tensor_sum(parts[0], merge_gate)
    gate_merged, gate_ratio, gate_inverse, gate_wide = found
    branch_sums = [first_sum, tensor_sum(parts[1])[0]]

    middles, normed_mlp, hiddens, gate_grads, gate_inner = [], [], [], [], 0.0
    db_parts, down_parts, down_grads, down_inner = [], [], [], 0.0
    turn = scalars[0]
    for m in range(micros):
        middle, b, d2, hidden, dgu, c_gate, c_down, *sums = feed_forward(
            turn,
            branch_sums[m],
            inputs,
            grad_out,
            out_ratio,
            down_ratio,
            mlp_row,
            gate_merged,
            gate_ratio,
            down_merged,
            m,
            pieces[m],
            1 + m,
        )
        db, y = sums[: pieces[m]], sums[pieces[m] :]
        turn = after(scalars[1], c_down)
        middles.append(middle)
        normed_mlp.append(b)
        hiddens.append(hidden)
        gate_grads.append(dgu)
        gate_inner = gate_inner + c_gate
        down_inner = down_inner + c_down
        down_grads.append(d2)
        db_parts.append(db)
        down_parts.append(y)
    gate_tall = gate_first_t.reshape(gate_rank, width).astype(bf16)

    def adapters_feed_forward(pair):
        inner_now, down_now = after(gate_inner, pair), after(down_inner, pair)
        down_now = line_total(down_now)
        in_found = adapter_in(
            normed_mlp,
            gate_grads,
            gate_merged,
            gate_tall,
            gate_wide,
            inner_now * gate_ratio * gate_inverse * gate_inverse,
            rank,
        )
        out_found = adapter_out(
            hiddens,
            down_grads,
            down_merged,
            jnp.pad(down_first_t, ((0, 0), (0, down_merged.shape[0] - units))),
            feedforward_output_second,
            down_now * down_ratio * down_inverse * down_inverse,
        )
        return [*in_found, *out_found, down_now]

    first_sum, found = tensor_sum(db_parts[0], adapters_feed_forward, [down_inner])
    gate_left, gate_right, up_right, down_left, down_right, down_inner = found
    db_sums = [first_sum, tensor_sum(db_parts[1])[0]]
    gate_mag = from_blocks(gate_inner * gate_inverse, 2, units)[:, 0]
    down_mag = down_inner * down_inverse
    down_parts[0] = [after(down_parts[0][0], db_sums[1][0])]
    down_sums = [tensor_sum(part)[0] for part in down_parts]

    middle_grads, out_grads, out_inner, qkv_grads, qkv_inner, da_parts = [], [], 0.0, [], 0.0, []
    exchanged = []
    turn = scalars[0]
    for m in range(micros):
        dh, d1, c_out, dy, far_grad = attend_back(
            turn,
            db_sums[m],
            middles[m],
            grad_out,
            branch_sums[m],
            mlp_row,
            out_ratio,
            out_merged,
            projected,
            far_packs[m],
            cosine,
            sine_signed,
            m,
        )
        turn = after(scalars[1], c_out)
        middle_grads.append(dh)
        out_grads.append(d1)
        out_inner = out_inner + c_out
        returned, _ = pair_exchange(far_grad, distance[m], sibling_distance[m])
        exchanged.append((dy, returned))
    turn = inner
    for m in range(micros):
        dy, returned = exchanged[m]
        dqkv, c_qkv, *da = project_back(
            turn,
            dy,
            returned,
            projected,
            cosine,
            sine_signed,
            qkv_ratio,
            qkv_merged,
            2 - m,
            m,
        )
        turn = after(inner, c_qkv)
        qkv_grads.append(dqkv)
        qkv_inner = qkv_inner + c_qkv
        da_parts.append(da)
    def adapters_attention(pair):
        out_now, qkv_now = after(out_inner, pair), after(qkv_inner, pair) / qkv_ratio
        out_found = adapter_out(
            attended,
            out_grads,
            out_merged,
            out_first_t,
            attention_output_second,
            out_now * out_ratio * out_inverse * out_inverse,
        )
        in_found = adapter_in(
            [normed],
            qkv_grads,
            qkv_merged,
            qkv_first_t.reshape(3 * rank, width).astype(bf16),
            jnp.concatenate(list(diagonal(attention_input_second)), axis=1),
            qkv_now * qkv_ratio * qkv_inverse * qkv_inverse,
            rank,
        )
        return [*out_found, *in_found, qkv_now]

    found = adapters_attention(qkv_inner)
    out_left, out_right, qkv_left, qkv_right, qkv_inner = found
    low_units = [piece[:, :units] for piece in (gate_right, up_right, down_left)]
    magnitudes = [gate_mag, down_mag, qkv_inner * qkv_inverse, out_inner * out_inverse]

    def wide(piece):
        return jnp.pad(piece.astype(bf16), ((0, 0), (0, width - piece.shape[1])))

    magnitudes = jnp.concatenate([wide(piece) for piece in magnitudes], axis=0)
    magnitudes = jnp.pad(magnitudes, ((0, rank - magnitudes.shape[0]), (0, 0)))
    pieces = [gate_left, down_right, qkv_left, out_right]
    line_rows = 7 * rank
    pieces += [wide(piece) for piece in low_units]
    pieces += [jnp.concatenate([qkv_right, out_left], axis=1), magnitudes]
    share = dp_share(jnp.concatenate(pieces, axis=0), line_rows)
    da_last = after(da_parts[1][0], *down_sums[0])
    da_sums = [tensor_sum(da_parts[0])[0], tensor_sum([da_last])[0]]
    layer_out, layer_grad = None, None
    for m in range(micros):
        layer_out = finish_output(
            scalars[m], down_sums[m], middles[m], down_ratio, m, micros, layer_out
        )
    layer_grad = finish_input(
        scalars[0], da_sums[0], inputs, middle_grads[0], attn_row, 0, micros, None
    )
    totals = dp_gather(after(share, layer_out, layer_grad, da_sums[1][0]))
    found, at = [], 0
    for piece in pieces:
        found.append(totals[at : at + piece.shape[0]])
        at += piece.shape[0]
    gate_left, down_right, qkv_left, out_right, gate_right, up_right, down_left, rights, mags = found
    gate_left = gate_left.reshape(2, rank, width)
    qkv_left = qkv_left.reshape(3, rank, width)
    gate_right = jnp.stack([gate_right[:, :units], up_right[:, :units]])
    down_left = down_left[:, :units]
    qkv_right = jnp.stack([rights[:, g * cols : (g + 1) * cols] for g in range(3)])
    out_left = rights[:, 3 * cols :]
    gate_mag, down_mag, out_mag = mags[:2, :units], mags[2], mags[4]
    qkv_mag = mags[3, : 3 * cols].reshape(3, cols)

    layer_grad = finish_input(
        scalars[1], da_sums[1], inputs, middle_grads[1], attn_row, 1, micros, layer_grad
    )
    return (
        layer_out,
        layer_grad,
        jnp.swapaxes(qkv_left, 1, 2),
        qkv_right,
        qkv_mag,
        out_left.T,
        out_right,
        out_mag,
        jnp.swapaxes(gate_left, 1, 2),
        gate_right,
        gate_mag,
        down_left.T,
        down_right,
        down_mag,
    )


def solution(mesh):
    in_specs = (
        P(None, "dp", None, None),
        P(None, "dp"),
        P(None, "dp", None),
        P(None, "dp"),
        P(None, "dp", None),
        P(),
        P(),
        P(None, None, "tensor"),
        P(),
        P(None, None, "tensor"),
        P(None, "tensor"),
        P("tensor", None),
        P("tensor", None),
        P(),
        P(),
        P(None, None, "tensor"),
        P(),
        P(None, None, "tensor"),
        P(None, "tensor"),
        P("tensor", None),
        P("tensor", None),
        P(),
        P(),
        P(None, "dp", None, None),
    )
    out_specs = (
        P(None, "dp", None, None),
        P(None, "dp", None, None),
        P(),
        P(None, None, "tensor"),
        P(None, "tensor"),
        P("tensor", None),
        P(),
        P(),
        P(),
        P(None, None, "tensor"),
        P(None, "tensor"),
        P("tensor", None),
        P(),
        P(),
    )
    device_step = fast_device if fits_fast(mesh) else general_device
    return jax.shard_map(
        device_step, mesh=mesh, in_specs=in_specs, out_specs=out_specs, check_vma=False
    )
```
